32 devices in a mesh: group: 2 (over x), ty: 8 (over z, y), tx: 2 (over core).
Axes of the slice: x: 2, y: 2, z: 4, core: 2. Of those that a mesh axis runs over, the one named last changes fastest.
Arguments:
- sweeps: bfloat16 [8192, 48, 128], P(('group', 'ty', 'tx')), parts along dimension 0, may hold values from -12 to 12
- route_block: int32 [32, 16, 16], P(('group', 'ty', 'tx')), parts along dimension 0, may hold values from 0 to 255
- route_cell: int32 [32, 16, 16], P(('group', 'ty', 'tx')), parts along dimension 0, may hold values from 0 to 383
- route_templ: int32 [32, 16, 16], P(('group', 'ty', 'tx')), parts along dimension 0, may hold values from 0 to 31
- route_count: int32 [32, 16], P(('group', 'ty', 'tx')), parts along dimension 0, may hold values from 2 to 16, as said below
- footprint: bfloat16 [32, 128, 128], replicated, may hold values from 0 to 13, as said below
- conv_first: bfloat16 [9, 64, 48], replicated, may hold values from -0.3125 to 0.3125
- bias_first: float32 [64], replicated, may hold values from -3 to 3
- conv_second: bfloat16 [9, 64, 64], replicated, may hold values from -0.25 to 0.25
- bias_second: float32 [64], replicated, may hold values from -3 to 3
Outputs:
- encoded: bfloat16 [64, 3072, 512], P(None, ('group', 'ty'), 'tx'), parts along dimension 1
The draws below stay inside these ranges and needn't reach their ends.
There are 2 independent parts, one for each index of `group`. The reference program is written for one: setup_inputs(seed, part) draws one part's arguments, and reference() takes and returns one part's arrays. A program takes and returns all parts, laid end to end along the dimension named above; an argument that names none is the same for every part. Nothing has to cross between parts.
Inputs may be any that keep to these rules, and one draw needn't show every extreme that they name: `route_count`: in every draw one tile receives 16 live slots from every device. `footprint`: nonnegative weights.
All inputs are finite; a program needn't handle non-finite values.
Results may differ from the reference program's by a relative error of at most 0.0036.
Values may be sent and summed in bfloat16 or wider, within the bound.
No kernel may reach another device: no remote copies, remote signals or barrier semaphores. Data moves between devices by JAX's collectives and lax.ppermute only.
A program may use at most 256 MiB of HBM per device.

```python
import math
import jax
import jax.numpy as jnp
from jax import lax

CHAN = 48
HID = 64
BLOCK = 128
TEMPL = 32
CAP = 16
BLK_DEV = 256
TH = 192
TW = 256
PEERS = 16
BLOCKS = 4096
CBLK = 384
NH = 1536
NW = 512
N_TY = 8
N_TX = 2


def draw_route_count(key, part):
    key = jax.random.fold_in(key, 3)
    level = jax.random.randint(jax.random.fold_in(key, 11), (PEERS,), 1, 5)
    lowest = CAP * level // 8
    highest = CAP * level // 4 + 1
    raw_units = jax.random.randint(jax.random.fold_in(key, 12), (PEERS, PEERS), 0, 1048576)
    counts = lowest[None, :] + raw_units % (highest - lowest)[None, :]
    busiest = jax.random.randint(jax.random.fold_in(key, 13), (), 0, PEERS)
    counts = jnp.where(jnp.arange(PEERS)[None, :] == busiest, CAP, counts)
    return counts.astype(jnp.int32)


def draw_footprint(key, part):
    key = jax.random.fold_in(key, 5)
    uniform_part = jax.random.uniform(jax.random.fold_in(key, 1), (TEMPL, BLOCK, BLOCK), jnp.float32)
    row_scale = jnp.exp(jax.random.uniform(jax.random.fold_in(key, 2), (TEMPL, BLOCK, 1), jnp.float32) * math.log(10.0))
    col_scale = jnp.exp(jax.random.uniform(jax.random.fold_in(key, 3), (TEMPL, 1, BLOCK), jnp.float32) * math.log(10.0))
    return (uniform_part * row_scale * col_scale * 0.1).astype(jnp.bfloat16)


def touch_ends(drawn, stream_key, least, top_value):
    shape = drawn.shape
    spot = [jax.random.randint(jax.random.fold_in(stream_key, axis), (), 0, shape[axis]) for axis in range(len(shape))]
    drawn = drawn.at[tuple(spot)].set(least)
    longest = shape.index(max(shape))
    spot[longest] = (spot[longest] + 1) % shape[longest]
    return drawn.at[tuple(spot)].set(top_value)


def levels(stream_key, shape, pieces, smallest, largest):
    def one(axis_at, parts):
        heights = jax.random.uniform(jax.random.fold_in(jax.random.fold_in(stream_key, 6), axis_at), (parts,), jnp.float32, smallest / len(pieces), largest / len(pieces))
        return jnp.repeat(jnp.exp(heights), shape[axis_at] // parts).reshape((-1,) + (1,) * (len(shape) - axis_at - 1))

    factor_of = one(*pieces[0])
    for cut in pieces[1:]:
        factor_of = factor_of * one(*cut)
    return factor_of


def bell_draw(stream_key, shape, spread, bound, shards=(), held_as=jnp.bfloat16):
    array = spread * jax.random.normal(stream_key, shape, jnp.float32)
    if shards:
        array = array * levels(stream_key, shape, shards, -0.22, 0.18)
    return jnp.clip(array, -bound, bound).astype(held_as)


def setup_inputs(seed: int = 0, part: int = 0) -> dict:
    arg_keys = jax.random.split(jax.random.key(seed), 11)
    part_splits = jax.random.split(jax.random.fold_in(arg_keys[10], part), 11)
    sweeps = bell_draw(part_splits[0], (BLOCKS, CHAN, BLOCK), 2.0, 12.0, ((0, 16),))
    route_block = touch_ends(jax.random.randint(part_splits[1], (PEERS, PEERS, CAP), 0, BLK_DEV), jax.random.fold_in(part_splits[1], 1), 0, BLK_DEV - 1).astype(jnp.int32)
    route_cell = touch_ends(jax.random.randint(part_splits[2], (PEERS, PEERS, CAP), 0, CBLK), jax.random.fold_in(part_splits[2], 1), 0, CBLK - 1).astype(jnp.int32)
    route_templ = touch_ends(jax.random.randint(part_splits[3], (PEERS, PEERS, CAP), 0, TEMPL), jax.random.fold_in(part_splits[3], 1), 0, TEMPL - 1).astype(jnp.int32)
    route_count = draw_route_count(jax.random.fold_in(jax.random.fold_in(arg_keys[10], part), 71), part)
    footprint = draw_footprint(jax.random.fold_in(arg_keys[10], 71), part)
    conv_first = bell_draw(arg_keys[6], (9, HID, CHAN), (9 * CHAN) ** -0.5, 0.3125)
    bias_first = bell_draw(arg_keys[7], (HID,), 0.5, 3.0, (), jnp.float32)
    conv_second = bell_draw(arg_keys[8], (9, HID, HID), (9 * HID) ** -0.5, 0.25)
    bias_second = bell_draw(arg_keys[9], (HID,), 0.5, 3.0, (), jnp.float32)
    return {"sweeps": sweeps, "route_block": route_block, "route_cell": route_cell, "route_templ": route_templ, "route_count": route_count, "footprint": footprint, "conv_first": conv_first, "bias_first": bias_first, "conv_second": conv_second, "bias_second": bias_second}


def stencil(padded, kernel, bias):
    height = padded.shape[1] - 2
    span_cols = padded.shape[2] - 2
    summed = jnp.zeros((kernel.shape[1], height, span_cols), jnp.float32)
    for tap_row in range(3):
        for tap_col in range(3):
            window = padded[:, tap_row:tap_row + height, tap_col:tap_col + span_cols].astype(jnp.float32)
            summed = summed + jnp.einsum("oc,chw->ohw", kernel[3 * tap_row + tap_col].astype(jnp.float32), window, precision=lax.Precision.HIGHEST)
    return summed + bias[:, None, None]


def reference(sweeps, route_block, route_cell, route_templ, route_count, footprint, conv_first, bias_first, conv_second, bias_second):
    peer_count = route_block.shape[0]
    capacity = route_block.shape[2]
    row_weight = jnp.sum(footprint.astype(jnp.float32), axis=2)
    anchor = (jnp.arange(peer_count, dtype=jnp.int32) * BLK_DEV)[:, None]
    slot_index = jnp.arange(capacity, dtype=jnp.int32)

    def one_tile(target_tile):
        block_ids = (route_block[:, target_tile, :] + anchor).astype(jnp.int32)
        samples = sweeps[block_ids].astype(jnp.float32)
        template = route_templ[:, target_tile, :]
        matrices = footprint[template].astype(jnp.float32)
        is_live = (slot_index[None, :] < route_count[:, target_tile][:, None]).astype(jnp.float32)
        terms = jnp.einsum("psxy,pscy->pscx", matrices, samples, precision=lax.Precision.HIGHEST)
        terms = terms * is_live[:, :, None, None]
        weights = row_weight[template] * is_live[:, :, None]
        targets = route_cell[:, target_tile, :].reshape(-1)
        numerator = jax.ops.segment_sum(terms.reshape(-1, CHAN, BLOCK), targets, num_segments=CBLK)
        denominator = jax.ops.segment_sum(weights.reshape(-1, BLOCK), targets, num_segments=CBLK)
        composite = (numerator / (1.0 + denominator)[:, None, :]).astype(jnp.bfloat16)
        return jnp.transpose(composite, (1, 0, 2)).reshape(CHAN, TH, TW)

    all_tiles = lax.map(one_tile, jnp.arange(peer_count, dtype=jnp.int32))
    full_grid = all_tiles.reshape(N_TY, N_TX, CHAN, TH, TW).transpose(2, 0, 3, 1, 4).reshape(CHAN, NH, NW)
    padded = jnp.pad(full_grid, ((0, 0), (1, 1), (1, 1)))
    hidden = jax.nn.silu(stencil(padded, conv_first, bias_first)).astype(jnp.bfloat16)
    padded_hidden = jnp.pad(hidden, ((0, 0), (1, 1), (1, 1)))
    return stencil(padded_hidden, conv_second, bias_second).astype(jnp.bfloat16)
```

```python
import functools

import jax
import jax.numpy as jnp
from jax import lax
from jax.experimental import pallas as pl
from jax.experimental.pallas import tpu as pltpu
from jax.sharding import PartitionSpec as P

TH = 192
TW = 256
CBLK = 384
LANES = 128
HALO = 2
EDGE_TILES = 2
INFO_ROWS = 16
CELL_BASE = 32
STEPS = 4
UNROLL = 8
GROUP_ONE = 3
GROUP_TWO = 2
OUT_ROWS = 16
VMEM_LIMIT = 56 * 1024 * 1024

F32 = jnp.float32
BF16 = jnp.bfloat16


def lane_index(shape):
    return lax.broadcasted_iota(jnp.int32, shape, len(shape) - 1)


def silu(value):
    half = 0.5 * value
    return half + half * jnp.tanh(half)


def composite_kernel(
    capacity, channels, cell_ref, templ_ref, col_ref, recv_ref, table_ref, weight_ref,
    comp_ref, edge_ref, acc, den, strip,
):
    step = pl.program_id(0)
    sources = recv_ref.shape[0]
    col = col_ref[0]

    @pl.when(step == 0)
    def clear():
        def clear_block(i, carry):
            acc[i] = jnp.zeros(acc.shape[1:], F32)
            return carry

        lax.fori_loop(0, acc.shape[0], clear_block, 0, unroll=4)
        den[...] = jnp.zeros(den.shape, F32)
        strip[...] = jnp.zeros(strip.shape, F32)

    per_source = capacity // UNROLL

    def add_slots(i, carry):
        source = i // per_source
        first = (i % per_source) * UNROLL
        slot = (step * sources + source) * capacity + first
        terms = []
        for u in range(UNROLL):
            row = pl.multiple_of((first + u) * channels, 16)
            block = recv_ref[source, pl.ds(row, channels), :]
            terms.append(
                jnp.dot(block, table_ref[templ_ref[slot + u]], preferred_element_type=F32)
            )
        for u in range(UNROLL):
            cell = cell_ref[slot + u]
            acc[cell] += terms[u]
            den[pl.ds(cell, 1), :] += weight_ref[pl.ds(templ_ref[slot + u], 1), :]
        return carry

    lax.fori_loop(0, sources * per_source, add_slots, 0)

    @pl.when(step == pl.num_programs(0) - 1)
    def finish():
        den[...] = 1.0 / (1.0 + den[...])
        lane = lane_index((channels, LANES))

        def one_row(r, carry):
            out = pl.multiple_of(r * channels, 16)
            parts = []
            for m in range(2):
                value = (acc[2 * r + m] * den[pl.ds(2 * r + m, 1), :]).astype(BF16)
                comp_ref[pl.ds(out, channels), m * LANES : (m + 1) * LANES] = value
                parts.append(value)
            side = jnp.where(col == 0, parts[1], parts[0]).astype(F32)
            at = r + HALO
            start = jnp.where(col == 0, LANES - 2, 0)
            side = pltpu.roll(side, (at - start + LANES) % LANES, 1)
            for p in range(2):
                tile = (at + p) // LANES
                strip[p, tile] = jnp.where(lane == (at + p) % LANES, side, strip[p, tile])
            return carry

        lax.fori_loop(0, TH, one_row, 0, unroll=2)
        edge_ref[...] = strip[...].astype(BF16)


def encoder_kernel(
    channels, hid, place_ref, comp_ref, up_ref, down_ref, own_ref, side_ref, side_up_ref, side_down_ref,
    first_ref, second_ref, edge_first_ref, edge_second_ref, bias_first_ref, bias_second_ref,
    out_ref, field, hidden, edge_one, edge_two, stage, sems,
):
    col = place_ref[0]
    at_top = place_ref[1]
    at_bottom = place_ref[2]
    target = jnp.where(col == 0, LANES - 1, 0)
    left_scale = jnp.where(col == 0, 0.0, 1.0)
    right_scale = jnp.where(col == 0, 1.0, 0.0)
    rows_ext = TH + 2 * HALO
    rows_hid = TH + 2

    def taps_sum(full, count, edge, first_row):
        rows = count * hid
        parts = []
        for r in range(count):
            at = first_row + r
            parts.append(
                pltpu.roll(edge[at // LANES], (target - at % LANES + LANES) % LANES, 1)
            )
        fix = jnp.concatenate(parts, axis=0)
        lane = lane_index((rows, LANES))
        left = full[0:rows]
        mid = full[rows : 2 * rows]
        right = full[2 * rows : 3 * rows]
        left_a = pltpu.roll(left[:, :LANES], 1, 1)
        left_b = pltpu.roll(left[:, LANES:], 1, 1)
        right_a = pltpu.roll(right[:, :LANES], LANES - 1, 1)
        right_b = pltpu.roll(right[:, LANES:], LANES - 1, 1)
        out_a = (
            mid[:, :LANES]
            + jnp.where(lane == 0, fix * left_scale, left_a)
            + jnp.where(lane == LANES - 1, right_b, right_a)
        )
        out_b = (
            mid[:, LANES:]
            + jnp.where(lane == 0, left_a, left_b)
            + jnp.where(lane == LANES - 1, fix * right_scale, right_b)
        )
        return out_a, out_b

    @pl.when(pl.program_id(0) == 0)
    def first_layer():
        copies = [
            pltpu.make_async_copy(
                comp_ref, field.at[pl.ds(HALO * channels, TH * channels), :], sems.at[0]
            ),
            pltpu.make_async_copy(up_ref, field.at[pl.ds(0, HALO * channels), :], sems.at[1]),
            pltpu.make_async_copy(
                down_ref,
                field.at[pl.ds((TH + HALO) * channels, HALO * channels), :],
                sems.at[2],
            ),
        ]
        for copy in copies:
            copy.start()
        for copy in copies:
            copy.wait()

        lane = lane_index((channels, LANES))
        strips = []
        for p in range(2):
            head = jnp.where(
                (lane >= p) & (lane < p + HALO),
                pltpu.roll(side_up_ref[p].astype(F32), (LANES - TH % LANES) % LANES, 1),
                side_ref[p, 0].astype(F32),
            )
            base = (TH + HALO) % LANES + p
            tail = jnp.where(
                (lane >= base) & (lane < base + HALO),
                pltpu.roll(side_down_ref[p].astype(F32), TH % LANES, 1),
                side_ref[p, 1].astype(F32),
            )
            strips.append(jnp.concatenate([head, tail], axis=1))
        strips[1] = pltpu.roll(strips[1], EDGE_TILES * LANES - 1, 1)
        near = jnp.where(col == 0, strips[0], strips[1])
        far = jnp.where(col == 0, strips[1], strips[0])

        own = [
            jnp.concatenate([own_ref[p, 0], own_ref[p, 1]], axis=1).astype(F32) for p in range(2)
        ]
        own[1] = pltpu.roll(own[1], EDGE_TILES * LANES - 1, 1)
        own = jnp.where(col == 0, own[1], own[0])
        wide = lane_index((channels, EDGE_TILES * LANES))
        for k, row in enumerate([0, 1, TH + HALO, TH + HALO + 1]):
            tiles = field[row * channels : (row + 1) * channels, :].astype(F32)
            tile = jnp.where(col == 0, tiles[:, LANES:], tiles[:, :LANES])
            moved = pltpu.roll(tile, (row % LANES - target + LANES) % LANES, 1)
            own = jnp.where(wide == row, jnp.concatenate([moved, moved], axis=1), own)

        stack = jnp.concatenate([near, far, own], axis=0).astype(BF16)
        result = jnp.dot(edge_first_ref[...], stack, preferred_element_type=F32)
        span = EDGE_TILES * LANES
        total = result[0 : 2 * hid]
        for a in range(1, 3):
            total = total + pltpu.roll(result[2 * hid * a : 2 * hid * (a + 1)], span - a, 1)
        beyond = total[0:hid] + bias_first_ref[0:hid, 0:1]
        beyond = silu(beyond)
        lane_hid = lane_index((hid, span))
        drop = ((lane_hid == 0) & (at_top == 1)) | ((lane_hid == rows_hid - 1) & (at_bottom == 1))
        beyond = jnp.where(drop | (lane_hid >= rows_hid), 0.0, beyond)
        spill = jnp.dot(edge_second_ref[...], beyond.astype(BF16), preferred_element_type=F32)
        second = spill[0:hid]
        for a in range(1, 3):
            second = second + pltpu.roll(spill[hid * a : hid * (a + 1)], span - a, 1)
        for tile in range(EDGE_TILES):
            edge_one[tile] = total[hid : 2 * hid, tile * LANES : (tile + 1) * LANES]
            edge_two[tile] = second[:, tile * LANES : (tile + 1) * LANES]

        rows = GROUP_ONE * hid
        groups = -(-rows_hid // GROUP_ONE)

        def one_group(g, carry):
            first_row = jnp.minimum(g * GROUP_ONE, rows_hid - GROUP_ONE)
            window = field[
                pl.ds(pl.multiple_of(first_row * channels, 16), (GROUP_ONE + 2) * channels), :
            ]
            full = jnp.dot(first_ref[...], window, preferred_element_type=F32)
            out_a, out_b = taps_sum(full, GROUP_ONE, edge_one, first_row)
            place = pl.ds(pl.multiple_of(first_row * hid, 16), rows)
            bias = bias_first_ref[...]
            hidden[place, 0:LANES] = silu(out_a + bias).astype(BF16)
            hidden[place, LANES:TW] = silu(out_b + bias).astype(BF16)
            return carry

        lax.fori_loop(0, groups, one_group, 0)

        @pl.when(at_top == 1)
        def clear_top():
            hidden[0:hid, :] = jnp.zeros((hid, TW), BF16)

        @pl.when(at_bottom == 1)
        def clear_bottom():
            hidden[(rows_hid - 1) * hid : rows_hid * hid, :] = jnp.zeros((hid, TW), BF16)

    base = pl.program_id(0) * OUT_ROWS
    for g in range(OUT_ROWS // GROUP_TWO):
        row = base + g * GROUP_TWO
        window = hidden[pl.ds(pl.multiple_of(row * hid, 16), (GROUP_TWO + 2) * hid), :]
        full = jnp.dot(second_ref[...], window, preferred_element_type=F32)
        out_a, out_b = taps_sum(full, GROUP_TWO, edge_two, row)
        bias = bias_second_ref[...]
        for half, value in enumerate((out_a + bias, out_b + bias)):
            for r in range(GROUP_TWO):
                stage[half, pl.ds(g * GROUP_TWO + r, hid, stride=OUT_ROWS), :] = value[
                    r * hid : (r + 1) * hid
                ]
    for half in range(2):
        out_ref[:, :, half * LANES : (half + 1) * LANES] = (
            stage[half].reshape(hid, OUT_ROWS, LANES).astype(BF16)
        )


def banded(kernel, count):
    hid, channels = kernel.shape[1:]
    taps = kernel.reshape(3, 3, hid, channels)
    full = jnp.zeros((3, count, hid, count + 2, channels), kernel.dtype)
    for r in range(count):
        full = full.at[:, r, :, r : r + 3, :].set(jnp.transpose(taps, (1, 2, 0, 3)))
    return full.reshape(3 * count * hid, (count + 2) * channels)


def whole_in_vmem():
    return pl.BlockSpec(memory_space=pltpu.VMEM)


def composite(received, cells, templates, col, table, row_weight, capacity, channels):
    peers = received.shape[0]
    per_step = peers // STEPS
    rows = received.shape[1]
    return pl.pallas_call(
        functools.partial(composite_kernel, capacity, channels),
        grid_spec=pltpu.PrefetchScalarGridSpec(
            num_scalar_prefetch=3,
            grid=(STEPS,),
            in_specs=[
                pl.BlockSpec((per_step, rows, LANES), lambda i, *_: (i, 0, 0)),
                whole_in_vmem(),
                whole_in_vmem(),
            ],
            out_specs=[whole_in_vmem(), whole_in_vmem()],
            scratch_shapes=[
                pltpu.VMEM((CBLK + 1, channels, LANES), F32),
                pltpu.VMEM((CBLK + 8, LANES), F32),
                pltpu.VMEM((2, EDGE_TILES, channels, LANES), F32),
            ],
        ),
        out_shape=[
            jax.ShapeDtypeStruct((TH * channels, TW), BF16),
            jax.ShapeDtypeStruct((2, EDGE_TILES, channels, LANES), BF16),
        ],
        compiler_params=pltpu.CompilerParams(
            dimension_semantics=("arbitrary",), vmem_limit_bytes=VMEM_LIMIT
        ),
        name="composite",
    )(cells, templates, col, received, table, row_weight)


def encoder(place, field, up, down, own, side, side_up, side_down, weights, channels, hid):
    return pl.pallas_call(
        functools.partial(encoder_kernel, channels, hid),
        grid_spec=pltpu.PrefetchScalarGridSpec(
            num_scalar_prefetch=1,
            grid=(TH // OUT_ROWS,),
            in_specs=[pl.BlockSpec(memory_space=pl.ANY)] * 3 + [whole_in_vmem()] * 10,
            out_specs=pl.BlockSpec((hid, OUT_ROWS, TW), lambda i, *_: (0, i, 0)),
            scratch_shapes=[
                pltpu.VMEM(((TH + 2 * HALO) * channels, TW), BF16),
                pltpu.VMEM(((TH + 2) * hid, TW), BF16),
                pltpu.VMEM((EDGE_TILES, hid, LANES), F32),
                pltpu.VMEM((EDGE_TILES, hid, LANES), F32),
                pltpu.VMEM((2, hid * OUT_ROWS, LANES), F32),
                pltpu.SemaphoreType.DMA((3,)),
            ],
        ),
        out_shape=jax.ShapeDtypeStruct((hid, TH, TW), BF16),
        compiler_params=pltpu.CompilerParams(
            dimension_semantics=("arbitrary",), vmem_limit_bytes=VMEM_LIMIT
        ),
        name="encoder",
    )(place, field, up, down, own, side, side_up, side_down, *weights)


def layer_weights(conv_first, bias_first, conv_second, bias_second, col):
    hid = conv_first.shape[1]
    inner = jnp.where(col == 0, 2, 0)
    taps_one = conv_first.reshape(3, 3, hid, -1)
    taps_two = conv_second.reshape(3, 3, hid, -1)
    in_one = lax.dynamic_index_in_dim(taps_one, inner, 1, keepdims=False)
    out_one = lax.dynamic_index_in_dim(taps_one, 2 - inner, 1, keepdims=False)
    in_two = lax.dynamic_index_in_dim(taps_two, inner, 1, keepdims=False)
    nothing = jnp.zeros_like(in_one)
    beyond = jnp.concatenate([taps_one[:, 1], in_one, out_one], axis=2)
    onto = jnp.concatenate([in_one, nothing, nothing], axis=2)
    edge_first = jnp.concatenate([beyond, onto], axis=1).reshape(6 * hid, -1)
    edge_second = in_two.reshape(3 * hid, -1)
    spread_one = jnp.broadcast_to(bias_first[None, :, None], (GROUP_ONE, hid, LANES))
    spread_two = jnp.broadcast_to(bias_second[None, :, None], (GROUP_TWO, hid, LANES))
    return (
        banded(conv_first, GROUP_ONE),
        banded(conv_second, GROUP_TWO),
        edge_first,
        edge_second,
        spread_one.reshape(-1, LANES),
        spread_two.reshape(-1, LANES),
    )


def shards(
    sweeps, route_block, route_cell, route_templ, route_count, footprint,
    conv_first, bias_first, conv_second, bias_second,
):
    peers, capacity = route_block.shape[1:]
    channels = sweeps.shape[1]
    hid = conv_first.shape[1]
    rows = lax.axis_size("ty")
    col = lax.axis_index("tx")
    row = lax.axis_index("ty")

    live = lax.broadcasted_iota(jnp.int32, (peers, capacity), 1) < route_count[0][:, None]
    cell = jnp.where(live, route_cell[0], CBLK)
    info = jnp.stack([cell // CELL_BASE, cell % CELL_BASE, route_templ[0]], axis=1).astype(BF16)
    info = jnp.pad(info, ((0, 0), (0, INFO_ROWS - 3), (0, LANES - capacity)))
    packets = sweeps[route_block[0]].reshape(peers, capacity * channels, LANES)
    packets = jnp.concatenate([packets, info], axis=1)
    received = lax.all_to_all(packets, ("ty", "tx"), split_axis=0, concat_axis=0, tiled=True)

    arrived = received[:, capacity * channels : capacity * channels + 3, :capacity].astype(jnp.int32)
    cells = (arrived[:, 0] * CELL_BASE + arrived[:, 1]).reshape(-1)
    templates = arrived[:, 2].reshape(-1)
    table = jnp.transpose(footprint, (0, 2, 1))
    row_weight = jnp.sum(footprint.astype(F32), axis=2)
    field, own = composite(
        received, cells, templates, col.reshape(1), table, row_weight, capacity, channels
    )

    rim = HALO * channels
    onward = [(i, i + 1) for i in range(rows - 1)]
    back = [(i + 1, i) for i in range(rows - 1)]
    cross = [
        (2 * i + j, 2 * k + 1 - j) for i, k in onward for j in range(2)
    ]
    cross_back = [(b, a) for a, b in cross]
    up = lax.ppermute(field[-rim:], "ty", onward)
    down = lax.ppermute(field[:rim], "ty", back)
    side = lax.ppermute(own, "tx", [(0, 1), (1, 0)])
    side_up = lax.ppermute(own[:, 1], ("ty", "tx"), cross)
    side_down = lax.ppermute(own[:, 0], ("ty", "tx"), cross_back)

    place = jnp.stack([col, row == 0, row == rows - 1]).astype(jnp.int32)
    weights = layer_weights(conv_first, bias_first, conv_second, bias_second, col)
    return encoder(place, field, up, down, own, side, side_up, side_down, weights, channels, hid)


def solution(mesh):
    split = ("group", "ty", "tx")
    in_specs = (
        P(split, None, None),
        P(split, None, None),
        P(split, None, None),
        P(split, None, None),
        P(split, None),
        P(),
        P(),
        P(),
        P(),
        P(),
    )
    out_specs = P(None, ("group", "ty"), "tx")
    return jax.shard_map(shards, mesh=mesh, in_specs=in_specs, out_specs=out_specs, check_vma=False)
```

```python
import functools

import jax
import jax.numpy as jnp
from jax import lax
from jax.experimental import pallas as pl
from jax.experimental.pallas import tpu as pltpu
from jax.sharding import PartitionSpec as P

TH = 192
TW = 256
CBLK = 384
LANES = 128
HALO = 2
EDGE_TILES = 2
LANE_BASE = 8
ROW_STEPS = 4
CHUNK = 8
LOADS = 4
GROUP_ONE = 3
GROUP_TWO = 2
OUT_ROWS = 32
PREP = 8
VMEM_LIMIT = 56 * 1024 * 1024

F32 = jnp.float32
BF16 = jnp.bfloat16


def lane_index(shape):
    return lax.broadcasted_iota(jnp.int32, shape, len(shape) - 1)


def silu(value):
    half = 0.5 * value
    return half + half * jnp.tanh(half)


def composite_kernel(
    capacity, channels, cell_ref, templ_ref, col_ref, recv_ref, table_ref, weight_ref,
    comp_ref, edge_ref, acc, den, strip, recv, sems,
):
    step = pl.program_id(0)
    peers = recv_ref.shape[0]
    part = peers // LOADS
    col = col_ref[0]

    @pl.when(step == 0)
    def add_up():
        copies = [
            pltpu.make_async_copy(
                recv_ref.at[pl.ds(k * part, part)], recv.at[pl.ds(k * part, part)], sems.at[k]
            )
            for k in range(LOADS)
        ]
        for copy in copies:
            copy.start()

        def clear_block(i, carry):
            acc[i] = jnp.zeros(acc.shape[1:], F32)
            return carry

        lax.fori_loop(0, CBLK, clear_block, 0, unroll=8)
        den[...] = jnp.zeros(den.shape, F32)
        strip[...] = jnp.zeros(strip.shape, BF16)

        def add_slots(source, carry):
            terms = []
            for q in range(capacity):
                block = recv[source, q * channels : (q + 1) * channels, :]
                template = templ_ref[source * capacity + q]
                terms.append(jnp.dot(block, table_ref[template], preferred_element_type=F32))
            for q in range(capacity):
                cell = cell_ref[source * capacity + q]
                acc[cell] += terms[q]
                template = templ_ref[source * capacity + q]
                den[pl.ds(cell, 1), :] += weight_ref[pl.ds(template, 1), :]
            return carry

        for k in range(LOADS):
            copies[k].wait()
            lax.fori_loop(k * part, (k + 1) * part, add_slots, 0)
        den[...] = 1.0 / (1.0 + den[...])

    rows = TH // ROW_STEPS
    lane = lane_index((channels, LANES))
    near = jnp.where(col == 0, LANES - 1, 0)
    far = jnp.where(col == 0, LANES - 2, 1)

    def some_rows(i, carry):
        base = step * rows + i * CHUNK
        picked = [jnp.zeros((channels, LANES), F32), jnp.zeros((channels, LANES), F32)]
        for u in range(CHUNK):
            r = base + u
            out = pl.multiple_of((i * CHUNK + u) * channels, 16)
            parts = []
            for m in range(2):
                value = acc[2 * r + m] * den[pl.ds(2 * r + m, 1), :]
                comp_ref[pl.ds(out, channels), m * LANES : (m + 1) * LANES] = value.astype(BF16)
                parts.append(value)
            side = jnp.where(col == 0, parts[1], parts[0])
            at = (r + LANE_BASE) % LANES
            for p, start in enumerate((near, far)):
                moved = pltpu.roll(side, (at - start + LANES) % LANES, 1)
                picked[p] = jnp.where(lane == at, moved, picked[p])
        tile = (base + LANE_BASE) // LANES
        first = (base + LANE_BASE) % LANES
        inside = (lane >= first) & (lane < first + CHUNK)
        for p in range(2):
            strip[p, tile] = jnp.where(
                inside, picked[p], strip[p, tile].astype(F32)
            ).astype(BF16)
        return carry

    lax.fori_loop(0, rows // CHUNK, some_rows, 0)

    @pl.when(step == ROW_STEPS - 1)
    def finish():
        edge_ref[...] = strip[...]


def shifted(value, left, right):
    lane = lane_index((value.shape[0], LANES))
    first, last = value[:, :LANES], value[:, LANES:]
    first_left, last_left = pltpu.roll(first, 1, 1), pltpu.roll(last, 1, 1)
    first_right, last_right = pltpu.roll(first, LANES - 1, 1), pltpu.roll(last, LANES - 1, 1)
    before = (
        jnp.where(lane == 0, left, first_left),
        jnp.where(lane == 0, first_left, last_left),
    )
    after = (
        jnp.where(lane == LANES - 1, last_right, first_right),
        jnp.where(lane == LANES - 1, right, last_right),
    )
    return before, after


def encoder_kernel(
    channels, hid, place_ref, comp_ref, up_ref, down_ref, own_ref, side_ref, side_up_ref, side_down_ref,
    first_ref, second_ref, edge_first_ref, bias_first_ref, bias_second_ref,
    out_ref, field, hidden, edge_one, edge_two, stage, sems,
):
    col = place_ref[0]
    at_top = place_ref[1]
    at_bottom = place_ref[2]
    target = jnp.where(col == 0, LANES - 1, 0)
    rows_hid = TH + 2
    span = EDGE_TILES * LANES

    def halo_columns(strip, lane_at):
        moved = pltpu.roll(
            strip[lane_at // LANES], (target - lane_at % LANES + LANES) % LANES, 1
        )
        nothing = jnp.zeros_like(moved)
        return jnp.where(col == 0, nothing, moved), jnp.where(col == 0, moved, nothing)

    @pl.when(pl.program_id(0) == 0)
    def first_layer():
        copies = [
            pltpu.make_async_copy(up_ref, field.at[pl.ds(0, HALO), 1], sems.at[0]),
            pltpu.make_async_copy(down_ref, field.at[pl.ds(TH + HALO, HALO), 1], sems.at[1]),
            pltpu.make_async_copy(comp_ref, field.at[pl.ds(HALO, TH), 1], sems.at[2]),
        ]
        for copy in copies:
            copy.start()
        for copy in copies:
            copy.wait()

        wide = lane_index((channels, span))

        def strip_of(ref, p):
            return jnp.concatenate([ref[p, 0], ref[p, 1]], axis=1).astype(F32)

        def put(strip, lane_at, tile, start):
            moved = pltpu.roll(tile, (lane_at % LANES - start + LANES) % LANES, 1)
            return jnp.where(wide == lane_at, jnp.concatenate([moved, moved], axis=1), strip)

        own = strip_of(own_ref, 0)
        sides = [strip_of(side_ref, p) for p in range(2)]
        starts = [jnp.where(col == 0, 0, LANES - 1), jnp.where(col == 0, 1, LANES - 2)]
        for ref, at_row, lane_at in (
            (side_up_ref, 0, LANE_BASE - HALO),
            (side_down_ref, TH + HALO, TH + LANE_BASE),
        ):
            for k in range(HALO):
                tiles = ref[k].astype(F32)
                tile = jnp.where(col == 0, tiles[:, :LANES], tiles[:, LANES:])
                sides = [put(sides[p], lane_at + k, tile, starts[p]) for p in range(2)]
                tiles = field[at_row + k, 1].astype(F32)
                tile = jnp.where(col == 0, tiles[:, LANES:], tiles[:, :LANES])
                own = put(own, lane_at + k, tile, target)

        stack = jnp.concatenate([sides[0], sides[1], own], axis=0).astype(BF16)
        result = jnp.dot(edge_first_ref[...], stack, preferred_element_type=F32)
        total = result[0:hid]
        for a in range(1, 3):
            total = total + pltpu.roll(result[hid * a : hid * (a + 1)], span - a, 1)
        beyond = silu(total + bias_first_ref[0:hid, 0:1])
        lane_hid = lane_index((hid, span))
        first_lane = LANE_BASE - HALO
        drop = ((lane_hid == first_lane) & (at_top == 1)) | (
            (lane_hid == first_lane + rows_hid - 1) & (at_bottom == 1)
        )
        beyond = jnp.where(drop, 0.0, beyond).astype(BF16)
        for tile in range(EDGE_TILES):
            edge_one[tile] = sides[0][:, tile * LANES : (tile + 1) * LANES].astype(BF16)
            edge_two[tile] = beyond[:, tile * LANES : (tile + 1) * LANES]

        def prepare(i, carry):
            for u in range(PREP):
                row = i * PREP + u
                left, right = halo_columns(edge_one, row + LANE_BASE - HALO)
                before, after = shifted(field[row, 1], left, right)
                for half in range(2):
                    place = slice(half * LANES, (half + 1) * LANES)
                    field[row, 0, :, place] = before[half]
                    field[row, 2, :, place] = after[half]
            return carry

        rows_ext = TH + 2 * HALO
        lax.fori_loop(0, -(-rows_ext // PREP), prepare, 0)

        def one_group(first_row):
            window = field[pl.ds(first_row, GROUP_ONE + 2)]
            window = window.reshape((GROUP_ONE + 2) * 3 * channels, TW)
            full = jnp.dot(first_ref[...], window, preferred_element_type=F32)
            for r in range(GROUP_ONE):
                value = full[r * hid : (r + 1) * hid]
                bias = bias_first_ref[0:hid, :]
                value = silu(value + jnp.concatenate([bias, bias], axis=1)).astype(BF16)
                row = first_row + r
                left, right = halo_columns(edge_two, row + LANE_BASE - HALO)
                before, after = shifted(value, left, right)
                hidden[row, 1] = value
                for half in range(2):
                    place = slice(half * LANES, (half + 1) * LANES)
                    hidden[row, 0, :, place] = before[half]
                    hidden[row, 2, :, place] = after[half]

        def some_groups(i, carry):
            for u in range(PREP):
                one_group((i * PREP + u) * GROUP_ONE)
            return carry

        lax.fori_loop(0, rows_hid // (GROUP_ONE * PREP), some_groups, 0)
        done = rows_hid // (GROUP_ONE * PREP) * GROUP_ONE * PREP
        while done < rows_hid:
            one_group(min(done, rows_hid - GROUP_ONE))
            done += GROUP_ONE

        @pl.when(at_top == 1)
        def clear_top():
            hidden[0] = jnp.zeros(hidden.shape[1:], BF16)

        @pl.when(at_bottom == 1)
        def clear_bottom():
            hidden[rows_hid - 1] = jnp.zeros(hidden.shape[1:], BF16)

    base = pl.program_id(0) * OUT_ROWS
    for g in range(OUT_ROWS // GROUP_TWO):
        window = hidden[pl.ds(base + g * GROUP_TWO, GROUP_TWO + 2)]
        window = window.reshape((GROUP_TWO + 2) * 3 * hid, TW)
        full = jnp.dot(second_ref[...], window, preferred_element_type=F32)
        bias = bias_second_ref[...]
        for half in range(2):
            value = full[:, half * LANES : (half + 1) * LANES] + bias
            for r in range(GROUP_TWO):
                stage[half, pl.ds(g * GROUP_TWO + r, hid, stride=OUT_ROWS), :] = value[
                    r * hid : (r + 1) * hid
                ]
    for half in range(2):
        out_ref[:, :, half * LANES : (half + 1) * LANES] = (
            stage[half].reshape(hid, OUT_ROWS, LANES).astype(BF16)
        )


def banded(kernel, count):
    hid, channels = kernel.shape[1:]
    taps = jnp.transpose(kernel.reshape(3, 3, hid, channels), (2, 0, 1, 3))
    taps = taps.reshape(hid, 9 * channels)
    span = 3 * channels
    rows = [jnp.pad(taps, ((0, 0), (r * span, (count - 1 - r) * span))) for r in range(count)]
    return jnp.concatenate(rows, axis=0)


def whole_in_vmem():
    return pl.BlockSpec(memory_space=pltpu.VMEM)


def composite(received, cells, templates, col, table, row_weight, capacity, channels):
    peers = received.shape[0]
    rows = TH // ROW_STEPS * channels
    return pl.pallas_call(
        functools.partial(composite_kernel, capacity, channels),
        grid_spec=pltpu.PrefetchScalarGridSpec(
            num_scalar_prefetch=3,
            grid=(ROW_STEPS,),
            in_specs=[pl.BlockSpec(memory_space=pl.ANY), whole_in_vmem(), whole_in_vmem()],
            out_specs=[pl.BlockSpec((rows, TW), lambda i, *_: (i, 0)), whole_in_vmem()],
            scratch_shapes=[
                pltpu.VMEM((CBLK + 1, channels, LANES), F32),
                pltpu.VMEM((CBLK + 8, LANES), F32),
                pltpu.VMEM((2, EDGE_TILES, channels, LANES), BF16),
                pltpu.VMEM((peers, capacity * channels, LANES), BF16),
                pltpu.SemaphoreType.DMA((LOADS,)),
            ],
        ),
        out_shape=[
            jax.ShapeDtypeStruct((TH * channels, TW), BF16),
            jax.ShapeDtypeStruct((2, EDGE_TILES, channels, LANES), BF16),
        ],
        compiler_params=pltpu.CompilerParams(
            dimension_semantics=("arbitrary",), vmem_limit_bytes=VMEM_LIMIT
        ),
        name="composite",
    )(cells, templates, col, received, table, row_weight)


def encoder(place, field, up, down, own, side, side_up, side_down, weights, channels, hid):
    return pl.pallas_call(
        functools.partial(encoder_kernel, channels, hid),
        grid_spec=pltpu.PrefetchScalarGridSpec(
            num_scalar_prefetch=1,
            grid=(TH // OUT_ROWS,),
            in_specs=[pl.BlockSpec(memory_space=pl.ANY)] * 3 + [whole_in_vmem()] * 9,
            out_specs=pl.BlockSpec((hid, OUT_ROWS, TW), lambda i, *_: (0, i, 0)),
            scratch_shapes=[
                pltpu.VMEM((-(-(TH + 2 * HALO) // PREP) * PREP, 3, channels, TW), BF16),
                pltpu.VMEM((TH + 2, 3, hid, TW), BF16),
                pltpu.VMEM((EDGE_TILES, channels, LANES), BF16),
                pltpu.VMEM((EDGE_TILES, hid, LANES), BF16),
                pltpu.VMEM((2, hid * OUT_ROWS, LANES), F32),
                pltpu.SemaphoreType.DMA((3,)),
            ],
        ),
        out_shape=jax.ShapeDtypeStruct((hid, TH, TW), BF16),
        compiler_params=pltpu.CompilerParams(
            dimension_semantics=("arbitrary",), vmem_limit_bytes=VMEM_LIMIT
        ),
        name="encoder",
    )(place, field, up, down, own, side, side_up, side_down, *weights)


def layer_weights(conv_first, bias_first, conv_second, bias_second, col):
    hid = conv_first.shape[1]
    taps = conv_first.reshape(3, 3, hid, -1)
    inner = jnp.where(col == 0, taps[:, 2], taps[:, 0])
    outer = jnp.where(col == 0, taps[:, 0], taps[:, 2])
    edge_first = jnp.concatenate([taps[:, 1], inner, outer], axis=2).reshape(3 * hid, -1)
    return (
        banded(conv_first, GROUP_ONE),
        banded(conv_second, GROUP_TWO),
        edge_first,
        jnp.broadcast_to(bias_first[:, None], (hid, LANES)),
        jnp.broadcast_to(bias_second[None, :, None], (GROUP_TWO, hid, LANES)).reshape(-1, LANES),
    )


def shards(
    sweeps, route_block, route_cell, route_templ, route_count, footprint,
    conv_first, bias_first, conv_second, bias_second,
):
    peers, capacity = route_block.shape[1:]
    channels = sweeps.shape[1]
    hid = conv_first.shape[1]
    rows = lax.axis_size("ty")
    col = lax.axis_index("tx")
    row = lax.axis_index("ty")
    tiles = ("ty", "tx")

    packets = sweeps[route_block[0]].reshape(peers, capacity * channels, LANES)
    received = lax.all_to_all(packets, tiles, split_axis=0, concat_axis=0, tiled=True)

    live = lax.broadcasted_iota(jnp.int32, (peers, capacity), 1) < route_count[0][:, None]
    cell = jnp.where(live, route_cell[0], CBLK)
    info = jnp.concatenate([cell, route_templ[0]], axis=1)
    info = lax.all_gather(info, tiles, axis=0, tiled=False)
    info = lax.dynamic_index_in_dim(info, lax.axis_index(tiles), 1, keepdims=False)
    cells = info[:, :capacity].reshape(-1)
    templates = info[:, capacity:].reshape(-1)
    table = jnp.transpose(footprint, (0, 2, 1))
    row_weight = jnp.sum(footprint.astype(F32), axis=2)
    place = jnp.stack([col, row == 0, row == rows - 1]).astype(jnp.int32)
    weights = layer_weights(conv_first, bias_first, conv_second, bias_second, col)
    ready = lax.optimization_barrier((received, cells, templates, table, row_weight, place, weights))
    received, cells, templates, table, row_weight, place, weights = ready
    field, own = composite(
        received, cells, templates, place[:1], table, row_weight, capacity, channels
    )

    field = field.reshape(TH, channels, TW)
    onward = [(i, i + 1) for i in range(rows - 1)]
    back = [(i + 1, i) for i in range(rows - 1)]
    swap = [(0, 1), (1, 0)]
    up = lax.ppermute(field[-HALO:], "ty", onward)
    down = lax.ppermute(field[:HALO], "ty", back)
    side = lax.ppermute(own, "tx", swap)
    side_up = lax.ppermute(up, "tx", swap)
    side_down = lax.ppermute(down, "tx", swap)
    return encoder(place, field, up, down, own, side, side_up, side_down, weights, channels, hid)


def solution(mesh):
    split = ("group", "ty", "tx")
    in_specs = (
        P(split, None, None),
        P(split, None, None),
        P(split, None, None),
        P(split, None, None),
        P(split, None),
        P(),
        P(),
        P(),
        P(),
        P(),
    )
    out_specs = P(None, ("group", "ty"), "tx")
    return jax.shard_map(shards, mesh=mesh, in_specs=in_specs, out_specs=out_specs, check_vma=False)
```

```python
import functools

import jax
import jax.numpy as jnp
from jax import lax
from jax.experimental import pallas as pl
from jax.experimental.pallas import tpu as pltpu
from jax.sharding import PartitionSpec as P

TH = 192
TW = 256
CBLK = 384
LANES = 128
HALO = 2
EDGE_TILES = 2
LANE_BASE = 8
ROW_STEPS = 4
CHUNK = 8
LOADS = 4
GROUP = 2
OUT_ROWS = 16
LAG = 2
PACK_STEPS = 1
INFO_ROWS = 16
CELL_BASE = 32
VMEM_LIMIT = 56 * 1024 * 1024

F32 = jnp.float32
BF16 = jnp.bfloat16


def lane_index(shape):
    return lax.broadcasted_iota(jnp.int32, shape, len(shape) - 1)


def silu(value):
    half = 0.5 * value
    return half + half * jnp.tanh(half)


def pack_kernel(
    channels, block_ref, count_ref, sweeps_ref, cell_ref, templ_ref, out_ref, padded, sem
):
    part = out_ref.shape[0]
    capacity = block_ref.shape[1]
    held = capacity * channels
    first = pl.program_id(0) * part

    def send_tile(d, carry):
        for q in range(capacity):
            pltpu.make_async_copy(
                sweeps_ref.at[block_ref[first + d, q]],
                out_ref.at[d, pl.ds(q * channels, channels), :],
                sem,
            ).start()
        return carry

    lax.fori_loop(0, part, send_tile, 0)
    padded[...] = jnp.zeros(padded.shape, F32)
    padded[0, :, 0:capacity] = cell_ref[0].astype(F32)
    padded[1, :, 0:capacity] = templ_ref[0].astype(F32)
    lane = lane_index((1, LANES))
    which = lax.broadcasted_iota(jnp.int32, (INFO_ROWS, LANES), 0)
    for d in range(part):
        live = lane < count_ref[0, first + d]
        cell = jnp.where(live, padded[0, pl.ds(first + d, 1), :], float(CBLK))
        high = jnp.floor(cell * (1.0 / CELL_BASE))
        low = cell - high * CELL_BASE
        template = padded[1, pl.ds(first + d, 1), :]
        rows = jnp.where(which == 0, high, jnp.where(which == 1, low, template))
        out_ref[d, held : held + INFO_ROWS, :] = rows.astype(BF16)
    arrived = out_ref.at[:, pl.ds(0, held), :]
    pltpu.make_async_copy(arrived, arrived, sem).wait()


def composite_kernel(
    capacity, channels, col_ref, recv_ref, table_ref, weight_ref,
    comp_ref, edge_ref, acc, den, strip, recv, raw, numbers, slots, sems,
):
    step = pl.program_id(0)
    peers = recv_ref.shape[0]
    part = peers // LOADS
    col = col_ref[0]

    @pl.when(step == 0)
    def add_up():
        held = capacity * channels
        listing = pltpu.make_async_copy(
            recv_ref.at[:, pl.ds(held, INFO_ROWS), :], raw, sems.at[LOADS]
        )
        listing.start()
        copies = [
            pltpu.make_async_copy(
                recv_ref.at[pl.ds(k * part, part), pl.ds(0, held), :],
                recv.at[pl.ds(k * part, part)],
                sems.at[k],
            )
            for k in range(LOADS)
        ]
        for copy in copies:
            copy.start()
        listing.wait()
        for source in range(peers):
            rows = raw[source].astype(F32)
            numbers[source : source + 1, :] = (
                rows[0:1] * CELL_BASE + rows[1:2]
            ).astype(jnp.int32)
            numbers[peers + source : peers + source + 1, :] = rows[2:3].astype(jnp.int32)
        moved = pltpu.make_async_copy(numbers, slots, sems.at[LOADS + 1])
        moved.start()

        def clear_block(i, carry):
            acc[i] = jnp.zeros(acc.shape[1:], F32)
            return carry

        lax.fori_loop(0, CBLK, clear_block, 0, unroll=8)
        den[...] = jnp.zeros(den.shape, F32)
        strip[...] = jnp.zeros(strip.shape, BF16)

        moved.wait()

        def add_slots(source, carry):
            terms = []
            for q in range(capacity):
                block = recv[source, q * channels : (q + 1) * channels, :]
                template = slots[peers + source, q]
                terms.append(jnp.dot(block, table_ref[template], preferred_element_type=F32))
            for q in range(capacity):
                cell = slots[source, q]
                acc[cell] += terms[q]
                template = slots[peers + source, q]
                den[pl.ds(cell, 1), :] += weight_ref[pl.ds(template, 1), :]
            return carry

        for k in range(LOADS):
            copies[k].wait()
            lax.fori_loop(k * part, (k + 1) * part, add_slots, 0)
        den[...] = 1.0 / (1.0 + den[...])

    rows = TH // ROW_STEPS
    lane = lane_index((channels, LANES))
    near = jnp.where(col == 0, LANES - 1, 0)
    far = jnp.where(col == 0, LANES - 2, 1)

    def some_rows(i, carry):
        base = step * rows + i * CHUNK
        picked = [jnp.zeros((channels, LANES), F32), jnp.zeros((channels, LANES), F32)]
        for u in range(CHUNK):
            r = base + u
            out = pl.multiple_of((i * CHUNK + u) * channels, 16)
            parts = []
            for m in range(2):
                value = acc[2 * r + m] * den[pl.ds(2 * r + m, 1), :]
                comp_ref[pl.ds(out, channels), m * LANES : (m + 1) * LANES] = value.astype(BF16)
                parts.append(value)
            side = jnp.where(col == 0, parts[1], parts[0])
            at = (r + LANE_BASE) % LANES
            for p, start in enumerate((near, far)):
                moved = pltpu.roll(side, (at - start + LANES) % LANES, 1)
                picked[p] = jnp.where(lane == at, moved, picked[p])
        tile = (base + LANE_BASE) // LANES
        first = (base + LANE_BASE) % LANES
        inside = (lane >= first) & (lane < first + CHUNK)
        for p in range(2):
            strip[p, tile] = jnp.where(
                inside, picked[p], strip[p, tile].astype(F32)
            ).astype(BF16)
        return carry

    lax.fori_loop(0, rows // CHUNK, some_rows, 0)

    @pl.when(step == ROW_STEPS - 1)
    def finish():
        edge_ref[...] = strip[...]


def shifted(value, left, right):
    lane = lane_index((value.shape[0], LANES))
    first, last = value[:, :LANES], value[:, LANES:]
    first_left, last_left = pltpu.roll(first, 1, 1), pltpu.roll(last, 1, 1)
    first_right, last_right = pltpu.roll(first, LANES - 1, 1), pltpu.roll(last, LANES - 1, 1)
    before = (
        jnp.where(lane == 0, left, first_left),
        jnp.where(lane == 0, first_left, last_left),
    )
    after = (
        jnp.where(lane == LANES - 1, last_right, first_right),
        jnp.where(lane == LANES - 1, right, last_right),
    )
    return before, after


def encoder_kernel(
    channels, hid, place_ref, comp_ref, up_ref, down_ref, own_ref, side_ref, side_up_ref, side_down_ref,
    first_ref, second_ref, edge_first_ref, bias_first_ref, bias_second_ref,
    out_ref, field, hidden, edge_one, edge_two, stage, sems,
):
    col = place_ref[0]
    at_top = place_ref[1]
    at_bottom = place_ref[2]
    target = jnp.where(col == 0, LANES - 1, 0)
    rows_hid = TH + 2
    span = EDGE_TILES * LANES
    step = pl.program_id(0)
    parts = TH // OUT_ROWS

    def halo_columns(strip, lane_at):
        moved = pltpu.roll(
            strip[lane_at // LANES], (target - lane_at % LANES + LANES) % LANES, 1
        )
        nothing = jnp.zeros_like(moved)
        return jnp.where(col == 0, nothing, moved), jnp.where(col == 0, moved, nothing)

    def put_row(ref, strip, row, value):
        left, right = halo_columns(strip, row + LANE_BASE - HALO)
        before, after = shifted(value, left, right)
        for half in range(2):
            place = slice(half * LANES, (half + 1) * LANES)
            ref[row, 0, :, place] = before[half]
            ref[row, 2, :, place] = after[half]

    def prepare(row):
        put_row(field, edge_one, row, field[row, 1])

    def first_group(first_row):
        window = field[pl.ds(first_row, GROUP + 2)].reshape((GROUP + 2) * 3 * channels, TW)
        full = jnp.dot(first_ref[...], window, preferred_element_type=F32)
        bias = jnp.concatenate([bias_first_ref[...]] * 2, axis=1)
        for r in range(GROUP):
            value = silu(full[r * hid : (r + 1) * hid] + bias).astype(BF16)
            hidden[first_row + r, 1] = value
            put_row(hidden, edge_two, first_row + r, value)

    def second_group(g, first_row):
        window = hidden[pl.ds(first_row, GROUP + 2)].reshape((GROUP + 2) * 3 * hid, TW)
        full = jnp.dot(second_ref[...], window, preferred_element_type=F32)
        bias = bias_second_ref[...]
        for half in range(2):
            value = full[:, half * LANES : (half + 1) * LANES] + bias
            for r in range(GROUP):
                stage[half, pl.ds(g * GROUP + r, hid, stride=OUT_ROWS), :] = value[
                    r * hid : (r + 1) * hid
                ]

    def rows_copy(k):
        return pltpu.make_async_copy(
            comp_ref.at[pl.ds(k * OUT_ROWS, OUT_ROWS)],
            field.at[pl.ds(HALO + k * OUT_ROWS, OUT_ROWS), 1],
            sems.at[k],
        )

    @pl.when(step == 0)
    def start():
        up = pltpu.make_async_copy(up_ref, field.at[pl.ds(0, HALO), 1], sems.at[parts])
        down = pltpu.make_async_copy(
            down_ref, field.at[pl.ds(TH + HALO, HALO), 1], sems.at[parts + 1]
        )
        up.start()
        down.start()
        for k in range(parts):
            rows_copy(k).start()
        up.wait()
        down.wait()

        wide = lane_index((channels, span))

        def strip_of(ref, p):
            return jnp.concatenate([ref[p, 0], ref[p, 1]], axis=1).astype(F32)

        def put(strip, lane_at, tile, start):
            moved = pltpu.roll(tile, (lane_at % LANES - start + LANES) % LANES, 1)
            return jnp.where(wide == lane_at, jnp.concatenate([moved, moved], axis=1), strip)

        own = strip_of(own_ref, 0)
        sides = [strip_of(side_ref, p) for p in range(2)]
        starts = [jnp.where(col == 0, 0, LANES - 1), jnp.where(col == 0, 1, LANES - 2)]
        for ref, at_row, lane_at in (
            (side_up_ref, 0, LANE_BASE - HALO),
            (side_down_ref, TH + HALO, TH + LANE_BASE),
        ):
            for k in range(HALO):
                tiles = ref[k].astype(F32)
                tile = jnp.where(col == 0, tiles[:, :LANES], tiles[:, LANES:])
                sides = [put(sides[p], lane_at + k, tile, starts[p]) for p in range(2)]
                tiles = field[at_row + k, 1].astype(F32)
                tile = jnp.where(col == 0, tiles[:, LANES:], tiles[:, :LANES])
                own = put(own, lane_at + k, tile, target)

        stack = jnp.concatenate([sides[0], sides[1], own], axis=0).astype(BF16)
        result = jnp.dot(edge_first_ref[...], stack, preferred_element_type=F32)
        total = result[0:hid]
        for a in range(1, 3):
            total = total + pltpu.roll(result[hid * a : hid * (a + 1)], span - a, 1)
        beyond = silu(total + bias_first_ref[:, 0:1])
        lane_hid = lane_index((hid, span))
        first_lane = LANE_BASE - HALO
        drop = ((lane_hid == first_lane) & (at_top == 1)) | (
            (lane_hid == first_lane + rows_hid - 1) & (at_bottom == 1)
        )
        beyond = jnp.where(drop, 0.0, beyond).astype(BF16)
        for tile in range(EDGE_TILES):
            edge_one[tile] = sides[0][:, tile * LANES : (tile + 1) * LANES].astype(BF16)
            edge_two[tile] = beyond[:, tile * LANES : (tile + 1) * LANES]

        rows_copy(0).wait()
        for row in range(2 * HALO):
            prepare(row)
        first_group(0)

        @pl.when(at_top == 1)
        def clear_top():
            hidden[0] = jnp.zeros(hidden.shape[1:], BF16)

    @pl.when(step < parts - 1)
    def arrive():
        rows_copy(step + 1).wait()

    second_row = (step - LAG) * OUT_ROWS
    second_row = jnp.maximum(second_row, 0)
    first_row = jnp.maximum((step - 1) * OUT_ROWS, 0) + GROUP
    ready_row = step * OUT_ROWS + 2 * GROUP
    for g in range(OUT_ROWS // GROUP):
        second_group(g, second_row + g * GROUP)
    for g in range(OUT_ROWS // GROUP):
        first_group(first_row + g * GROUP)
    for r in range(OUT_ROWS):
        prepare(ready_row + r)
    for half in range(2):
        out_ref[:, :, half * LANES : (half + 1) * LANES] = (
            stage[half].reshape(hid, OUT_ROWS, LANES).astype(BF16)
        )

    @pl.when((step == parts) & (at_bottom == 1))
    def clear_bottom():
        hidden[rows_hid - 1] = jnp.zeros(hidden.shape[1:], BF16)


def banded(kernel, count):
    hid, channels = kernel.shape[1:]
    taps = jnp.transpose(kernel.reshape(3, 3, hid, channels), (2, 0, 1, 3))
    taps = taps.reshape(hid, 9 * channels)
    span = 3 * channels
    rows = [jnp.pad(taps, ((0, 0), (r * span, (count - 1 - r) * span))) for r in range(count)]
    return jnp.concatenate(rows, axis=0)


def whole_in_vmem():
    return pl.BlockSpec(memory_space=pltpu.VMEM)


def pack(route_block, route_count, sweeps, route_cell, route_templ):
    peers, capacity = route_block.shape
    channels = sweeps.shape[1]
    rows = capacity * channels + INFO_ROWS
    part = peers // PACK_STEPS
    return pl.pallas_call(
        functools.partial(pack_kernel, channels),
        grid_spec=pltpu.PrefetchScalarGridSpec(
            num_scalar_prefetch=2,
            grid=(PACK_STEPS,),
            in_specs=[pl.BlockSpec(memory_space=pl.ANY), whole_in_vmem(), whole_in_vmem()],
            out_specs=pl.BlockSpec((part, rows, LANES), lambda i, *_: (i, 0, 0)),
            scratch_shapes=[pltpu.VMEM((2, peers, LANES), F32), pltpu.SemaphoreType.DMA],
        ),
        out_shape=jax.ShapeDtypeStruct((peers, rows, LANES), BF16),
        compiler_params=pltpu.CompilerParams(
            dimension_semantics=("arbitrary",), vmem_limit_bytes=VMEM_LIMIT
        ),
        name="pack",
    )(route_block, route_count, sweeps, route_cell, route_templ)


def composite(received, col, table, row_weight, capacity, channels):
    peers = received.shape[0]
    rows = TH // ROW_STEPS * channels
    return pl.pallas_call(
        functools.partial(composite_kernel, capacity, channels),
        grid_spec=pltpu.PrefetchScalarGridSpec(
            num_scalar_prefetch=1,
            grid=(ROW_STEPS,),
            in_specs=[pl.BlockSpec(memory_space=pl.ANY), whole_in_vmem(), whole_in_vmem()],
            out_specs=[pl.BlockSpec((rows, TW), lambda i, *_: (i, 0)), whole_in_vmem()],
            scratch_shapes=[
                pltpu.VMEM((CBLK + 1, channels, LANES), F32),
                pltpu.VMEM((CBLK + 8, LANES), F32),
                pltpu.VMEM((2, EDGE_TILES, channels, LANES), BF16),
                pltpu.VMEM((peers, capacity * channels, LANES), BF16),
                pltpu.VMEM((peers, INFO_ROWS, LANES), BF16),
                pltpu.VMEM((2 * peers, LANES), jnp.int32),
                pltpu.SMEM((2 * peers, LANES), jnp.int32),
                pltpu.SemaphoreType.DMA((LOADS + 2,)),
            ],
        ),
        out_shape=[
            jax.ShapeDtypeStruct((TH * channels, TW), BF16),
            jax.ShapeDtypeStruct((2, EDGE_TILES, channels, LANES), BF16),
        ],
        compiler_params=pltpu.CompilerParams(
            dimension_semantics=("arbitrary",), vmem_limit_bytes=VMEM_LIMIT
        ),
        name="composite",
    )(col, received, table, row_weight)


def encoder(place, field, up, down, own, side, side_up, side_down, weights, channels, hid):
    parts = TH // OUT_ROWS
    steps = parts + LAG
    return pl.pallas_call(
        functools.partial(encoder_kernel, channels, hid),
        grid_spec=pltpu.PrefetchScalarGridSpec(
            num_scalar_prefetch=1,
            grid=(steps,),
            in_specs=[pl.BlockSpec(memory_space=pl.ANY)] * 3 + [whole_in_vmem()] * 9,
            out_specs=pl.BlockSpec(
                (hid, OUT_ROWS, TW), lambda i, *_: (0, jnp.maximum(i - LAG, 0), 0)
            ),
            scratch_shapes=[
                pltpu.VMEM((steps * OUT_ROWS + 2 * GROUP, 3, channels, TW), BF16),
                pltpu.VMEM(((steps - 1) * OUT_ROWS + GROUP, 3, hid, TW), BF16),
                pltpu.VMEM((EDGE_TILES, channels, LANES), BF16),
                pltpu.VMEM((EDGE_TILES, hid, LANES), BF16),
                pltpu.VMEM((2, hid * OUT_ROWS, LANES), F32),
                pltpu.SemaphoreType.DMA((parts + 2,)),
            ],
        ),
        out_shape=jax.ShapeDtypeStruct((hid, TH, TW), BF16),
        compiler_params=pltpu.CompilerParams(
            dimension_semantics=("arbitrary",), vmem_limit_bytes=VMEM_LIMIT
        ),
        name="encoder",
    )(place, field, up, down, own, side, side_up, side_down, *weights)


def layer_weights(conv_first, bias_first, conv_second, bias_second, col):
    hid = conv_first.shape[1]
    taps = conv_first.reshape(3, 3, hid, -1)
    inner = jnp.where(col == 0, taps[:, 2], taps[:, 0])
    outer = jnp.where(col == 0, taps[:, 0], taps[:, 2])
    edge_first = jnp.concatenate([taps[:, 1], inner, outer], axis=2).reshape(3 * hid, -1)
    return (
        banded(conv_first, GROUP),
        banded(conv_second, GROUP),
        edge_first,
        jnp.broadcast_to(bias_first[:, None], (hid, LANES)),
        jnp.broadcast_to(bias_second[None, :, None], (GROUP, hid, LANES)).reshape(-1, LANES),
    )


def shards(
    sweeps, route_block, route_cell, route_templ, route_count, footprint,
    conv_first, bias_first, conv_second, bias_second,
):
    peers, capacity = route_block.shape[1:]
    channels = sweeps.shape[1]
    hid = conv_first.shape[1]
    rows = lax.axis_size("ty")
    col = lax.axis_index("tx")
    row = lax.axis_index("ty")
    tiles = ("ty", "tx")

    packets = pack(route_block[0], route_count, sweeps, route_cell, route_templ)
    received = lax.all_to_all(packets, tiles, split_axis=0, concat_axis=0, tiled=True)
    table = jnp.transpose(footprint, (0, 2, 1))
    row_weight = jnp.sum(footprint.astype(F32), axis=2)
    place = jnp.stack([col, row == 0, row == rows - 1]).astype(jnp.int32)
    weights = layer_weights(conv_first, bias_first, conv_second, bias_second, col)
    received, table, row_weight, place, weights = lax.optimization_barrier(
        (received, table, row_weight, place, weights)
    )
    field, own = composite(received, place[:1], table, row_weight, capacity, channels)

    field = field.reshape(TH, channels, TW)
    onward = [(i, i + 1) for i in range(rows - 1)]
    back = [(i + 1, i) for i in range(rows - 1)]
    swap = [(0, 1), (1, 0)]
    up = lax.ppermute(field[-HALO:], "ty", onward)
    down = lax.ppermute(field[:HALO], "ty", back)
    side = lax.ppermute(own, "tx", swap)
    side_up = lax.ppermute(up, "tx", swap)
    side_down = lax.ppermute(down, "tx", swap)
    return encoder(place, field, up, down, own, side, side_up, side_down, weights, channels, hid)


def solution(mesh):
    split = ("group", "ty", "tx")
    in_specs = (
        P(split, None, None),
        P(split, None, None),
        P(split, None, None),
        P(split, None, None),
        P(split, None),
        P(),
        P(),
        P(),
        P(),
        P(),
    )
    out_specs = P(None, ("group", "ty"), "tx")
    return jax.shard_map(shards, mesh=mesh, in_specs=in_specs, out_specs=out_specs, check_vma=False)
```

```python
import functools

import jax
import jax.numpy as jnp
from jax import lax
from jax.experimental import pallas as pl
from jax.experimental.pallas import tpu as pltpu
from jax.sharding import PartitionSpec as P

TH = 192
TW = 256
CBLK = 384
LANES = 128
HALO = 2
EDGE_TILES = 2
LANE_BASE = 8
ROW_STEPS = 4
CHUNK = 8
LOADS = 4
GROUP = 2
OUT_ROWS = 16
LAG = 2
PACK_STEPS = 1
INFO_ROWS = 16
CELL_BASE = 32
VMEM_LIMIT = 56 * 1024 * 1024

F32 = jnp.float32
BF16 = jnp.bfloat16


def lane_index(shape):
    return lax.broadcasted_iota(jnp.int32, shape, len(shape) - 1)


def silu(value):
    half = 0.5 * value
    return half + half * jnp.tanh(half)


def pack_kernel(
    channels, block_ref, count_ref, sweeps_ref, cell_ref, templ_ref, out_ref, padded, sem
):
    part = out_ref.shape[0]
    capacity = block_ref.shape[1]
    held = capacity * channels
    first = pl.program_id(0) * part

    def send_tile(d, carry):
        for q in range(capacity):
            pltpu.make_async_copy(
                sweeps_ref.at[block_ref[first + d, q]],
                out_ref.at[d, pl.ds(q * channels, channels), :],
                sem,
            ).start()
        return carry

    lax.fori_loop(0, part, send_tile, 0)
    padded[...] = jnp.zeros(padded.shape, F32)
    padded[0, :, 0:capacity] = cell_ref[0].astype(F32)
    padded[1, :, 0:capacity] = templ_ref[0].astype(F32)
    lane = lane_index((1, LANES))
    which = lax.broadcasted_iota(jnp.int32, (INFO_ROWS, LANES), 0)
    for d in range(part):
        live = lane < count_ref[0, first + d]
        cell = jnp.where(live, padded[0, pl.ds(first + d, 1), :], float(CBLK))
        high = jnp.floor(cell * (1.0 / CELL_BASE))
        low = cell - high * CELL_BASE
        template = padded[1, pl.ds(first + d, 1), :]
        rows = jnp.where(which == 0, high, jnp.where(which == 1, low, template))
        out_ref[d, held : held + INFO_ROWS, :] = rows.astype(BF16)
    arrived = out_ref.at[:, pl.ds(0, held), :]
    pltpu.make_async_copy(arrived, arrived, sem).wait()


def composite_kernel(
    capacity, channels, col_ref, recv_ref, table_ref, weight_ref,
    comp_ref, edge_ref, rim_a, rim_b, acc, den, strip, recv, raw, numbers, slots, sems,
):
    step = pl.program_id(0)
    peers = recv_ref.shape[0]
    part = peers // LOADS
    col = col_ref[0]
    odd = col_ref[3]

    @pl.when(step == 0)
    def add_up():
        held = capacity * channels
        listing = pltpu.make_async_copy(
            recv_ref.at[:, pl.ds(held, INFO_ROWS), :], raw, sems.at[LOADS]
        )
        listing.start()
        copies = [
            pltpu.make_async_copy(
                recv_ref.at[pl.ds(k * part, part), pl.ds(0, held), :],
                recv.at[pl.ds(k * part, part)],
                sems.at[k],
            )
            for k in range(LOADS)
        ]
        for copy in copies:
            copy.start()
        listing.wait()
        for source in range(peers):
            rows = raw[source].astype(F32)
            numbers[source : source + 1, :] = (
                rows[0:1] * CELL_BASE + rows[1:2]
            ).astype(jnp.int32)
            numbers[peers + source : peers + source + 1, :] = rows[2:3].astype(jnp.int32)
        moved = pltpu.make_async_copy(numbers, slots, sems.at[LOADS + 1])
        moved.start()

        def clear_block(i, carry):
            acc[i] = jnp.zeros(acc.shape[1:], F32)
            return carry

        lax.fori_loop(0, CBLK, clear_block, 0, unroll=8)
        den[...] = jnp.zeros(den.shape, F32)
        strip[...] = jnp.zeros(strip.shape, BF16)

        moved.wait()

        def add_slots(source, carry):
            terms = []
            for q in range(capacity):
                block = recv[source, q * channels : (q + 1) * channels, :]
                template = slots[peers + source, q]
                terms.append(jnp.dot(block, table_ref[template], preferred_element_type=F32))
            for q in range(capacity):
                cell = slots[source, q]
                acc[cell] += terms[q]
                template = slots[peers + source, q]
                den[pl.ds(cell, 1), :] += weight_ref[pl.ds(template, 1), :]
            return carry

        for k in range(LOADS):
            copies[k].wait()
            lax.fori_loop(k * part, (k + 1) * part, add_slots, 0)
        den[...] = 1.0 / (1.0 + den[...])

    rows = TH // ROW_STEPS
    lane = lane_index((channels, LANES))
    near = jnp.where(col == 0, LANES - 1, 0)
    far = jnp.where(col == 0, LANES - 2, 1)

    def some_rows(i, carry):
        base = step * rows + i * CHUNK
        picked = [jnp.zeros((channels, LANES), F32), jnp.zeros((channels, LANES), F32)]
        for u in range(CHUNK):
            r = base + u
            out = pl.multiple_of((i * CHUNK + u) * channels, 16)
            parts = []
            for m in range(2):
                value = acc[2 * r + m] * den[pl.ds(2 * r + m, 1), :]
                comp_ref[pl.ds(out, channels), m * LANES : (m + 1) * LANES] = value.astype(BF16)
                parts.append(value)
            side = jnp.where(col == 0, parts[1], parts[0])
            at = (r + LANE_BASE) % LANES
            for p, start in enumerate((near, far)):
                moved = pltpu.roll(side, (at - start + LANES) % LANES, 1)
                picked[p] = jnp.where(lane == at, moved, picked[p])
        tile = (base + LANE_BASE) // LANES
        first = (base + LANE_BASE) % LANES
        inside = (lane >= first) & (lane < first + CHUNK)
        for p in range(2):
            strip[p, tile] = jnp.where(
                inside, picked[p], strip[p, tile].astype(F32)
            ).astype(BF16)
        return carry

    lax.fori_loop(0, rows // CHUNK, some_rows, 0)

    rim = HALO * channels
    top = step == 0
    bottom = step == ROW_STEPS - 1

    @pl.when((top & (odd == 1)) | (bottom & (odd == 0)))
    def rim_to_a():
        begin = pl.multiple_of(jnp.where(top, 0, rows * channels - rim), 16)
        rim_a[...] = comp_ref[pl.ds(begin, rim), :].reshape(HALO, channels, TW)

    @pl.when((top & (odd == 0)) | (bottom & (odd == 1)))
    def rim_to_b():
        begin = pl.multiple_of(jnp.where(top, 0, rows * channels - rim), 16)
        rim_b[...] = comp_ref[pl.ds(begin, rim), :].reshape(HALO, channels, TW)

    @pl.when(bottom)
    def finish():
        edge_ref[...] = strip[...]


def shifted(value, left, right):
    lane = lane_index((value.shape[0], LANES))
    first, last = value[:, :LANES], value[:, LANES:]
    first_left, last_left = pltpu.roll(first, 1, 1), pltpu.roll(last, 1, 1)
    first_right, last_right = pltpu.roll(first, LANES - 1, 1), pltpu.roll(last, LANES - 1, 1)
    before = (
        jnp.where(lane == 0, left, first_left),
        jnp.where(lane == 0, first_left, last_left),
    )
    after = (
        jnp.where(lane == LANES - 1, last_right, first_right),
        jnp.where(lane == LANES - 1, right, last_right),
    )
    return before, after


def encoder_kernel(
    channels, hid, place_ref, comp_ref, rim_a_ref, rim_b_ref, own_ref, side_ref, side_a_ref, side_b_ref,
    first_ref, second_ref, edge_first_ref, bias_first_ref, bias_second_ref,
    out_ref, field, hidden, edge_one, edge_two, biases, stage, sems,
):
    col = place_ref[0]
    at_top = place_ref[1]
    at_bottom = place_ref[2]
    odd = place_ref[3]
    target = jnp.where(col == 0, LANES - 1, 0)
    rows_hid = TH + 2
    span = EDGE_TILES * LANES
    step = pl.program_id(0)
    parts = TH // OUT_ROWS

    def halo_columns(strip, lane_at):
        moved = pltpu.roll(
            strip[lane_at // LANES], (target - lane_at % LANES + LANES) % LANES, 1
        )
        nothing = jnp.zeros_like(moved)
        return jnp.where(col == 0, nothing, moved), jnp.where(col == 0, moved, nothing)

    def put_row(ref, strip, row, value):
        left, right = halo_columns(strip, row + LANE_BASE - HALO)
        before, after = shifted(value, left, right)
        for half in range(2):
            place = slice(half * LANES, (half + 1) * LANES)
            ref[row, 0, :, place] = before[half]
            ref[row, 2, :, place] = after[half]

    def prepare(row):
        put_row(field, edge_one, row, field[row, 1])

    def first_group(first_row):
        window = field[pl.ds(first_row, GROUP + 2)].reshape((GROUP + 2) * 3 * channels, TW)
        full = jnp.dot(first_ref[...], window, preferred_element_type=F32)
        bias = jnp.concatenate([biases[0]] * 2, axis=1)
        for r in range(GROUP):
            value = silu(full[r * hid : (r + 1) * hid] + bias).astype(BF16)
            hidden[first_row + r, 1] = value
            put_row(hidden, edge_two, first_row + r, value)

    def second_group(g, first_row):
        window = hidden[pl.ds(first_row, GROUP + 2)].reshape((GROUP + 2) * 3 * hid, TW)
        full = jnp.dot(second_ref[...], window, preferred_element_type=F32)
        bias = jnp.concatenate([biases[1]] * GROUP, axis=0)
        for half in range(2):
            value = full[:, half * LANES : (half + 1) * LANES] + bias
            for r in range(GROUP):
                stage[half, g * GROUP + r] = value[r * hid : (r + 1) * hid]

    def rows_copy(k):
        return pltpu.make_async_copy(
            comp_ref.at[pl.ds(k * OUT_ROWS, OUT_ROWS)],
            field.at[pl.ds(HALO + k * OUT_ROWS, OUT_ROWS), 1],
            sems.at[k],
        )

    @pl.when(step == 0)
    def start():
        row_a = jnp.where(odd == 1, 0, TH + HALO)
        row_b = jnp.where(odd == 1, TH + HALO, 0)
        rims = [
            pltpu.make_async_copy(
                ref, field.at[pl.ds(row, HALO), 1], sems.at[parts + k]
            )
            for k, (ref, row) in enumerate(((rim_a_ref, row_a), (rim_b_ref, row_b)))
        ]
        for rim in rims:
            rim.start()
        for k in range(parts):
            rows_copy(k).start()
        for rim in rims:
            rim.wait()

        across = lax.broadcasted_iota(jnp.int32, (hid, hid), 0)
        for k, ref in enumerate((bias_first_ref, bias_second_ref)):
            square = jnp.where(across == lane_index((hid, hid)), ref[...], 0.0)
            biases[k] = jnp.broadcast_to(jnp.sum(square, axis=1, keepdims=True), (hid, LANES))

        wide = lane_index((channels, span))

        def strip_of(ref, p):
            return jnp.concatenate([ref[p, 0], ref[p, 1]], axis=1).astype(F32)

        def put(strip, lane_at, tile, start):
            moved = pltpu.roll(tile, (lane_at % LANES - start + LANES) % LANES, 1)
            return jnp.where(wide == lane_at, jnp.concatenate([moved, moved], axis=1), strip)

        own = strip_of(own_ref, 0)
        sides = [strip_of(side_ref, p) for p in range(2)]
        starts = [jnp.where(col == 0, 0, LANES - 1), jnp.where(col == 0, 1, LANES - 2)]
        for above, at_row, lane_at in (
            (1, 0, LANE_BASE - HALO),
            (0, TH + HALO, TH + LANE_BASE),
        ):
            for k in range(HALO):
                tiles = jnp.where(
                    odd == above, side_a_ref[k].astype(F32), side_b_ref[k].astype(F32)
                )
                tile = jnp.where(col == 0, tiles[:, :LANES], tiles[:, LANES:])
                sides = [put(sides[p], lane_at + k, tile, starts[p]) for p in range(2)]
                tiles = field[at_row + k, 1].astype(F32)
                tile = jnp.where(col == 0, tiles[:, LANES:], tiles[:, :LANES])
                own = put(own, lane_at + k, tile, target)

        stack = jnp.concatenate([sides[0], sides[1], own], axis=0).astype(BF16)
        result = jnp.dot(edge_first_ref[...], stack, preferred_element_type=F32)
        total = result[0:hid]
        for a in range(1, 3):
            total = total + pltpu.roll(result[hid * a : hid * (a + 1)], span - a, 1)
        beyond = silu(total + jnp.concatenate([biases[0]] * EDGE_TILES, axis=1))
        lane_hid = lane_index((hid, span))
        first_lane = LANE_BASE - HALO
        drop = ((lane_hid == first_lane) & (at_top == 1)) | (
            (lane_hid == first_lane + rows_hid - 1) & (at_bottom == 1)
        )
        beyond = jnp.where(drop, 0.0, beyond).astype(BF16)
        for tile in range(EDGE_TILES):
            edge_one[tile] = sides[0][:, tile * LANES : (tile + 1) * LANES].astype(BF16)
            edge_two[tile] = beyond[:, tile * LANES : (tile + 1) * LANES]

        rows_copy(0).wait()
        for row in range(2 * HALO):
            prepare(row)
        first_group(0)

        @pl.when(at_top == 1)
        def clear_top():
            hidden[0] = jnp.zeros(hidden.shape[1:], BF16)

    @pl.when(step < parts - 1)
    def arrive():
        rows_copy(step + 1).wait()

    @pl.when((step >= LAG) & (step < parts))
    def steady():
        second_row = jnp.maximum((step - LAG) * OUT_ROWS, 0)
        first_row = jnp.maximum((step - 1) * OUT_ROWS, 0) + GROUP
        for g in range(OUT_ROWS // GROUP):
            second_group(g, second_row + g * GROUP)
        for g in range(OUT_ROWS // GROUP):
            first_group(first_row + g * GROUP)
        for r in range(OUT_ROWS):
            prepare(step * OUT_ROWS + 2 * GROUP + r)
        for half in range(2):
            out_ref[:, :, half * LANES : (half + 1) * LANES] = jnp.swapaxes(stage[half], 0, 1).astype(
                BF16
            )


    @pl.when(step >= parts)
    def last_ones():
        for g in range(OUT_ROWS // GROUP):
            second_group(g, (step - LAG) * OUT_ROWS + g * GROUP)
        for half in range(2):
            out_ref[:, :, half * LANES : (half + 1) * LANES] = jnp.swapaxes(
                stage[half], 0, 1
            ).astype(BF16)

    @pl.when(((step >= 1) & (step < LAG)) | (step == parts))
    def first_ones():
        for g in range(OUT_ROWS // GROUP):
            first_group((step - 1) * OUT_ROWS + GROUP + g * GROUP)

    @pl.when(step < LAG)
    def shift_ones():
        for r in range(OUT_ROWS):
            prepare(step * OUT_ROWS + 2 * GROUP + r)

    @pl.when((step == parts) & (at_bottom == 1))
    def clear_bottom():
        hidden[rows_hid - 1] = jnp.zeros(hidden.shape[1:], BF16)


def banded(kernel, count):
    hid, channels = kernel.shape[1:]
    taps = jnp.transpose(kernel.reshape(3, 3, hid, channels), (2, 0, 1, 3))
    taps = taps.reshape(hid, 9 * channels)
    span = 3 * channels
    rows = [jnp.pad(taps, ((0, 0), (r * span, (count - 1 - r) * span))) for r in range(count)]
    return jnp.concatenate(rows, axis=0)


def whole_in_vmem():
    return pl.BlockSpec(memory_space=pltpu.VMEM)


def pack(route_block, route_count, sweeps, route_cell, route_templ):
    peers, capacity = route_block.shape
    channels = sweeps.shape[1]
    rows = capacity * channels + INFO_ROWS
    part = peers // PACK_STEPS
    return pl.pallas_call(
        functools.partial(pack_kernel, channels),
        grid_spec=pltpu.PrefetchScalarGridSpec(
            num_scalar_prefetch=2,
            grid=(PACK_STEPS,),
            in_specs=[pl.BlockSpec(memory_space=pl.ANY), whole_in_vmem(), whole_in_vmem()],
            out_specs=pl.BlockSpec((part, rows, LANES), lambda i, *_: (i, 0, 0)),
            scratch_shapes=[pltpu.VMEM((2, peers, LANES), F32), pltpu.SemaphoreType.DMA],
        ),
        out_shape=jax.ShapeDtypeStruct((peers, rows, LANES), BF16),
        compiler_params=pltpu.CompilerParams(
            dimension_semantics=("arbitrary",), vmem_limit_bytes=VMEM_LIMIT
        ),
        name="pack",
    )(route_block, route_count, sweeps, route_cell, route_templ)


def composite(received, col, table, row_weight, capacity, channels):
    peers = received.shape[0]
    rows = TH // ROW_STEPS * channels
    return pl.pallas_call(
        functools.partial(composite_kernel, capacity, channels),
        grid_spec=pltpu.PrefetchScalarGridSpec(
            num_scalar_prefetch=1,
            grid=(ROW_STEPS,),
            in_specs=[pl.BlockSpec(memory_space=pl.ANY), whole_in_vmem(), whole_in_vmem()],
            out_specs=[pl.BlockSpec((rows, TW), lambda i, *_: (i, 0))] + [whole_in_vmem()] * 3,
            scratch_shapes=[
                pltpu.VMEM((CBLK + 1, channels, LANES), F32),
                pltpu.VMEM((CBLK + 8, LANES), F32),
                pltpu.VMEM((2, EDGE_TILES, channels, LANES), BF16),
                pltpu.VMEM((peers, capacity * channels, LANES), BF16),
                pltpu.VMEM((peers, INFO_ROWS, LANES), BF16),
                pltpu.VMEM((2 * peers, LANES), jnp.int32),
                pltpu.SMEM((2 * peers, LANES), jnp.int32),
                pltpu.SemaphoreType.DMA((LOADS + 2,)),
            ],
        ),
        out_shape=[
            jax.ShapeDtypeStruct((TH * channels, TW), BF16),
            jax.ShapeDtypeStruct((2, EDGE_TILES, channels, LANES), BF16),
            jax.ShapeDtypeStruct((HALO, channels, TW), BF16),
            jax.ShapeDtypeStruct((HALO, channels, TW), BF16),
        ],
        compiler_params=pltpu.CompilerParams(
            dimension_semantics=("arbitrary",), vmem_limit_bytes=VMEM_LIMIT
        ),
        name="composite",
    )(col, received, table, row_weight)


def encoder(place, field, rim_a, rim_b, own, side, side_a, side_b, weights, channels, hid):
    parts = TH // OUT_ROWS
    steps = parts + LAG
    return pl.pallas_call(
        functools.partial(encoder_kernel, channels, hid),
        grid_spec=pltpu.PrefetchScalarGridSpec(
            num_scalar_prefetch=1,
            grid=(steps,),
            in_specs=[pl.BlockSpec(memory_space=pl.ANY)] * 3 + [whole_in_vmem()] * 9,
            out_specs=pl.BlockSpec(
                (hid, OUT_ROWS, TW), lambda i, *_: (0, jnp.maximum(i - LAG, 0), 0)
            ),
            scratch_shapes=[
                pltpu.VMEM((steps * OUT_ROWS + 2 * GROUP, 3, channels, TW), BF16),
                pltpu.VMEM(((steps - 1) * OUT_ROWS + GROUP, 3, hid, TW), BF16),
                pltpu.VMEM((EDGE_TILES, channels, LANES), BF16),
                pltpu.VMEM((EDGE_TILES, hid, LANES), BF16),
                pltpu.VMEM((2, hid, LANES), F32),
                pltpu.VMEM((2, OUT_ROWS, hid, LANES), F32),
                pltpu.SemaphoreType.DMA((parts + 2,)),
            ],
        ),
        out_shape=jax.ShapeDtypeStruct((hid, TH, TW), BF16),
        compiler_params=pltpu.CompilerParams(
            dimension_semantics=("arbitrary",), vmem_limit_bytes=VMEM_LIMIT
        ),
        name="encoder",
    )(place, field, rim_a, rim_b, own, side, side_a, side_b, *weights)


def layer_weights(conv_first, bias_first, conv_second, bias_second, col):
    hid = conv_first.shape[1]
    taps = conv_first.reshape(3, 3, hid, -1)
    inner = jnp.where(col == 0, taps[:, 2], taps[:, 0])
    outer = jnp.where(col == 0, taps[:, 0], taps[:, 2])
    edge_first = jnp.concatenate([taps[:, 1], inner, outer], axis=2).reshape(3 * hid, -1)
    return (
        banded(conv_first, GROUP),
        banded(conv_second, GROUP),
        edge_first,
        bias_first.reshape(1, hid),
        bias_second.reshape(1, hid),
    )


def shards(
    sweeps, route_block, route_cell, route_templ, route_count, footprint,
    conv_first, bias_first, conv_second, bias_second,
):
    peers, capacity = route_block.shape[1:]
    channels = sweeps.shape[1]
    hid = conv_first.shape[1]
    rows = lax.axis_size("ty")
    col = lax.axis_index("tx")
    row = lax.axis_index("ty")
    tiles = ("ty", "tx")

    packets = pack(route_block[0], route_count, sweeps, route_cell, route_templ)
    received = lax.all_to_all(packets, tiles, split_axis=0, concat_axis=0, tiled=True)
    table = jnp.transpose(footprint, (0, 2, 1))
    row_weight = jnp.sum(footprint.astype(F32), axis=2)
    place = jnp.stack([col, row == 0, row == rows - 1, row % 2]).astype(jnp.int32)
    weights = layer_weights(conv_first, bias_first, conv_second, bias_second, col)
    received, table, row_weight, place, weights = lax.optimization_barrier(
        (received, table, row_weight, place, weights)
    )
    field, own, rim_a, rim_b = composite(received, place, table, row_weight, capacity, channels)

    field = field.reshape(TH, channels, TW)
    swap = [(0, 1), (1, 0)]
    pairs_a = [p for i in range(0, rows - 1, 2) for p in ((i, i + 1), (i + 1, i))]
    pairs_b = [p for i in range(1, rows - 1, 2) for p in ((i, i + 1), (i + 1, i))]
    side = lax.ppermute(own, "tx", swap)
    rim_a = lax.ppermute(rim_a, "ty", pairs_a)
    rim_b = lax.ppermute(rim_b, "ty", pairs_b)
    side_a = lax.ppermute(rim_a, "tx", swap)
    side_b = lax.ppermute(rim_b, "tx", swap)
    return encoder(place, field, rim_a, rim_b, own, side, side_a, side_b, weights, channels, hid)


def solution(mesh):
    split = ("group", "ty", "tx")
    in_specs = (
        P(split, None, None),
        P(split, None, None),
        P(split, None, None),
        P(split, None, None),
        P(split, None),
        P(),
        P(),
        P(),
        P(),
        P(),
    )
    out_specs = P(None, ("group", "ty"), "tx")
    return jax.shard_map(shards, mesh=mesh, in_specs=in_specs, out_specs=out_specs, check_vma=False)
```

```python
import functools

import jax
import jax.numpy as jnp
from jax import lax
from jax.experimental import pallas as pl
from jax.experimental.pallas import tpu as pltpu
from jax.sharding import PartitionSpec as P

TH = 192
TW = 256
CBLK = 384
LANES = 128
HALO = 2
EDGE_TILES = 2
LANE_BASE = 8
ROW_STEPS = 4
CHUNK = 8
LOADS = 4
GROUP = 2
OUT_ROWS = 16
LAG = 2
PACK_STEPS = 1
INFO_ROWS = 16
CELL_BASE = 32
MIB = 1024 * 1024
PACK_VMEM = 12 * MIB
COMPOSITE_VMEM = 26 * MIB
ENCODER_VMEM = 45 * MIB

F32 = jnp.float32
BF16 = jnp.bfloat16


def lane_index(shape):
    return lax.broadcasted_iota(jnp.int32, shape, len(shape) - 1)


def silu(value):
    half = 0.5 * value
    return half + half * jnp.tanh(half)


def pack_kernel(
    channels, block_ref, count_ref, sweeps_ref, cell_ref, templ_ref, out_ref, padded, sem
):
    part = out_ref.shape[0]
    capacity = block_ref.shape[1]
    held = capacity * channels
    first = pl.program_id(0) * part

    def send_tile(d, carry):
        for q in range(capacity):
            pltpu.make_async_copy(
                sweeps_ref.at[block_ref[first + d, q]],
                out_ref.at[d, pl.ds(q * channels, channels), :],
                sem,
            ).start()
        return carry

    lax.fori_loop(0, part, send_tile, 0)
    padded[...] = jnp.zeros(padded.shape, F32)
    padded[0, :, 0:capacity] = cell_ref[0].astype(F32)
    padded[1, :, 0:capacity] = templ_ref[0].astype(F32)
    lane = lane_index((1, LANES))
    which = lax.broadcasted_iota(jnp.int32, (INFO_ROWS, LANES), 0)
    for d in range(part):
        live = lane < count_ref[0, first + d]
        cell = jnp.where(live, padded[0, pl.ds(first + d, 1), :], float(CBLK))
        high = jnp.floor(cell * (1.0 / CELL_BASE))
        low = cell - high * CELL_BASE
        template = padded[1, pl.ds(first + d, 1), :]
        rows = jnp.where(which == 0, high, jnp.where(which == 1, low, template))
        out_ref[d, held : held + INFO_ROWS, :] = rows.astype(BF16)
    arrived = out_ref.at[:, pl.ds(0, held), :]
    pltpu.make_async_copy(arrived, arrived, sem).wait()


def composite_kernel(
    capacity, channels, col_ref, recv_ref, table_ref, weight_ref,
    comp_ref, edge_ref, rim_a, rim_b, acc, den, strip, recv, raw, numbers, slots, sems,
):
    step = pl.program_id(0)
    peers = recv_ref.shape[0]
    part = peers // LOADS
    col = col_ref[0]
    odd = col_ref[3]

    @pl.when(step == 0)
    def add_up():
        held = capacity * channels
        listing = pltpu.make_async_copy(
            recv_ref.at[:, pl.ds(held, INFO_ROWS), :], raw, sems.at[LOADS]
        )
        listing.start()
        copies = [
            pltpu.make_async_copy(
                recv_ref.at[pl.ds(k * part, part), pl.ds(0, held), :],
                recv.at[pl.ds(k * part, part)],
                sems.at[k],
            )
            for k in range(LOADS)
        ]
        for copy in copies:
            copy.start()
        listing.wait()
        for source in range(peers):
            rows = raw[source].astype(F32)
            numbers[source : source + 1, :] = (
                rows[0:1] * CELL_BASE + rows[1:2]
            ).astype(jnp.int32)
            numbers[peers + source : peers + source + 1, :] = rows[2:3].astype(jnp.int32)
        moved = pltpu.make_async_copy(numbers, slots, sems.at[LOADS + 1])
        moved.start()

        def clear_block(i, carry):
            acc[i] = jnp.zeros(acc.shape[1:], F32)
            return carry

        lax.fori_loop(0, CBLK, clear_block, 0, unroll=8)
        den[...] = jnp.zeros(den.shape, F32)
        strip[...] = jnp.zeros(strip.shape, BF16)

        moved.wait()

        def add_slots(source, carry):
            terms = []
            for q in range(capacity):
                block = recv[source, q * channels : (q + 1) * channels, :]
                template = slots[peers + source, q]
                terms.append(jnp.dot(block, table_ref[template], preferred_element_type=F32))
            for q in range(capacity):
                cell = slots[source, q]
                acc[cell] += terms[q]
                template = slots[peers + source, q]
                den[pl.ds(cell, 1), :] += weight_ref[pl.ds(template, 1), :]
            return carry

        for k in range(LOADS):
            copies[k].wait()
            lax.fori_loop(k * part, (k + 1) * part, add_slots, 0)
        den[...] = 1.0 / (1.0 + den[...])

    rows = TH // ROW_STEPS
    lane = lane_index((channels, LANES))
    near = jnp.where(col == 0, LANES - 1, 0)
    far = jnp.where(col == 0, LANES - 2, 1)

    def some_rows(i, carry):
        base = step * rows + i * CHUNK
        picked = [jnp.zeros((channels, LANES), F32), jnp.zeros((channels, LANES), F32)]
        for u in range(CHUNK):
            r = base + u
            out = pl.multiple_of((i * CHUNK + u) * channels, 16)
            parts = []
            for m in range(2):
                value = acc[2 * r + m] * den[pl.ds(2 * r + m, 1), :]
                comp_ref[pl.ds(out, channels), m * LANES : (m + 1) * LANES] = value.astype(BF16)
                parts.append(value)
            side = jnp.where(col == 0, parts[1], parts[0])
            at = (r + LANE_BASE) % LANES
            for p, start in enumerate((near, far)):
                moved = pltpu.roll(side, (at - start + LANES) % LANES, 1)
                picked[p] = jnp.where(lane == at, moved, picked[p])
        tile = (base + LANE_BASE) // LANES
        first = (base + LANE_BASE) % LANES
        inside = (lane >= first) & (lane < first + CHUNK)
        for p in range(2):
            strip[p, tile] = jnp.where(
                inside, picked[p], strip[p, tile].astype(F32)
            ).astype(BF16)
        return carry

    lax.fori_loop(0, rows // CHUNK, some_rows, 0)

    rim = HALO * channels
    top = step == 0
    bottom = step == ROW_STEPS - 1

    @pl.when((top & (odd == 1)) | (bottom & (odd == 0)))
    def rim_to_a():
        begin = pl.multiple_of(jnp.where(top, 0, rows * channels - rim), 16)
        rim_a[...] = comp_ref[pl.ds(begin, rim), :].reshape(HALO, channels, TW)

    @pl.when((top & (odd == 0)) | (bottom & (odd == 1)))
    def rim_to_b():
        begin = pl.multiple_of(jnp.where(top, 0, rows * channels - rim), 16)
        rim_b[...] = comp_ref[pl.ds(begin, rim), :].reshape(HALO, channels, TW)

    @pl.when(bottom)
    def finish():
        edge_ref[...] = strip[...]


def shifted(value, left, right):
    lane = lane_index((value.shape[0], LANES))
    first, last = value[:, :LANES], value[:, LANES:]
    first_left, last_left = pltpu.roll(first, 1, 1), pltpu.roll(last, 1, 1)
    first_right, last_right = pltpu.roll(first, LANES - 1, 1), pltpu.roll(last, LANES - 1, 1)
    before = (
        jnp.where(lane == 0, left, first_left),
        jnp.where(lane == 0, first_left, last_left),
    )
    after = (
        jnp.where(lane == LANES - 1, last_right, first_right),
        jnp.where(lane == LANES - 1, right, last_right),
    )
    return before, after


def encoder_kernel(
    channels, hid, place_ref, comp_ref, rim_a_ref, rim_b_ref, own_ref, side_ref, side_a_ref, side_b_ref,
    first_ref, second_ref, edge_first_ref, bias_first_ref, bias_second_ref,
    out_ref, field, hidden, edge_one, edge_two, biases, stage, sems,
):
    col = place_ref[0]
    at_top = place_ref[1]
    at_bottom = place_ref[2]
    odd = place_ref[3]
    target = jnp.where(col == 0, LANES - 1, 0)
    rows_hid = TH + 2
    span = EDGE_TILES * LANES
    step = pl.program_id(0)
    parts = TH // OUT_ROWS

    def halo_columns(strip, lane_at):
        moved = pltpu.roll(
            strip[lane_at // LANES], (target - lane_at % LANES + LANES) % LANES, 1
        )
        nothing = jnp.zeros_like(moved)
        return jnp.where(col == 0, nothing, moved), jnp.where(col == 0, moved, nothing)

    def put_row(ref, strip, row, value):
        left, right = halo_columns(strip, row + LANE_BASE - HALO)
        before, after = shifted(value, left, right)
        for half in range(2):
            place = slice(half * LANES, (half + 1) * LANES)
            ref[row, 0, :, place] = before[half]
            ref[row, 2, :, place] = after[half]

    def prepare(row):
        put_row(field, edge_one, row, field[row, 1])

    def first_group(first_row):
        window = field[pl.ds(first_row, GROUP + 2)].reshape((GROUP + 2) * 3 * channels, TW)
        full = jnp.dot(first_ref[...], window, preferred_element_type=F32)
        bias = jnp.concatenate([biases[0]] * 2, axis=1)
        for r in range(GROUP):
            value = silu(full[r * hid : (r + 1) * hid] + bias).astype(BF16)
            hidden[first_row + r, 1] = value
            put_row(hidden, edge_two, first_row + r, value)

    def second_group(g, first_row):
        window = hidden[pl.ds(first_row, GROUP + 2)].reshape((GROUP + 2) * 3 * hid, TW)
        full = jnp.dot(second_ref[...], window, preferred_element_type=F32)
        bias = jnp.concatenate([biases[1]] * GROUP, axis=0)
        for half in range(2):
            value = full[:, half * LANES : (half + 1) * LANES] + bias
            for r in range(GROUP):
                stage[half, g * GROUP + r] = value[r * hid : (r + 1) * hid]

    def rows_copy(k):
        return pltpu.make_async_copy(
            comp_ref.at[pl.ds(k * OUT_ROWS, OUT_ROWS)],
            field.at[pl.ds(HALO + k * OUT_ROWS, OUT_ROWS), 1],
            sems.at[k],
        )

    @pl.when(step == 0)
    def start():
        row_a = jnp.where(odd == 1, 0, TH + HALO)
        row_b = jnp.where(odd == 1, TH + HALO, 0)
        rims = [
            pltpu.make_async_copy(
                ref, field.at[pl.ds(row, HALO), 1], sems.at[parts + k]
            )
            for k, (ref, row) in enumerate(((rim_a_ref, row_a), (rim_b_ref, row_b)))
        ]
        for rim in rims:
            rim.start()
        for k in range(parts):
            rows_copy(k).start()
        for rim in rims:
            rim.wait()

        across = lax.broadcasted_iota(jnp.int32, (hid, hid), 0)
        for k, ref in enumerate((bias_first_ref, bias_second_ref)):
            square = jnp.where(across == lane_index((hid, hid)), ref[...], 0.0)
            biases[k] = jnp.broadcast_to(jnp.sum(square, axis=1, keepdims=True), (hid, LANES))

        wide = lane_index((channels, span))

        def strip_of(ref, p):
            return jnp.concatenate([ref[p, 0], ref[p, 1]], axis=1).astype(F32)

        def put(strip, lane_at, tile, start):
            moved = pltpu.roll(tile, (lane_at % LANES - start + LANES) % LANES, 1)
            return jnp.where(wide == lane_at, jnp.concatenate([moved, moved], axis=1), strip)

        own = strip_of(own_ref, 0)
        sides = [strip_of(side_ref, p) for p in range(2)]
        starts = [jnp.where(col == 0, 0, LANES - 1), jnp.where(col == 0, 1, LANES - 2)]
        for above, at_row, lane_at in (
            (1, 0, LANE_BASE - HALO),
            (0, TH + HALO, TH + LANE_BASE),
        ):
            for k in range(HALO):
                tiles = jnp.where(
                    odd == above, side_a_ref[k].astype(F32), side_b_ref[k].astype(F32)
                )
                tile = jnp.where(col == 0, tiles[:, :LANES], tiles[:, LANES:])
                sides = [put(sides[p], lane_at + k, tile, starts[p]) for p in range(2)]
                tiles = field[at_row + k, 1].astype(F32)
                tile = jnp.where(col == 0, tiles[:, LANES:], tiles[:, :LANES])
                own = put(own, lane_at + k, tile, target)

        stack = jnp.concatenate([sides[0], sides[1], own], axis=0).astype(BF16)
        result = jnp.dot(edge_first_ref[...], stack, preferred_element_type=F32)
        total = result[0:hid]
        for a in range(1, 3):
            total = total + pltpu.roll(result[hid * a : hid * (a + 1)], span - a, 1)
        beyond = silu(total + jnp.concatenate([biases[0]] * EDGE_TILES, axis=1))
        lane_hid = lane_index((hid, span))
        first_lane = LANE_BASE - HALO
        drop = ((lane_hid == first_lane) & (at_top == 1)) | (
            (lane_hid == first_lane + rows_hid - 1) & (at_bottom == 1)
        )
        beyond = jnp.where(drop, 0.0, beyond).astype(BF16)
        for tile in range(EDGE_TILES):
            edge_one[tile] = sides[0][:, tile * LANES : (tile + 1) * LANES].astype(BF16)
            edge_two[tile] = beyond[:, tile * LANES : (tile + 1) * LANES]

        rows_copy(0).wait()
        for row in range(2 * HALO):
            prepare(row)
        first_group(0)

        @pl.when(at_top == 1)
        def clear_top():
            hidden[0] = jnp.zeros(hidden.shape[1:], BF16)

    @pl.when(step < parts - 1)
    def arrive():
        rows_copy(step + 1).wait()

    @pl.when((step >= LAG) & (step < parts))
    def steady():
        second_row = jnp.maximum((step - LAG) * OUT_ROWS, 0)
        first_row = jnp.maximum((step - 1) * OUT_ROWS, 0) + GROUP
        for g in range(OUT_ROWS // GROUP):
            second_group(g, second_row + g * GROUP)
        for g in range(OUT_ROWS // GROUP):
            first_group(first_row + g * GROUP)
        for r in range(OUT_ROWS):
            prepare(step * OUT_ROWS + 2 * GROUP + r)
        for half in range(2):
            out_ref[:, :, half * LANES : (half + 1) * LANES] = jnp.swapaxes(stage[half], 0, 1).astype(
                BF16
            )


    @pl.when(step >= parts)
    def last_ones():
        for g in range(OUT_ROWS // GROUP):
            second_group(g, (step - LAG) * OUT_ROWS + g * GROUP)
        for half in range(2):
            out_ref[:, :, half * LANES : (half + 1) * LANES] = jnp.swapaxes(
                stage[half], 0, 1
            ).astype(BF16)

    @pl.when(((step >= 1) & (step < LAG)) | (step == parts))
    def first_ones():
        for g in range(OUT_ROWS // GROUP):
            first_group((step - 1) * OUT_ROWS + GROUP + g * GROUP)

    @pl.when(step < LAG)
    def shift_ones():
        for r in range(OUT_ROWS):
            prepare(step * OUT_ROWS + 2 * GROUP + r)

    @pl.when((step == parts) & (at_bottom == 1))
    def clear_bottom():
        hidden[rows_hid - 1] = jnp.zeros(hidden.shape[1:], BF16)


def banded(kernel, count):
    hid, channels = kernel.shape[1:]
    taps = jnp.transpose(kernel.reshape(3, 3, hid, channels), (2, 0, 1, 3))
    taps = taps.reshape(hid, 9 * channels)
    span = 3 * channels
    rows = [jnp.pad(taps, ((0, 0), (r * span, (count - 1 - r) * span))) for r in range(count)]
    return jnp.concatenate(rows, axis=0)


def whole_in_vmem():
    return pl.BlockSpec(memory_space=pltpu.VMEM)


def pack(route_block, route_count, sweeps, route_cell, route_templ):
    peers, capacity = route_block.shape
    channels = sweeps.shape[1]
    rows = capacity * channels + INFO_ROWS
    part = peers // PACK_STEPS
    return pl.pallas_call(
        functools.partial(pack_kernel, channels),
        grid_spec=pltpu.PrefetchScalarGridSpec(
            num_scalar_prefetch=2,
            grid=(PACK_STEPS,),
            in_specs=[pl.BlockSpec(memory_space=pl.ANY), whole_in_vmem(), whole_in_vmem()],
            out_specs=pl.BlockSpec((part, rows, LANES), lambda i, *_: (i, 0, 0)),
            scratch_shapes=[pltpu.VMEM((2, peers, LANES), F32), pltpu.SemaphoreType.DMA],
        ),
        out_shape=jax.ShapeDtypeStruct((peers, rows, LANES), BF16),
        compiler_params=pltpu.CompilerParams(
            dimension_semantics=("arbitrary",), vmem_limit_bytes=PACK_VMEM
        ),
        name="pack",
    )(route_block, route_count, sweeps, route_cell, route_templ)


def composite(received, col, table, row_weight, capacity, channels):
    peers = received.shape[0]
    rows = TH // ROW_STEPS * channels
    return pl.pallas_call(
        functools.partial(composite_kernel, capacity, channels),
        grid_spec=pltpu.PrefetchScalarGridSpec(
            num_scalar_prefetch=1,
            grid=(ROW_STEPS,),
            in_specs=[pl.BlockSpec(memory_space=pl.ANY), whole_in_vmem(), whole_in_vmem()],
            out_specs=[pl.BlockSpec((rows, TW), lambda i, *_: (i, 0))] + [whole_in_vmem()] * 3,
            scratch_shapes=[
                pltpu.VMEM((CBLK + 1, channels, LANES), F32),
                pltpu.VMEM((CBLK + 8, LANES), F32),
                pltpu.VMEM((2, EDGE_TILES, channels, LANES), BF16),
                pltpu.VMEM((peers, capacity * channels, LANES), BF16),
                pltpu.VMEM((peers, INFO_ROWS, LANES), BF16),
                pltpu.VMEM((2 * peers, LANES), jnp.int32),
                pltpu.SMEM((2 * peers, LANES), jnp.int32),
                pltpu.SemaphoreType.DMA((LOADS + 2,)),
            ],
        ),
        out_shape=[
            jax.ShapeDtypeStruct((TH * channels, TW), BF16),
            jax.ShapeDtypeStruct((2, EDGE_TILES, channels, LANES), BF16),
            jax.ShapeDtypeStruct((HALO, channels, TW), BF16),
            jax.ShapeDtypeStruct((HALO, channels, TW), BF16),
        ],
        compiler_params=pltpu.CompilerParams(
            dimension_semantics=("arbitrary",), vmem_limit_bytes=COMPOSITE_VMEM
        ),
        name="composite",
    )(col, received, table, row_weight)


def encoder(place, field, rim_a, rim_b, own, side, side_a, side_b, weights, channels, hid):
    parts = TH // OUT_ROWS
    steps = parts + LAG
    return pl.pallas_call(
        functools.partial(encoder_kernel, channels, hid),
        grid_spec=pltpu.PrefetchScalarGridSpec(
            num_scalar_prefetch=1,
            grid=(steps,),
            in_specs=[pl.BlockSpec(memory_space=pl.ANY)] * 3 + [whole_in_vmem()] * 9,
            out_specs=pl.BlockSpec(
                (hid, OUT_ROWS, TW), lambda i, *_: (0, jnp.maximum(i - LAG, 0), 0)
            ),
            scratch_shapes=[
                pltpu.VMEM((steps * OUT_ROWS + 2 * GROUP, 3, channels, TW), BF16),
                pltpu.VMEM(((steps - 1) * OUT_ROWS + GROUP, 3, hid, TW), BF16),
                pltpu.VMEM((EDGE_TILES, channels, LANES), BF16),
                pltpu.VMEM((EDGE_TILES, hid, LANES), BF16),
                pltpu.VMEM((2, hid, LANES), F32),
                pltpu.VMEM((2, OUT_ROWS, hid, LANES), F32),
                pltpu.SemaphoreType.DMA((parts + 2,)),
            ],
        ),
        out_shape=jax.ShapeDtypeStruct((hid, TH, TW), BF16),
        compiler_params=pltpu.CompilerParams(
            dimension_semantics=("arbitrary",), vmem_limit_bytes=ENCODER_VMEM
        ),
        name="encoder",
    )(place, field, rim_a, rim_b, own, side, side_a, side_b, *weights)


def layer_weights(conv_first, bias_first, conv_second, bias_second, col):
    hid = conv_first.shape[1]
    taps = conv_first.reshape(3, 3, hid, -1)
    inner = jnp.where(col == 0, taps[:, 2], taps[:, 0])
    outer = jnp.where(col == 0, taps[:, 0], taps[:, 2])
    edge_first = jnp.concatenate([taps[:, 1], inner, outer], axis=2).reshape(3 * hid, -1)
    return (
        banded(conv_first, GROUP),
        banded(conv_second, GROUP),
        edge_first,
        bias_first.reshape(1, hid),
        bias_second.reshape(1, hid),
    )


def shards(
    sweeps, route_block, route_cell, route_templ, route_count, footprint,
    conv_first, bias_first, conv_second, bias_second,
):
    peers, capacity = route_block.shape[1:]
    channels = sweeps.shape[1]
    hid = conv_first.shape[1]
    rows = lax.axis_size("ty")
    col = lax.axis_index("tx")
    row = lax.axis_index("ty")
    tiles = ("ty", "tx")

    packets = pack(route_block[0], route_count, sweeps, route_cell, route_templ)
    received = lax.all_to_all(packets, tiles, split_axis=0, concat_axis=0, tiled=True)
    table = jnp.transpose(footprint, (0, 2, 1))
    row_weight = jnp.sum(footprint.astype(F32), axis=2)
    place = jnp.stack([col, row == 0, row == rows - 1, row % 2]).astype(jnp.int32)
    weights = layer_weights(conv_first, bias_first, conv_second, bias_second, col)
    received, table, row_weight, place, weights = lax.optimization_barrier(
        (received, table, row_weight, place, weights)
    )
    field, own, rim_a, rim_b = composite(received, place, table, row_weight, capacity, channels)

    field = field.reshape(TH, channels, TW)
    swap = [(0, 1), (1, 0)]
    pairs_a = [p for i in range(0, rows - 1, 2) for p in ((i, i + 1), (i + 1, i))]
    pairs_b = [p for i in range(1, rows - 1, 2) for p in ((i, i + 1), (i + 1, i))]
    side = lax.ppermute(own, "tx", swap)
    rim_a = lax.ppermute(rim_a, "ty", pairs_a)
    rim_b = lax.ppermute(rim_b, "ty", pairs_b)
    side_a = lax.ppermute(rim_a, "tx", swap)
    side_b = lax.ppermute(rim_b, "tx", swap)
    return encoder(place, field, rim_a, rim_b, own, side, side_a, side_b, weights, channels, hid)


def solution(mesh):
    split = ("group", "ty", "tx")
    in_specs = (
        P(split, None, None),
        P(split, None, None),
        P(split, None, None),
        P(split, None, None),
        P(split, None),
        P(),
        P(),
        P(),
        P(),
        P(),
    )
    out_specs = P(None, ("group", "ty"), "tx")
    return jax.shard_map(shards, mesh=mesh, in_specs=in_specs, out_specs=out_specs, check_vma=False)
```

```python
import functools

import jax
import jax.numpy as jnp
from jax import lax
from jax.experimental import pallas as pl
from jax.experimental.pallas import tpu as pltpu
from jax.sharding import PartitionSpec as P

TH = 192
TW = 256
CBLK = 384
LANES = 128
HALO = 2
EDGE_TILES = 2
LANE_BASE = 8
ROW_STEPS = 4
CHUNK = 8
LOADS = 4
GROUP = 2
OUT_ROWS = 16
LAG = 2
PACK_STEPS = 1
INFO_ROWS = 16
CELL_BASE = 32
MIB = 1024 * 1024
PACK_VMEM = 56 * MIB
COMPOSITE_VMEM = 26 * MIB
ENCODER_VMEM = 45 * MIB

F32 = jnp.float32
BF16 = jnp.bfloat16


def lane_index(shape):
    return lax.broadcasted_iota(jnp.int32, shape, len(shape) - 1)


def silu(value):
    half = 0.5 * value
    return half + half * jnp.tanh(half)


def pack_kernel(
    channels, block_ref, count_ref, sweeps_ref, cell_ref, templ_ref, out_ref, padded, sem
):
    part = out_ref.shape[0]
    capacity = block_ref.shape[1]
    held = capacity * channels
    first = pl.program_id(0) * part

    def send_tile(d, carry):
        for q in range(capacity):
            pltpu.make_async_copy(
                sweeps_ref.at[block_ref[first + d, q]],
                out_ref.at[d, pl.ds(q * channels, channels), :],
                sem,
            ).start()
        return carry

    lax.fori_loop(0, part, send_tile, 0)
    padded[...] = jnp.zeros(padded.shape, F32)
    padded[0, :, 0:capacity] = cell_ref[0].astype(F32)
    padded[1, :, 0:capacity] = templ_ref[0].astype(F32)
    lane = lane_index((1, LANES))
    which = lax.broadcasted_iota(jnp.int32, (INFO_ROWS, LANES), 0)
    for d in range(part):
        live = lane < count_ref[0, first + d]
        cell = jnp.where(live, padded[0, pl.ds(first + d, 1), :], float(CBLK))
        high = jnp.floor(cell * (1.0 / CELL_BASE))
        low = cell - high * CELL_BASE
        template = padded[1, pl.ds(first + d, 1), :]
        rows = jnp.where(which == 0, high, jnp.where(which == 1, low, template))
        out_ref[d, held : held + INFO_ROWS, :] = rows.astype(BF16)
    arrived = out_ref.at[:, pl.ds(0, held), :]
    pltpu.make_async_copy(arrived, arrived, sem).wait()


def composite_kernel(
    capacity, channels, col_ref, recv_ref, table_ref, weight_ref,
    comp_ref, edge_ref, rim_a, rim_b, acc, den, strip, recv, raw, numbers, slots, sems,
):
    step = pl.program_id(0)
    peers = recv_ref.shape[0]
    part = peers // LOADS
    col = col_ref[0]
    odd = col_ref[3]

    @pl.when(step == 0)
    def add_up():
        held = capacity * channels
        listing = pltpu.make_async_copy(
            recv_ref.at[:, pl.ds(held, INFO_ROWS), :], raw, sems.at[LOADS]
        )
        listing.start()
        copies = [
            pltpu.make_async_copy(
                recv_ref.at[pl.ds(k * part, part), pl.ds(0, held), :],
                recv.at[pl.ds(k * part, part)],
                sems.at[k],
            )
            for k in range(LOADS)
        ]
        for copy in copies:
            copy.start()
        listing.wait()
        for source in range(peers):
            rows = raw[source].astype(F32)
            numbers[source : source + 1, :] = (
                rows[0:1] * CELL_BASE + rows[1:2]
            ).astype(jnp.int32)
            numbers[peers + source : peers + source + 1, :] = rows[2:3].astype(jnp.int32)
        moved = pltpu.make_async_copy(numbers, slots, sems.at[LOADS + 1])
        moved.start()

        def clear_block(i, carry):
            acc[i] = jnp.zeros(acc.shape[1:], F32)
            return carry

        lax.fori_loop(0, CBLK, clear_block, 0, unroll=8)
        den[...] = jnp.zeros(den.shape, F32)
        strip[...] = jnp.zeros(strip.shape, BF16)

        moved.wait()

        def add_slots(source, carry):
            terms = []
            for q in range(capacity):
                block = recv[source, q * channels : (q + 1) * channels, :]
                template = slots[peers + source, q]
                terms.append(jnp.dot(block, table_ref[template], preferred_element_type=F32))
            for q in range(capacity):
                cell = slots[source, q]
                acc[cell] += terms[q]
                template = slots[peers + source, q]
                den[pl.ds(cell, 1), :] += weight_ref[pl.ds(template, 1), :]
            return carry

        for k in range(LOADS):
            copies[k].wait()
            lax.fori_loop(k * part, (k + 1) * part, add_slots, 0)
        den[...] = 1.0 / (1.0 + den[...])

    rows = TH // ROW_STEPS
    lane = lane_index((channels, LANES))
    near = jnp.where(col == 0, LANES - 1, 0)
    far = jnp.where(col == 0, LANES - 2, 1)

    def some_rows(i, carry):
        base = step * rows + i * CHUNK
        picked = [jnp.zeros((channels, LANES), F32), jnp.zeros((channels, LANES), F32)]
        for u in range(CHUNK):
            r = base + u
            out = pl.multiple_of((i * CHUNK + u) * channels, 16)
            parts = []
            for m in range(2):
                value = acc[2 * r + m] * den[pl.ds(2 * r + m, 1), :]
                comp_ref[pl.ds(out, channels), m * LANES : (m + 1) * LANES] = value.astype(BF16)
                parts.append(value)
            side = jnp.where(col == 0, parts[1], parts[0])
            at = (r + LANE_BASE) % LANES
            for p, start in enumerate((near, far)):
                moved = pltpu.roll(side, (at - start + LANES) % LANES, 1)
                picked[p] = jnp.where(lane == at, moved, picked[p])
        tile = (base + LANE_BASE) // LANES
        first = (base + LANE_BASE) % LANES
        inside = (lane >= first) & (lane < first + CHUNK)
        for p in range(2):
            strip[p, tile] = jnp.where(
                inside, picked[p], strip[p, tile].astype(F32)
            ).astype(BF16)
        return carry

    lax.fori_loop(0, rows // CHUNK, some_rows, 0)

    rim = HALO * channels
    top = step == 0
    bottom = step == ROW_STEPS - 1

    @pl.when((top & (odd == 1)) | (bottom & (odd == 0)))
    def rim_to_a():
        begin = pl.multiple_of(jnp.where(top, 0, rows * channels - rim), 16)
        rim_a[...] = comp_ref[pl.ds(begin, rim), :].reshape(HALO, channels, TW)

    @pl.when((top & (odd == 0)) | (bottom & (odd == 1)))
    def rim_to_b():
        begin = pl.multiple_of(jnp.where(top, 0, rows * channels - rim), 16)
        rim_b[...] = comp_ref[pl.ds(begin, rim), :].reshape(HALO, channels, TW)

    @pl.when(bottom)
    def finish():
        edge_ref[...] = strip[...]


def shifted(value, left, right):
    lane = lane_index((value.shape[0], LANES))
    first, last = value[:, :LANES], value[:, LANES:]
    first_left, last_left = pltpu.roll(first, 1, 1), pltpu.roll(last, 1, 1)
    first_right, last_right = pltpu.roll(first, LANES - 1, 1), pltpu.roll(last, LANES - 1, 1)
    before = (
        jnp.where(lane == 0, left, first_left),
        jnp.where(lane == 0, first_left, last_left),
    )
    after = (
        jnp.where(lane == LANES - 1, last_right, first_right),
        jnp.where(lane == LANES - 1, right, last_right),
    )
    return before, after


def encoder_kernel(
    channels, hid, place_ref, comp_ref, rim_a_ref, rim_b_ref, own_ref, side_ref, side_a_ref, side_b_ref,
    first_ref, second_ref, edge_first_ref, bias_first_ref, bias_second_ref,
    out_ref, field, hidden, edge_one, edge_two, biases, stage, sems,
):
    col = place_ref[0]
    at_top = place_ref[1]
    at_bottom = place_ref[2]
    odd = place_ref[3]
    target = jnp.where(col == 0, LANES - 1, 0)
    rows_hid = TH + 2
    span = EDGE_TILES * LANES
    step = pl.program_id(0)
    parts = TH // OUT_ROWS

    def halo_columns(strip, lane_at):
        moved = pltpu.roll(
            strip[lane_at // LANES], (target - lane_at % LANES + LANES) % LANES, 1
        )
        nothing = jnp.zeros_like(moved)
        return jnp.where(col == 0, nothing, moved), jnp.where(col == 0, moved, nothing)

    def put_row(ref, strip, row, value):
        left, right = halo_columns(strip, row + LANE_BASE - HALO)
        before, after = shifted(value, left, right)
        for half in range(2):
            place = slice(half * LANES, (half + 1) * LANES)
            ref[row, 0, :, place] = before[half]
            ref[row, 2, :, place] = after[half]

    def prepare(row):
        put_row(field, edge_one, row, field[row, 1])

    def first_group(first_row):
        window = field[pl.ds(first_row, GROUP + 2)].reshape((GROUP + 2) * 3 * channels, TW)
        full = jnp.dot(first_ref[...], window, preferred_element_type=F32)
        bias = jnp.concatenate([biases[0]] * 2, axis=1)
        for r in range(GROUP):
            value = silu(full[r * hid : (r + 1) * hid] + bias).astype(BF16)
            hidden[first_row + r, 1] = value
            put_row(hidden, edge_two, first_row + r, value)

    def second_group(g, first_row):
        window = hidden[pl.ds(first_row, GROUP + 2)].reshape((GROUP + 2) * 3 * hid, TW)
        full = jnp.dot(second_ref[...], window, preferred_element_type=F32)
        bias = jnp.concatenate([biases[1]] * GROUP, axis=0)
        for half in range(2):
            value = full[:, half * LANES : (half + 1) * LANES] + bias
            for r in range(GROUP):
                stage[half, g * GROUP + r] = value[r * hid : (r + 1) * hid]

    def rows_copy(k):
        return pltpu.make_async_copy(
            comp_ref.at[pl.ds(k * OUT_ROWS, OUT_ROWS)],
            field.at[pl.ds(HALO + k * OUT_ROWS, OUT_ROWS), 1],
            sems.at[k],
        )

    @pl.when(step == 0)
    def start():
        row_a = jnp.where(odd == 1, 0, TH + HALO)
        row_b = jnp.where(odd == 1, TH + HALO, 0)
        rims = [
            pltpu.make_async_copy(
                ref, field.at[pl.ds(row, HALO), 1], sems.at[parts + k]
            )
            for k, (ref, row) in enumerate(((rim_a_ref, row_a), (rim_b_ref, row_b)))
        ]
        for rim in rims:
            rim.start()
        for k in range(parts):
            rows_copy(k).start()
        for rim in rims:
            rim.wait()

        across = lax.broadcasted_iota(jnp.int32, (hid, hid), 0)
        for k, ref in enumerate((bias_first_ref, bias_second_ref)):
            square = jnp.where(across == lane_index((hid, hid)), ref[...], 0.0)
            biases[k] = jnp.broadcast_to(jnp.sum(square, axis=1, keepdims=True), (hid, LANES))

        wide = lane_index((channels, span))

        def strip_of(ref, p):
            return jnp.concatenate([ref[p, 0], ref[p, 1]], axis=1).astype(F32)

        def put(strip, lane_at, tile, start):
            moved = pltpu.roll(tile, (lane_at % LANES - start + LANES) % LANES, 1)
            return jnp.where(wide == lane_at, jnp.concatenate([moved, moved], axis=1), strip)

        own = strip_of(own_ref, 0)
        sides = [strip_of(side_ref, p) for p in range(2)]
        starts = [jnp.where(col == 0, 0, LANES - 1), jnp.where(col == 0, 1, LANES - 2)]
        for above, at_row, lane_at in (
            (1, 0, LANE_BASE - HALO),
            (0, TH + HALO, TH + LANE_BASE),
        ):
            for k in range(HALO):
                tiles = jnp.where(
                    odd == above, side_a_ref[k].astype(F32), side_b_ref[k].astype(F32)
                )
                tile = jnp.where(col == 0, tiles[:, :LANES], tiles[:, LANES:])
                sides = [put(sides[p], lane_at + k, tile, starts[p]) for p in range(2)]
                tiles = field[at_row + k, 1].astype(F32)
                tile = jnp.where(col == 0, tiles[:, LANES:], tiles[:, :LANES])
                own = put(own, lane_at + k, tile, target)

        stack = jnp.concatenate([sides[0], sides[1], own], axis=0).astype(BF16)
        result = jnp.dot(edge_first_ref[...], stack, preferred_element_type=F32)
        total = result[0:hid]
        for a in range(1, 3):
            total = total + pltpu.roll(result[hid * a : hid * (a + 1)], span - a, 1)
        beyond = silu(total + jnp.concatenate([biases[0]] * EDGE_TILES, axis=1))
        lane_hid = lane_index((hid, span))
        first_lane = LANE_BASE - HALO
        drop = ((lane_hid == first_lane) & (at_top == 1)) | (
            (lane_hid == first_lane + rows_hid - 1) & (at_bottom == 1)
        )
        beyond = jnp.where(drop, 0.0, beyond).astype(BF16)
        for tile in range(EDGE_TILES):
            edge_one[tile] = sides[0][:, tile * LANES : (tile + 1) * LANES].astype(BF16)
            edge_two[tile] = beyond[:, tile * LANES : (tile + 1) * LANES]

        rows_copy(0).wait()
        for row in range(2 * HALO):
            prepare(row)
        first_group(0)

        @pl.when(at_top == 1)
        def clear_top():
            hidden[0] = jnp.zeros(hidden.shape[1:], BF16)

    @pl.when(step < parts - 1)
    def arrive():
        rows_copy(step + 1).wait()

    @pl.when((step >= LAG) & (step < parts))
    def steady():
        second_row = jnp.maximum((step - LAG) * OUT_ROWS, 0)
        first_row = jnp.maximum((step - 1) * OUT_ROWS, 0) + GROUP
        for g in range(OUT_ROWS // GROUP):
            second_group(g, second_row + g * GROUP)
        for g in range(OUT_ROWS // GROUP):
            first_group(first_row + g * GROUP)
        for r in range(OUT_ROWS):
            prepare(step * OUT_ROWS + 2 * GROUP + r)
        for half in range(2):
            out_ref[:, :, half * LANES : (half + 1) * LANES] = jnp.swapaxes(stage[half], 0, 1).astype(
                BF16
            )


    @pl.when(step >= parts)
    def last_ones():
        for g in range(OUT_ROWS // GROUP):
            second_group(g, (step - LAG) * OUT_ROWS + g * GROUP)
        for half in range(2):
            out_ref[:, :, half * LANES : (half + 1) * LANES] = jnp.swapaxes(
                stage[half], 0, 1
            ).astype(BF16)

    @pl.when(((step >= 1) & (step < LAG)) | (step == parts))
    def first_ones():
        for g in range(OUT_ROWS // GROUP):
            first_group((step - 1) * OUT_ROWS + GROUP + g * GROUP)

    @pl.when(step < LAG)
    def shift_ones():
        for r in range(OUT_ROWS):
            prepare(step * OUT_ROWS + 2 * GROUP + r)

    @pl.when((step == parts) & (at_bottom == 1))
    def clear_bottom():
        hidden[rows_hid - 1] = jnp.zeros(hidden.shape[1:], BF16)


def banded(kernel, count):
    hid, channels = kernel.shape[1:]
    taps = jnp.transpose(kernel.reshape(3, 3, hid, channels), (2, 0, 1, 3))
    taps = taps.reshape(hid, 9 * channels)
    span = 3 * channels
    rows = [jnp.pad(taps, ((0, 0), (r * span, (count - 1 - r) * span))) for r in range(count)]
    return jnp.concatenate(rows, axis=0)


def whole_in_vmem():
    return pl.BlockSpec(memory_space=pltpu.VMEM)


def pack(route_block, route_count, sweeps, route_cell, route_templ):
    peers, capacity = route_block.shape
    channels = sweeps.shape[1]
    rows = capacity * channels + INFO_ROWS
    part = peers // PACK_STEPS
    return pl.pallas_call(
        functools.partial(pack_kernel, channels),
        grid_spec=pltpu.PrefetchScalarGridSpec(
            num_scalar_prefetch=2,
            grid=(PACK_STEPS,),
            in_specs=[pl.BlockSpec(memory_space=pl.ANY), whole_in_vmem(), whole_in_vmem()],
            out_specs=pl.BlockSpec((part, rows, LANES), lambda i, *_: (i, 0, 0)),
            scratch_shapes=[pltpu.VMEM((2, peers, LANES), F32), pltpu.SemaphoreType.DMA],
        ),
        out_shape=jax.ShapeDtypeStruct((peers, rows, LANES), BF16),
        compiler_params=pltpu.CompilerParams(
            dimension_semantics=("arbitrary",), vmem_limit_bytes=PACK_VMEM
        ),
        name="pack",
    )(route_block, route_count, sweeps, route_cell, route_templ)


def composite(received, col, table, row_weight, capacity, channels):
    peers = received.shape[0]
    rows = TH // ROW_STEPS * channels
    return pl.pallas_call(
        functools.partial(composite_kernel, capacity, channels),
        grid_spec=pltpu.PrefetchScalarGridSpec(
            num_scalar_prefetch=1,
            grid=(ROW_STEPS,),
            in_specs=[pl.BlockSpec(memory_space=pl.ANY), whole_in_vmem(), whole_in_vmem()],
            out_specs=[pl.BlockSpec((rows, TW), lambda i, *_: (i, 0))] + [whole_in_vmem()] * 3,
            scratch_shapes=[
                pltpu.VMEM((CBLK + 1, channels, LANES), F32),
                pltpu.VMEM((CBLK + 8, LANES), F32),
                pltpu.VMEM((2, EDGE_TILES, channels, LANES), BF16),
                pltpu.VMEM((peers, capacity * channels, LANES), BF16),
                pltpu.VMEM((peers, INFO_ROWS, LANES), BF16),
                pltpu.VMEM((2 * peers, LANES), jnp.int32),
                pltpu.SMEM((2 * peers, LANES), jnp.int32),
                pltpu.SemaphoreType.DMA((LOADS + 2,)),
            ],
        ),
        out_shape=[
            jax.ShapeDtypeStruct((TH * channels, TW), BF16),
            jax.ShapeDtypeStruct((2, EDGE_TILES, channels, LANES), BF16),
            jax.ShapeDtypeStruct((HALO, channels, TW), BF16),
            jax.ShapeDtypeStruct((HALO, channels, TW), BF16),
        ],
        compiler_params=pltpu.CompilerParams(
            dimension_semantics=("arbitrary",), vmem_limit_bytes=COMPOSITE_VMEM
        ),
        name="composite",
    )(col, received, table, row_weight)


def encoder(place, field, rim_a, rim_b, own, side, side_a, side_b, weights, channels, hid):
    parts = TH // OUT_ROWS
    steps = parts + LAG
    return pl.pallas_call(
        functools.partial(encoder_kernel, channels, hid),
        grid_spec=pltpu.PrefetchScalarGridSpec(
            num_scalar_prefetch=1,
            grid=(steps,),
            in_specs=[pl.BlockSpec(memory_space=pl.ANY)] * 3 + [whole_in_vmem()] * 9,
            out_specs=pl.BlockSpec(
                (hid, OUT_ROWS, TW), lambda i, *_: (0, jnp.maximum(i - LAG, 0), 0)
            ),
            scratch_shapes=[
                pltpu.VMEM((steps * OUT_ROWS + 2 * GROUP, 3, channels, TW), BF16),
                pltpu.VMEM(((steps - 1) * OUT_ROWS + GROUP, 3, hid, TW), BF16),
                pltpu.VMEM((EDGE_TILES, channels, LANES), BF16),
                pltpu.VMEM((EDGE_TILES, hid, LANES), BF16),
                pltpu.VMEM((2, hid, LANES), F32),
                pltpu.VMEM((2, OUT_ROWS, hid, LANES), F32),
                pltpu.SemaphoreType.DMA((parts + 2,)),
            ],
        ),
        out_shape=jax.ShapeDtypeStruct((hid, TH, TW), BF16),
        compiler_params=pltpu.CompilerParams(
            dimension_semantics=("arbitrary",), vmem_limit_bytes=ENCODER_VMEM
        ),
        name="encoder",
    )(place, field, rim_a, rim_b, own, side, side_a, side_b, *weights)


def layer_weights(conv_first, bias_first, conv_second, bias_second, col):
    hid = conv_first.shape[1]
    taps = conv_first.reshape(3, 3, hid, -1)
    inner = jnp.where(col == 0, taps[:, 2], taps[:, 0])
    outer = jnp.where(col == 0, taps[:, 0], taps[:, 2])
    edge_first = jnp.concatenate([taps[:, 1], inner, outer], axis=2).reshape(3 * hid, -1)
    return (
        banded(conv_first, GROUP),
        banded(conv_second, GROUP),
        edge_first,
        bias_first.reshape(1, hid),
        bias_second.reshape(1, hid),
    )


def shards(
    sweeps, route_block, route_cell, route_templ, route_count, footprint,
    conv_first, bias_first, conv_second, bias_second,
):
    peers, capacity = route_block.shape[1:]
    channels = sweeps.shape[1]
    hid = conv_first.shape[1]
    rows = lax.axis_size("ty")
    col = lax.axis_index("tx")
    row = lax.axis_index("ty")
    tiles = ("ty", "tx")

    packets = pack(route_block[0], route_count, sweeps, route_cell, route_templ)
    received = lax.all_to_all(packets, tiles, split_axis=0, concat_axis=0, tiled=True)
    table = jnp.transpose(footprint, (0, 2, 1))
    row_weight = jnp.sum(footprint.astype(F32), axis=2)
    place = jnp.stack([col, row == 0, row == rows - 1, row % 2]).astype(jnp.int32)
    weights = layer_weights(conv_first, bias_first, conv_second, bias_second, col)
    received, table, row_weight, place, weights = lax.optimization_barrier(
        (received, table, row_weight, place, weights)
    )
    field, own, rim_a, rim_b = composite(received, place, table, row_weight, capacity, channels)

    field = field.reshape(TH, channels, TW)
    swap = [(0, 1), (1, 0)]
    pairs_a = [p for i in range(0, rows - 1, 2) for p in ((i, i + 1), (i + 1, i))]
    pairs_b = [p for i in range(1, rows - 1, 2) for p in ((i, i + 1), (i + 1, i))]
    side = lax.ppermute(own, "tx", swap)
    rim_a = lax.ppermute(rim_a, "ty", pairs_a)
    rim_b = lax.ppermute(rim_b, "ty", pairs_b)
    side_a = lax.ppermute(rim_a, "tx", swap)
    side_b = lax.ppermute(rim_b, "tx", swap)
    return encoder(place, field, rim_a, rim_b, own, side, side_a, side_b, weights, channels, hid)


def solution(mesh):
    split = ("group", "ty", "tx")
    in_specs = (
        P(split, None, None),
        P(split, None, None),
        P(split, None, None),
        P(split, None, None),
        P(split, None),
        P(),
        P(),
        P(),
        P(),
        P(),
    )
    out_specs = P(None, ("group", "ty"), "tx")
    return jax.shard_map(shards, mesh=mesh, in_specs=in_specs, out_specs=out_specs, check_vma=False)
```

```python
import functools

import jax
import jax.numpy as jnp
from jax import lax
from jax.experimental import pallas as pl
from jax.experimental.pallas import tpu as pltpu
from jax.sharding import PartitionSpec as P

TH = 192
TW = 256
CBLK = 384
LANES = 128
HALO = 2
EDGE_TILES = 2
LANE_BASE = 8
ROW_STEPS = 3
CHUNK = 8
LOADS = 4
GROUP = 2
OUT_ROWS = 32
LAG = 2
PACK_PARTS = 8
INFO_ROWS = 16
CELL_BASE = 32
MIB = 1024 * 1024
PACK_VMEM = 56 * MIB
COMPOSITE_VMEM = 26 * MIB
ENCODER_VMEM = 48 * MIB

F32 = jnp.float32
BF16 = jnp.bfloat16


def lane_index(shape):
    return lax.broadcasted_iota(jnp.int32, shape, len(shape) - 1)


def silu(value):
    half = 0.5 * value
    return half + half * jnp.tanh(half)


def pack_kernel(
    channels, block_ref, count_ref, sweeps_ref, cell_ref, templ_ref, out_ref, packets, padded, sems
):
    peers, capacity = block_ref.shape
    held = capacity * channels
    part = peers // PACK_PARTS

    def send_tile(d, carry):
        for q in range(capacity):
            pltpu.make_async_copy(
                sweeps_ref.at[block_ref[d, q]],
                packets.at[d, pl.ds(q * channels, channels), :],
                sems.at[d // part],
            ).start()
        return carry

    lax.fori_loop(0, peers, send_tile, 0)
    padded[...] = jnp.zeros(padded.shape, F32)
    padded[0, :, 0:capacity] = cell_ref[0].astype(F32)
    padded[1, :, 0:capacity] = templ_ref[0].astype(F32)
    lane = lane_index((1, LANES))
    which = lax.broadcasted_iota(jnp.int32, (INFO_ROWS, LANES), 0)
    for d in range(peers):
        live = lane < count_ref[0, d]
        cell = jnp.where(live, padded[0, d : d + 1, :], float(CBLK))
        high = jnp.floor(cell * (1.0 / CELL_BASE))
        low = cell - high * CELL_BASE
        template = padded[1, d : d + 1, :]
        rows = jnp.where(which == 0, high, jnp.where(which == 1, low, template))
        packets[d, held : held + INFO_ROWS, :] = rows.astype(BF16)
    leaving = []
    for k in range(PACK_PARTS):
        mine = pl.ds(k * part, part)
        arrived = packets.at[mine, pl.ds(0, held), :]
        pltpu.make_async_copy(arrived, arrived, sems.at[k]).wait()
        leaving.append(
            pltpu.make_async_copy(packets.at[mine], out_ref.at[mine], sems.at[PACK_PARTS + k])
        )
        leaving[-1].start()
    for copy in leaving:
        copy.wait()


def composite_kernel(
    capacity, channels, col_ref, recv_ref, table_ref, weight_ref,
    comp_ref, edge_ref, rim_a, rim_b, acc, den, strip, recv, table, raw, numbers, slots, sems,
):
    step = pl.program_id(0)
    peers = recv_ref.shape[0]
    part = peers // LOADS
    col = col_ref[0]
    odd = col_ref[3]

    @pl.when(step == 0)
    def add_up():
        held = capacity * channels
        listing = pltpu.make_async_copy(
            recv_ref.at[:, pl.ds(held, INFO_ROWS), :], raw, sems.at[LOADS]
        )
        listing.start()
        copies = [
            pltpu.make_async_copy(
                recv_ref.at[pl.ds(k * part, part), pl.ds(0, held), :],
                recv.at[pl.ds(k * part, part)],
                sems.at[k],
            )
            for k in range(LOADS)
        ]
        tables = pltpu.make_async_copy(table_ref, table, sems.at[LOADS + 2])
        tables.start()
        for copy in copies:
            copy.start()
        listing.wait()
        for source in range(peers):
            rows = raw[source].astype(F32)
            numbers[source : source + 1, :] = (
                rows[0:1] * CELL_BASE + rows[1:2]
            ).astype(jnp.int32)
            numbers[peers + source : peers + source + 1, :] = rows[2:3].astype(jnp.int32)
        moved = pltpu.make_async_copy(numbers, slots, sems.at[LOADS + 1])
        moved.start()

        def clear_block(i, carry):
            acc[i] = jnp.zeros(acc.shape[1:], F32)
            return carry

        lax.fori_loop(0, CBLK, clear_block, 0, unroll=8)
        den[...] = jnp.zeros(den.shape, F32)
        strip[...] = jnp.zeros(strip.shape, BF16)

        moved.wait()
        tables.wait()

        def add_slots(source, carry):
            terms = []
            for q in range(capacity):
                block = recv[source, q * channels : (q + 1) * channels, :]
                template = slots[peers + source, q]
                terms.append(jnp.dot(block, table[template], preferred_element_type=F32))
            for q in range(capacity):
                cell = slots[source, q]
                acc[cell] += terms[q]
                template = slots[peers + source, q]
                den[pl.ds(cell, 1), :] += weight_ref[pl.ds(template, 1), :]
            return carry

        for k in range(LOADS):
            copies[k].wait()
            lax.fori_loop(k * part, (k + 1) * part, add_slots, 0, unroll=4)
        den[...] = 1.0 / (1.0 + den[...])

    rows = TH // ROW_STEPS
    lane = lane_index((channels, LANES))
    near = jnp.where(col == 0, LANES - 1, 0)
    far = jnp.where(col == 0, LANES - 2, 1)

    def some_rows(i, carry):
        base = step * rows + i * CHUNK
        picked = [jnp.zeros((channels, LANES), BF16), jnp.zeros((channels, LANES), BF16)]
        for u in range(CHUNK):
            r = base + u
            out = pl.multiple_of((i * CHUNK + u) * channels, 16)
            parts = []
            for m in range(2):
                value = (acc[2 * r + m] * den[pl.ds(2 * r + m, 1), :]).astype(BF16)
                comp_ref[pl.ds(out, channels), m * LANES : (m + 1) * LANES] = value
                parts.append(value)
            side = jnp.where(col == 0, parts[1], parts[0])
            at = (r + LANE_BASE) % LANES
            for p, start in enumerate((near, far)):
                moved = pltpu.roll(side, (at - start + LANES) % LANES, 1)
                picked[p] = jnp.where(lane == at, moved, picked[p])
        tile = (base + LANE_BASE) // LANES
        first = (base + LANE_BASE) % LANES
        inside = (lane >= first) & (lane < first + CHUNK)
        for p in range(2):
            strip[p, tile] = jnp.where(inside, picked[p], strip[p, tile])
        return carry

    lax.fori_loop(0, rows // CHUNK, some_rows, 0, unroll=2)

    rim = HALO * channels
    top = step == 0
    bottom = step == ROW_STEPS - 1

    @pl.when((top & (odd == 1)) | (bottom & (odd == 0)))
    def rim_to_a():
        begin = pl.multiple_of(jnp.where(top, 0, rows * channels - rim), 16)
        rim_a[...] = comp_ref[pl.ds(begin, rim), :].reshape(HALO, channels, TW)

    @pl.when((top & (odd == 0)) | (bottom & (odd == 1)))
    def rim_to_b():
        begin = pl.multiple_of(jnp.where(top, 0, rows * channels - rim), 16)
        rim_b[...] = comp_ref[pl.ds(begin, rim), :].reshape(HALO, channels, TW)

    @pl.when(bottom)
    def finish():
        edge_ref[...] = strip[...]


def shifted(value, left, right):
    lane = lane_index((value.shape[0], LANES))
    first, last = value[:, :LANES], value[:, LANES:]
    first_left, last_left = pltpu.roll(first, 1, 1), pltpu.roll(last, 1, 1)
    first_right, last_right = pltpu.roll(first, LANES - 1, 1), pltpu.roll(last, LANES - 1, 1)
    before = (
        jnp.where(lane == 0, left, first_left),
        jnp.where(lane == 0, first_left, last_left),
    )
    after = (
        jnp.where(lane == LANES - 1, last_right, first_right),
        jnp.where(lane == LANES - 1, right, last_right),
    )
    return before, after


def encoder_kernel(
    channels, hid, place_ref, comp_ref, rim_a_ref, rim_b_ref, own_ref, side_ref, side_a_ref, side_b_ref,
    first_ref, second_ref, edge_first_ref, bias_first_ref, bias_second_ref,
    out_ref, field, hidden, edge_one, edge_two, biases, stage, sems,
):
    col = place_ref[0]
    at_top = place_ref[1]
    at_bottom = place_ref[2]
    odd = place_ref[3]
    target = jnp.where(col == 0, LANES - 1, 0)
    rows_hid = TH + 2
    span = EDGE_TILES * LANES
    step = pl.program_id(0)
    parts = TH // OUT_ROWS

    def halo_columns(strip, lane_at):
        moved = pltpu.roll(
            strip[lane_at // LANES], (target - lane_at % LANES + LANES) % LANES, 1
        )
        nothing = jnp.zeros_like(moved)
        return jnp.where(col == 0, nothing, moved), jnp.where(col == 0, moved, nothing)

    def put_row(ref, strip, row, value):
        left, right = halo_columns(strip, row + LANE_BASE - HALO)
        before, after = shifted(value, left, right)
        for half in range(2):
            place = slice(half * LANES, (half + 1) * LANES)
            ref[row, 0, :, place] = before[half]
            ref[row, 2, :, place] = after[half]

    def prepare(row):
        put_row(field, edge_one, row, field[row, 1])

    def first_group(first_row):
        window = field[pl.ds(first_row, GROUP + 2)].reshape((GROUP + 2) * 3 * channels, TW)
        full = jnp.dot(first_ref[...], window, preferred_element_type=F32)
        bias = jnp.concatenate([biases[0]] * 2, axis=1)
        for r in range(GROUP):
            value = silu(full[r * hid : (r + 1) * hid] + bias).astype(BF16)
            hidden[first_row + r, 1] = value
            put_row(hidden, edge_two, first_row + r, value)

    def second_group(g, first_row):
        window = hidden[pl.ds(first_row, GROUP + 2)].reshape((GROUP + 2) * 3 * hid, TW)
        full = jnp.dot(second_ref[...], window, preferred_element_type=F32)
        bias = jnp.concatenate([biases[1]] * GROUP, axis=0)
        for half in range(2):
            value = full[:, half * LANES : (half + 1) * LANES] + bias
            for r in range(GROUP):
                stage[half, g * GROUP + r] = value[r * hid : (r + 1) * hid]

    def rows_copy(k):
        return pltpu.make_async_copy(
            comp_ref.at[pl.ds(k * OUT_ROWS, OUT_ROWS)],
            field.at[pl.ds(HALO + k * OUT_ROWS, OUT_ROWS), 1],
            sems.at[k],
        )

    @pl.when(step == 0)
    def start():
        row_a = jnp.where(odd == 1, 0, TH + HALO)
        row_b = jnp.where(odd == 1, TH + HALO, 0)
        rims = [
            pltpu.make_async_copy(
                ref, field.at[pl.ds(row, HALO), 1], sems.at[parts + k]
            )
            for k, (ref, row) in enumerate(((rim_a_ref, row_a), (rim_b_ref, row_b)))
        ]
        for rim in rims:
            rim.start()
        for k in range(parts):
            rows_copy(k).start()
        for rim in rims:
            rim.wait()

        across = lax.broadcasted_iota(jnp.int32, (hid, hid), 0)
        for k, ref in enumerate((bias_first_ref, bias_second_ref)):
            square = jnp.where(across == lane_index((hid, hid)), ref[...], 0.0)
            biases[k] = jnp.broadcast_to(jnp.sum(square, axis=1, keepdims=True), (hid, LANES))

        wide = lane_index((channels, span))

        def strip_of(ref, p):
            return jnp.concatenate([ref[p, 0], ref[p, 1]], axis=1).astype(F32)

        def put(strip, lane_at, tile, start):
            moved = pltpu.roll(tile, (lane_at % LANES - start + LANES) % LANES, 1)
            return jnp.where(wide == lane_at, jnp.concatenate([moved, moved], axis=1), strip)

        own = strip_of(own_ref, 0)
        sides = [strip_of(side_ref, p) for p in range(2)]
        starts = [jnp.where(col == 0, 0, LANES - 1), jnp.where(col == 0, 1, LANES - 2)]
        for above, at_row, lane_at in (
            (1, 0, LANE_BASE - HALO),
            (0, TH + HALO, TH + LANE_BASE),
        ):
            for k in range(HALO):
                tiles = jnp.where(
                    odd == above, side_a_ref[k].astype(F32), side_b_ref[k].astype(F32)
                )
                tile = jnp.where(col == 0, tiles[:, :LANES], tiles[:, LANES:])
                sides = [put(sides[p], lane_at + k, tile, starts[p]) for p in range(2)]
                tiles = field[at_row + k, 1].astype(F32)
                tile = jnp.where(col == 0, tiles[:, LANES:], tiles[:, :LANES])
                own = put(own, lane_at + k, tile, target)

        stack = jnp.concatenate([sides[0], sides[1], own], axis=0).astype(BF16)
        result = jnp.dot(edge_first_ref[...], stack, preferred_element_type=F32)
        total = result[0:hid]
        for a in range(1, 3):
            total = total + pltpu.roll(result[hid * a : hid * (a + 1)], span - a, 1)
        beyond = silu(total + jnp.concatenate([biases[0]] * EDGE_TILES, axis=1))
        lane_hid = lane_index((hid, span))
        first_lane = LANE_BASE - HALO
        drop = ((lane_hid == first_lane) & (at_top == 1)) | (
            (lane_hid == first_lane + rows_hid - 1) & (at_bottom == 1)
        )
        beyond = jnp.where(drop, 0.0, beyond).astype(BF16)
        for tile in range(EDGE_TILES):
            edge_one[tile] = sides[0][:, tile * LANES : (tile + 1) * LANES].astype(BF16)
            edge_two[tile] = beyond[:, tile * LANES : (tile + 1) * LANES]

        rows_copy(0).wait()
        for row in range(2 * HALO):
            prepare(row)
        first_group(0)

        @pl.when(at_top == 1)
        def clear_top():
            hidden[0] = jnp.zeros(hidden.shape[1:], BF16)

    @pl.when(step < parts - 1)
    def arrive():
        rows_copy(step + 1).wait()

    @pl.when((step >= LAG) & (step < parts))
    def steady():
        second_row = jnp.maximum((step - LAG) * OUT_ROWS, 0)
        first_row = jnp.maximum((step - 1) * OUT_ROWS, 0) + GROUP
        for g in range(OUT_ROWS // GROUP):
            second_group(g, second_row + g * GROUP)
        for g in range(OUT_ROWS // GROUP):
            first_group(first_row + g * GROUP)
        for r in range(OUT_ROWS):
            prepare(step * OUT_ROWS + 2 * GROUP + r)
        for half in range(2):
            out_ref[:, :, half * LANES : (half + 1) * LANES] = jnp.swapaxes(stage[half], 0, 1).astype(
                BF16
            )


    @pl.when(step >= parts)
    def last_ones():
        for g in range(OUT_ROWS // GROUP):
            second_group(g, (step - LAG) * OUT_ROWS + g * GROUP)
        for half in range(2):
            out_ref[:, :, half * LANES : (half + 1) * LANES] = jnp.swapaxes(
                stage[half], 0, 1
            ).astype(BF16)

    @pl.when(((step >= 1) & (step < LAG)) | (step == parts))
    def first_ones():
        for g in range(OUT_ROWS // GROUP):
            first_group((step - 1) * OUT_ROWS + GROUP + g * GROUP)

    @pl.when(step < LAG)
    def shift_ones():
        for r in range(OUT_ROWS):
            prepare(step * OUT_ROWS + 2 * GROUP + r)

    @pl.when((step == parts) & (at_bottom == 1))
    def clear_bottom():
        hidden[rows_hid - 1] = jnp.zeros(hidden.shape[1:], BF16)


def banded(kernel, count):
    hid, channels = kernel.shape[1:]
    taps = jnp.transpose(kernel.reshape(3, 3, hid, channels), (2, 0, 1, 3))
    taps = taps.reshape(hid, 9 * channels)
    span = 3 * channels
    rows = [jnp.pad(taps, ((0, 0), (r * span, (count - 1 - r) * span))) for r in range(count)]
    return jnp.concatenate(rows, axis=0)


def whole_in_vmem():
    return pl.BlockSpec(memory_space=pltpu.VMEM)


def pack(route_block, route_count, sweeps, route_cell, route_templ):
    peers, capacity = route_block.shape
    channels = sweeps.shape[1]
    rows = capacity * channels + INFO_ROWS
    return pl.pallas_call(
        functools.partial(pack_kernel, channels),
        grid_spec=pltpu.PrefetchScalarGridSpec(
            num_scalar_prefetch=2,
            grid=(1,),
            in_specs=[pl.BlockSpec(memory_space=pl.ANY), whole_in_vmem(), whole_in_vmem()],
            out_specs=pl.BlockSpec(memory_space=pl.ANY),
            scratch_shapes=[
                pltpu.VMEM((peers, rows, LANES), BF16),
                pltpu.VMEM((2, peers, LANES), F32),
                pltpu.SemaphoreType.DMA((2 * PACK_PARTS,)),
            ],
        ),
        out_shape=jax.ShapeDtypeStruct((peers, rows, LANES), BF16),
        compiler_params=pltpu.CompilerParams(
            dimension_semantics=("arbitrary",), vmem_limit_bytes=PACK_VMEM
        ),
        name="pack",
    )(route_block, route_count, sweeps, route_cell, route_templ)


def composite(received, col, table, row_weight, capacity, channels):
    peers = received.shape[0]
    rows = TH // ROW_STEPS * channels
    return pl.pallas_call(
        functools.partial(composite_kernel, capacity, channels),
        grid_spec=pltpu.PrefetchScalarGridSpec(
            num_scalar_prefetch=1,
            grid=(ROW_STEPS,),
            in_specs=[
                pl.BlockSpec(memory_space=pl.ANY),
                pl.BlockSpec(memory_space=pltpu.HBM),
                whole_in_vmem(),
            ],
            out_specs=[pl.BlockSpec((rows, TW), lambda i, *_: (i, 0))] + [whole_in_vmem()] * 3,
            scratch_shapes=[
                pltpu.VMEM((CBLK + 1, channels, LANES), F32),
                pltpu.VMEM((CBLK + 8, LANES), F32),
                pltpu.VMEM((2, EDGE_TILES, channels, LANES), BF16),
                pltpu.VMEM((peers, capacity * channels, LANES), BF16),
                pltpu.VMEM(table.shape, BF16),
                pltpu.VMEM((peers, INFO_ROWS, LANES), BF16),
                pltpu.VMEM((2 * peers, LANES), jnp.int32),
                pltpu.SMEM((2 * peers, LANES), jnp.int32),
                pltpu.SemaphoreType.DMA((LOADS + 3,)),
            ],
        ),
        out_shape=[
            jax.ShapeDtypeStruct((TH * channels, TW), BF16),
            jax.ShapeDtypeStruct((2, EDGE_TILES, channels, LANES), BF16),
            jax.ShapeDtypeStruct((HALO, channels, TW), BF16),
            jax.ShapeDtypeStruct((HALO, channels, TW), BF16),
        ],
        compiler_params=pltpu.CompilerParams(
            dimension_semantics=("arbitrary",), vmem_limit_bytes=COMPOSITE_VMEM
        ),
        name="composite",
    )(col, received, table, row_weight)


def encoder(place, field, rim_a, rim_b, own, side, side_a, side_b, weights, channels, hid):
    parts = TH // OUT_ROWS
    steps = parts + LAG
    return pl.pallas_call(
        functools.partial(encoder_kernel, channels, hid),
        grid_spec=pltpu.PrefetchScalarGridSpec(
            num_scalar_prefetch=1,
            grid=(steps,),
            in_specs=[pl.BlockSpec(memory_space=pl.ANY)] * 3 + [whole_in_vmem()] * 9,
            out_specs=pl.BlockSpec(
                (hid, OUT_ROWS, TW), lambda i, *_: (0, jnp.maximum(i - LAG, 0), 0)
            ),
            scratch_shapes=[
                pltpu.VMEM((TH + 2 * HALO, 3, channels, TW), BF16),
                pltpu.VMEM((TH + 2, 3, hid, TW), BF16),
                pltpu.VMEM((EDGE_TILES, channels, LANES), BF16),
                pltpu.VMEM((EDGE_TILES, hid, LANES), BF16),
                pltpu.VMEM((2, hid, LANES), F32),
                pltpu.VMEM((2, OUT_ROWS, hid, LANES), F32),
                pltpu.SemaphoreType.DMA((parts + 2,)),
            ],
        ),
        out_shape=jax.ShapeDtypeStruct((hid, TH, TW), BF16),
        compiler_params=pltpu.CompilerParams(
            dimension_semantics=("arbitrary",), vmem_limit_bytes=ENCODER_VMEM
        ),
        name="encoder",
    )(place, field, rim_a, rim_b, own, side, side_a, side_b, *weights)


def layer_weights(conv_first, bias_first, conv_second, bias_second, col):
    hid = conv_first.shape[1]
    taps = conv_first.reshape(3, 3, hid, -1)
    inner = jnp.where(col == 0, taps[:, 2], taps[:, 0])
    outer = jnp.where(col == 0, taps[:, 0], taps[:, 2])
    edge_first = jnp.concatenate([taps[:, 1], inner, outer], axis=2).reshape(3 * hid, -1)
    return (
        banded(conv_first, GROUP),
        banded(conv_second, GROUP),
        edge_first,
        bias_first.reshape(1, hid),
        bias_second.reshape(1, hid),
    )


def shards(
    sweeps, route_block, route_cell, route_templ, route_count, footprint,
    conv_first, bias_first, conv_second, bias_second,
):
    peers, capacity = route_block.shape[1:]
    channels = sweeps.shape[1]
    hid = conv_first.shape[1]
    rows = lax.axis_size("ty")
    col = lax.axis_index("tx")
    row = lax.axis_index("ty")
    tiles = ("ty", "tx")

    packets = pack(route_block[0], route_count, sweeps, route_cell, route_templ)
    received = lax.all_to_all(packets, tiles, split_axis=0, concat_axis=0, tiled=True)
    table = jnp.transpose(footprint, (0, 2, 1))
    row_weight = jnp.sum(footprint.astype(F32), axis=2)
    place = jnp.stack([col, row == 0, row == rows - 1, row % 2]).astype(jnp.int32)
    weights = layer_weights(conv_first, bias_first, conv_second, bias_second, col)
    received, table, row_weight, place, weights = lax.optimization_barrier(
        (received, table, row_weight, place, weights)
    )
    field, own, rim_a, rim_b = composite(received, place, table, row_weight, capacity, channels)

    field = field.reshape(TH, channels, TW)
    swap = [(0, 1), (1, 0)]
    pairs_a = [p for i in range(0, rows - 1, 2) for p in ((i, i + 1), (i + 1, i))]
    pairs_b = [p for i in range(1, rows - 1, 2) for p in ((i, i + 1), (i + 1, i))]
    side = lax.ppermute(own, "tx", swap)
    rim_a = lax.ppermute(rim_a, "ty", pairs_a)
    rim_b = lax.ppermute(rim_b, "ty", pairs_b)
    side_a = lax.ppermute(rim_a, "tx", swap)
    side_b = lax.ppermute(rim_b, "tx", swap)
    return encoder(place, field, rim_a, rim_b, own, side, side_a, side_b, weights, channels, hid)


def solution(mesh):
    split = ("group", "ty", "tx")
    in_specs = (
        P(split, None, None),
        P(split, None, None),
        P(split, None, None),
        P(split, None, None),
        P(split, None),
        P(),
        P(),
        P(),
        P(),
        P(),
    )
    out_specs = P(None, ("group", "ty"), "tx")
    return jax.shard_map(shards, mesh=mesh, in_specs=in_specs, out_specs=out_specs, check_vma=False)
```

```python
import functools

import jax
import jax.numpy as jnp
from jax import lax
from jax.experimental import pallas as pl
from jax.experimental.pallas import tpu as pltpu
from jax.sharding import PartitionSpec as P

TH = 192
TW = 256
CBLK = 384
LANES = 128
HALO = 2
EDGE_TILES = 2
LANE_BASE = 8
ROW_STEPS = 3
CHUNK = 8
LOADS = 2
GROUP = 2
OUT_ROWS = 32
LAG = 2
PACK_PARTS = 8
INFO_ROWS = 16
CELL_BASE = 32
MIB = 1024 * 1024
PACK_VMEM = 56 * MIB
COMPOSITE_VMEM = 26 * MIB
ENCODER_VMEM = 48 * MIB

F32 = jnp.float32
BF16 = jnp.bfloat16


def lane_index(shape):
    return lax.broadcasted_iota(jnp.int32, shape, len(shape) - 1)


def silu(value):
    half = 0.5 * value
    return half + half * jnp.tanh(half)


def pack_kernel(
    channels, block_ref, count_ref, sweeps_ref, cell_ref, templ_ref, out_ref, packets, padded, sems
):
    peers, capacity = block_ref.shape
    held = capacity * channels
    part = peers // PACK_PARTS

    def send_tile(d, carry):
        for q in range(capacity):
            pltpu.make_async_copy(
                sweeps_ref.at[block_ref[d, q]],
                packets.at[d, pl.ds(q * channels, channels), :],
                sems.at[d // part],
            ).start()
        return carry

    lax.fori_loop(0, peers, send_tile, 0)
    padded[...] = jnp.zeros(padded.shape, F32)
    padded[0, :, 0:capacity] = cell_ref[0].astype(F32)
    padded[1, :, 0:capacity] = templ_ref[0].astype(F32)
    lane = lane_index((1, LANES))
    which = lax.broadcasted_iota(jnp.int32, (INFO_ROWS, LANES), 0)
    for d in range(peers):
        live = lane < count_ref[0, d]
        cell = jnp.where(live, padded[0, d : d + 1, :], float(CBLK))
        high = jnp.floor(cell * (1.0 / CELL_BASE))
        low = cell - high * CELL_BASE
        template = padded[1, d : d + 1, :]
        rows = jnp.where(which == 0, high, jnp.where(which == 1, low, template))
        packets[d, held : held + INFO_ROWS, :] = rows.astype(BF16)
    leaving = []
    for k in range(PACK_PARTS):
        mine = pl.ds(k * part, part)
        arrived = packets.at[mine, pl.ds(0, held), :]
        pltpu.make_async_copy(arrived, arrived, sems.at[k]).wait()
        leaving.append(
            pltpu.make_async_copy(packets.at[mine], out_ref.at[mine], sems.at[PACK_PARTS + k])
        )
        leaving[-1].start()
    for copy in leaving:
        copy.wait()


def composite_kernel(
    capacity, channels, col_ref, recv_ref, table_ref, weight_ref,
    comp_ref, edge_ref, rim_a, rim_b, acc, den, strip, recv, table, raw, numbers, slots, sems,
):
    step = pl.program_id(0)
    peers = recv_ref.shape[0]
    part = peers // LOADS
    col = col_ref[0]
    odd = col_ref[3]

    @pl.when(step == 0)
    def add_up():
        held = capacity * channels
        listing = pltpu.make_async_copy(
            recv_ref.at[:, pl.ds(held, INFO_ROWS), :], raw, sems.at[LOADS]
        )
        listing.start()
        copies = [
            pltpu.make_async_copy(
                recv_ref.at[pl.ds(k * part, part), pl.ds(0, held), :],
                recv.at[pl.ds(k * part, part)],
                sems.at[k],
            )
            for k in range(LOADS)
        ]
        tables = pltpu.make_async_copy(table_ref, table, sems.at[LOADS + 2])
        tables.start()
        for copy in copies:
            copy.start()
        listing.wait()
        for source in range(peers):
            rows = raw[source].astype(F32)
            numbers[source : source + 1, :] = (
                rows[0:1] * CELL_BASE + rows[1:2]
            ).astype(jnp.int32)
            numbers[peers + source : peers + source + 1, :] = rows[2:3].astype(jnp.int32)
        moved = pltpu.make_async_copy(numbers, slots, sems.at[LOADS + 1])
        moved.start()

        def clear_block(i, carry):
            acc[i] = jnp.zeros(acc.shape[1:], F32)
            return carry

        lax.fori_loop(0, CBLK, clear_block, 0, unroll=8)
        den[...] = jnp.zeros(den.shape, F32)
        strip[...] = jnp.zeros(strip.shape, BF16)

        moved.wait()
        tables.wait()

        def add_slots(source, carry):
            terms = []
            for q in range(capacity):
                block = recv[source, q * channels : (q + 1) * channels, :]
                template = slots[peers + source, q]
                terms.append(jnp.dot(block, table[template], preferred_element_type=F32))
            for q in range(capacity):
                cell = slots[source, q]
                acc[cell] += terms[q]
                template = slots[peers + source, q]
                den[pl.ds(cell, 1), :] += weight_ref[pl.ds(template, 1), :]
            return carry

        for k in range(LOADS):
            copies[k].wait()
            lax.fori_loop(k * part, (k + 1) * part, add_slots, 0, unroll=8)
        den[...] = 1.0 / (1.0 + den[...])

    rows = TH // ROW_STEPS
    lane = lane_index((channels, LANES))
    near = jnp.where(col == 0, LANES - 1, 0)
    far = jnp.where(col == 0, LANES - 2, 1)

    def some_rows(i, carry):
        base = step * rows + i * CHUNK
        picked = [jnp.zeros((channels, LANES), BF16), jnp.zeros((channels, LANES), BF16)]
        for u in range(CHUNK):
            r = base + u
            out = pl.multiple_of((i * CHUNK + u) * channels, 16)
            parts = []
            for m in range(2):
                value = (acc[2 * r + m] * den[pl.ds(2 * r + m, 1), :]).astype(BF16)
                comp_ref[pl.ds(out, channels), m * LANES : (m + 1) * LANES] = value
                parts.append(value)
            side = jnp.where(col == 0, parts[1], parts[0])
            at = (r + LANE_BASE) % LANES
            for p, start in enumerate((near, far)):
                moved = pltpu.roll(side, (at - start + LANES) % LANES, 1)
                picked[p] = jnp.where(lane == at, moved, picked[p])
        tile = (base + LANE_BASE) // LANES
        first = (base + LANE_BASE) % LANES
        inside = (lane >= first) & (lane < first + CHUNK)
        for p in range(2):
            strip[p, tile] = jnp.where(inside, picked[p], strip[p, tile])
        return carry

    lax.fori_loop(0, rows // CHUNK, some_rows, 0, unroll=4)

    rim = HALO * channels
    top = step == 0
    bottom = step == ROW_STEPS - 1

    @pl.when((top & (odd == 1)) | (bottom & (odd == 0)))
    def rim_to_a():
        begin = pl.multiple_of(jnp.where(top, 0, rows * channels - rim), 16)
        rim_a[...] = comp_ref[pl.ds(begin, rim), :].reshape(HALO, channels, TW)

    @pl.when((top & (odd == 0)) | (bottom & (odd == 1)))
    def rim_to_b():
        begin = pl.multiple_of(jnp.where(top, 0, rows * channels - rim), 16)
        rim_b[...] = comp_ref[pl.ds(begin, rim), :].reshape(HALO, channels, TW)

    @pl.when(bottom)
    def finish():
        edge_ref[...] = strip[...]


def shifted(value, left, right):
    lane = lane_index((value.shape[0], LANES))
    first, last = value[:, :LANES], value[:, LANES:]
    first_left, last_left = pltpu.roll(first, 1, 1), pltpu.roll(last, 1, 1)
    first_right, last_right = pltpu.roll(first, LANES - 1, 1), pltpu.roll(last, LANES - 1, 1)
    before = (
        jnp.where(lane == 0, left, first_left),
        jnp.where(lane == 0, first_left, last_left),
    )
    after = (
        jnp.where(lane == LANES - 1, last_right, first_right),
        jnp.where(lane == LANES - 1, right, last_right),
    )
    return before, after


def encoder_kernel(
    channels, hid, place_ref, comp_ref, rim_a_ref, rim_b_ref, own_ref, side_ref, side_a_ref, side_b_ref,
    first_ref, second_ref, edge_first_ref, bias_first_ref, bias_second_ref,
    out_ref, field, hidden, edge_one, edge_two, biases, stage, sems,
):
    col = place_ref[0]
    at_top = place_ref[1]
    at_bottom = place_ref[2]
    odd = place_ref[3]
    target = jnp.where(col == 0, LANES - 1, 0)
    rows_hid = TH + 2
    span = EDGE_TILES * LANES
    step = pl.program_id(0)
    parts = TH // OUT_ROWS

    def halo_columns(strip, lane_at):
        moved = pltpu.roll(
            strip[lane_at // LANES], (target - lane_at % LANES + LANES) % LANES, 1
        )
        nothing = jnp.zeros_like(moved)
        return jnp.where(col == 0, nothing, moved), jnp.where(col == 0, moved, nothing)

    def put_row(ref, strip, row, value):
        left, right = halo_columns(strip, row + LANE_BASE - HALO)
        before, after = shifted(value, left, right)
        for half in range(2):
            place = slice(half * LANES, (half + 1) * LANES)
            ref[row, 0, :, place] = before[half]
            ref[row, 2, :, place] = after[half]

    def prepare(row):
        put_row(field, edge_one, row, field[row, 1])

    def first_group(first_row):
        window = field[pl.ds(first_row, GROUP + 2)].reshape((GROUP + 2) * 3 * channels, TW)
        full = jnp.dot(first_ref[...], window, preferred_element_type=F32)
        bias = jnp.concatenate([biases[0]] * 2, axis=1)
        for r in range(GROUP):
            value = silu(full[r * hid : (r + 1) * hid] + bias).astype(BF16)
            hidden[first_row + r, 1] = value
            put_row(hidden, edge_two, first_row + r, value)

    def second_group(g, first_row):
        window = hidden[pl.ds(first_row, GROUP + 2)].reshape((GROUP + 2) * 3 * hid, TW)
        full = jnp.dot(second_ref[...], window, preferred_element_type=F32)
        bias = jnp.concatenate([biases[1]] * GROUP, axis=0)
        for half in range(2):
            value = full[:, half * LANES : (half + 1) * LANES] + bias
            for r in range(GROUP):
                stage[half, g * GROUP + r] = value[r * hid : (r + 1) * hid]

    def rows_copy(k):
        return pltpu.make_async_copy(
            comp_ref.at[pl.ds(k * OUT_ROWS, OUT_ROWS)],
            field.at[pl.ds(HALO + k * OUT_ROWS, OUT_ROWS), 1],
            sems.at[k],
        )

    @pl.when(step == 0)
    def start():
        row_a = jnp.where(odd == 1, 0, TH + HALO)
        row_b = jnp.where(odd == 1, TH + HALO, 0)
        rims = [
            pltpu.make_async_copy(
                ref, field.at[pl.ds(row, HALO), 1], sems.at[parts + k]
            )
            for k, (ref, row) in enumerate(((rim_a_ref, row_a), (rim_b_ref, row_b)))
        ]
        for rim in rims:
            rim.start()
        for k in range(parts):
            rows_copy(k).start()
        for rim in rims:
            rim.wait()

        across = lax.broadcasted_iota(jnp.int32, (hid, hid), 0)
        for k, ref in enumerate((bias_first_ref, bias_second_ref)):
            square = jnp.where(across == lane_index((hid, hid)), ref[...], 0.0)
            biases[k] = jnp.broadcast_to(jnp.sum(square, axis=1, keepdims=True), (hid, LANES))

        wide = lane_index((channels, span))

        def strip_of(ref, p):
            return jnp.concatenate([ref[p, 0], ref[p, 1]], axis=1).astype(F32)

        def put(strip, lane_at, tile, start):
            moved = pltpu.roll(tile, (lane_at % LANES - start + LANES) % LANES, 1)
            return jnp.where(wide == lane_at, jnp.concatenate([moved, moved], axis=1), strip)

        own = strip_of(own_ref, 0)
        sides = [strip_of(side_ref, p) for p in range(2)]
        starts = [jnp.where(col == 0, 0, LANES - 1), jnp.where(col == 0, 1, LANES - 2)]
        for above, at_row, lane_at in (
            (1, 0, LANE_BASE - HALO),
            (0, TH + HALO, TH + LANE_BASE),
        ):
            for k in range(HALO):
                tiles = jnp.where(
                    odd == above, side_a_ref[k].astype(F32), side_b_ref[k].astype(F32)
                )
                tile = jnp.where(col == 0, tiles[:, :LANES], tiles[:, LANES:])
                sides = [put(sides[p], lane_at + k, tile, starts[p]) for p in range(2)]
                tiles = field[at_row + k, 1].astype(F32)
                tile = jnp.where(col == 0, tiles[:, LANES:], tiles[:, :LANES])
                own = put(own, lane_at + k, tile, target)

        stack = jnp.concatenate([sides[0], sides[1], own], axis=0).astype(BF16)
        result = jnp.dot(edge_first_ref[...], stack, preferred_element_type=F32)
        total = result[0:hid]
        for a in range(1, 3):
            total = total + pltpu.roll(result[hid * a : hid * (a + 1)], span - a, 1)
        beyond = silu(total + jnp.concatenate([biases[0]] * EDGE_TILES, axis=1))
        lane_hid = lane_index((hid, span))
        first_lane = LANE_BASE - HALO
        drop = ((lane_hid == first_lane) & (at_top == 1)) | (
            (lane_hid == first_lane + rows_hid - 1) & (at_bottom == 1)
        )
        beyond = jnp.where(drop, 0.0, beyond).astype(BF16)
        for tile in range(EDGE_TILES):
            edge_one[tile] = sides[0][:, tile * LANES : (tile + 1) * LANES].astype(BF16)
            edge_two[tile] = beyond[:, tile * LANES : (tile + 1) * LANES]

        rows_copy(0).wait()
        for row in range(2 * HALO):
            prepare(row)
        first_group(0)

        @pl.when(at_top == 1)
        def clear_top():
            hidden[0] = jnp.zeros(hidden.shape[1:], BF16)

    @pl.when(step < parts - 1)
    def arrive():
        rows_copy(step + 1).wait()

    @pl.when((step >= LAG) & (step < parts))
    def steady():
        second_row = jnp.maximum((step - LAG) * OUT_ROWS, 0)
        first_row = jnp.maximum((step - 1) * OUT_ROWS, 0) + GROUP
        for g in range(OUT_ROWS // GROUP):
            second_group(g, second_row + g * GROUP)
        for g in range(OUT_ROWS // GROUP):
            first_group(first_row + g * GROUP)
        for r in range(OUT_ROWS):
            prepare(step * OUT_ROWS + 2 * GROUP + r)
        for half in range(2):
            out_ref[:, :, half * LANES : (half + 1) * LANES] = jnp.swapaxes(stage[half], 0, 1).astype(
                BF16
            )


    @pl.when(step >= parts)
    def last_ones():
        for g in range(OUT_ROWS // GROUP):
            second_group(g, (step - LAG) * OUT_ROWS + g * GROUP)
        for half in range(2):
            out_ref[:, :, half * LANES : (half + 1) * LANES] = jnp.swapaxes(
                stage[half], 0, 1
            ).astype(BF16)

    @pl.when(((step >= 1) & (step < LAG)) | (step == parts))
    def first_ones():
        for g in range(OUT_ROWS // GROUP):
            first_group((step - 1) * OUT_ROWS + GROUP + g * GROUP)

    @pl.when(step < LAG)
    def shift_ones():
        for r in range(OUT_ROWS):
            prepare(step * OUT_ROWS + 2 * GROUP + r)

    @pl.when((step == parts) & (at_bottom == 1))
    def clear_bottom():
        hidden[rows_hid - 1] = jnp.zeros(hidden.shape[1:], BF16)


def banded(kernel, count):
    hid, channels = kernel.shape[1:]
    taps = jnp.transpose(kernel.reshape(3, 3, hid, channels), (2, 0, 1, 3))
    taps = taps.reshape(hid, 9 * channels)
    span = 3 * channels
    rows = [jnp.pad(taps, ((0, 0), (r * span, (count - 1 - r) * span))) for r in range(count)]
    return jnp.concatenate(rows, axis=0)


def whole_in_vmem():
    return pl.BlockSpec(memory_space=pltpu.VMEM)


def pack(route_block, route_count, sweeps, route_cell, route_templ):
    peers, capacity = route_block.shape
    channels = sweeps.shape[1]
    rows = capacity * channels + INFO_ROWS
    return pl.pallas_call(
        functools.partial(pack_kernel, channels),
        grid_spec=pltpu.PrefetchScalarGridSpec(
            num_scalar_prefetch=2,
            grid=(1,),
            in_specs=[pl.BlockSpec(memory_space=pl.ANY), whole_in_vmem(), whole_in_vmem()],
            out_specs=pl.BlockSpec(memory_space=pl.ANY),
            scratch_shapes=[
                pltpu.VMEM((peers, rows, LANES), BF16),
                pltpu.VMEM((2, peers, LANES), F32),
                pltpu.SemaphoreType.DMA((2 * PACK_PARTS,)),
            ],
        ),
        out_shape=jax.ShapeDtypeStruct((peers, rows, LANES), BF16),
        compiler_params=pltpu.CompilerParams(
            dimension_semantics=("arbitrary",), vmem_limit_bytes=PACK_VMEM
        ),
        name="pack",
    )(route_block, route_count, sweeps, route_cell, route_templ)


def composite(received, col, table, row_weight, capacity, channels):
    peers = received.shape[0]
    rows = TH // ROW_STEPS * channels
    return pl.pallas_call(
        functools.partial(composite_kernel, capacity, channels),
        grid_spec=pltpu.PrefetchScalarGridSpec(
            num_scalar_prefetch=1,
            grid=(ROW_STEPS,),
            in_specs=[
                pl.BlockSpec(memory_space=pl.ANY),
                pl.BlockSpec(memory_space=pltpu.HBM),
                whole_in_vmem(),
            ],
            out_specs=[pl.BlockSpec((rows, TW), lambda i, *_: (i, 0))] + [whole_in_vmem()] * 3,
            scratch_shapes=[
                pltpu.VMEM((CBLK + 1, channels, LANES), F32),
                pltpu.VMEM((CBLK + 8, LANES), F32),
                pltpu.VMEM((2, EDGE_TILES, channels, LANES), BF16),
                pltpu.VMEM((peers, capacity * channels, LANES), BF16),
                pltpu.VMEM(table.shape, BF16),
                pltpu.VMEM((peers, INFO_ROWS, LANES), BF16),
                pltpu.VMEM((2 * peers, LANES), jnp.int32),
                pltpu.SMEM((2 * peers, LANES), jnp.int32),
                pltpu.SemaphoreType.DMA((LOADS + 3,)),
            ],
        ),
        out_shape=[
            jax.ShapeDtypeStruct((TH * channels, TW), BF16),
            jax.ShapeDtypeStruct((2, EDGE_TILES, channels, LANES), BF16),
            jax.ShapeDtypeStruct((HALO, channels, TW), BF16),
            jax.ShapeDtypeStruct((HALO, channels, TW), BF16),
        ],
        compiler_params=pltpu.CompilerParams(
            dimension_semantics=("arbitrary",), vmem_limit_bytes=COMPOSITE_VMEM
        ),
        name="composite",
    )(col, received, table, row_weight)


def encoder(place, field, rim_a, rim_b, own, side, side_a, side_b, weights, channels, hid):
    parts = TH // OUT_ROWS
    steps = parts + LAG
    return pl.pallas_call(
        functools.partial(encoder_kernel, channels, hid),
        grid_spec=pltpu.PrefetchScalarGridSpec(
            num_scalar_prefetch=1,
            grid=(steps,),
            in_specs=[pl.BlockSpec(memory_space=pl.ANY)] * 3 + [whole_in_vmem()] * 9,
            out_specs=pl.BlockSpec(
                (hid, OUT_ROWS, TW), lambda i, *_: (0, jnp.maximum(i - LAG, 0), 0)
            ),
            scratch_shapes=[
                pltpu.VMEM((TH + 2 * HALO, 3, channels, TW), BF16),
                pltpu.VMEM((TH + 2, 3, hid, TW), BF16),
                pltpu.VMEM((EDGE_TILES, channels, LANES), BF16),
                pltpu.VMEM((EDGE_TILES, hid, LANES), BF16),
                pltpu.VMEM((2, hid, LANES), F32),
                pltpu.VMEM((2, OUT_ROWS, hid, LANES), F32),
                pltpu.SemaphoreType.DMA((parts + 2,)),
            ],
        ),
        out_shape=jax.ShapeDtypeStruct((hid, TH, TW), BF16),
        compiler_params=pltpu.CompilerParams(
            dimension_semantics=("arbitrary",), vmem_limit_bytes=ENCODER_VMEM
        ),
        name="encoder",
    )(place, field, rim_a, rim_b, own, side, side_a, side_b, *weights)


def layer_weights(conv_first, bias_first, conv_second, bias_second, col):
    hid = conv_first.shape[1]
    taps = conv_first.reshape(3, 3, hid, -1)
    inner = jnp.where(col == 0, taps[:, 2], taps[:, 0])
    outer = jnp.where(col == 0, taps[:, 0], taps[:, 2])
    edge_first = jnp.concatenate([taps[:, 1], inner, outer], axis=2).reshape(3 * hid, -1)
    return (
        banded(conv_first, GROUP),
        banded(conv_second, GROUP),
        edge_first,
        bias_first.reshape(1, hid),
        bias_second.reshape(1, hid),
    )


def shards(
    sweeps, route_block, route_cell, route_templ, route_count, footprint,
    conv_first, bias_first, conv_second, bias_second,
):
    peers, capacity = route_block.shape[1:]
    channels = sweeps.shape[1]
    hid = conv_first.shape[1]
    rows = lax.axis_size("ty")
    col = lax.axis_index("tx")
    row = lax.axis_index("ty")
    tiles = ("ty", "tx")

    packets = pack(route_block[0], route_count, sweeps, route_cell, route_templ)
    received = lax.all_to_all(packets, tiles, split_axis=0, concat_axis=0, tiled=True)
    table = jnp.transpose(footprint, (0, 2, 1))
    row_weight = jnp.sum(footprint.astype(F32), axis=2)
    place = jnp.stack([col, row == 0, row == rows - 1, row % 2]).astype(jnp.int32)
    weights = layer_weights(conv_first, bias_first, conv_second, bias_second, col)
    received, table, row_weight, place, weights = lax.optimization_barrier(
        (received, table, row_weight, place, weights)
    )
    field, own, rim_a, rim_b = composite(received, place, table, row_weight, capacity, channels)

    field = field.reshape(TH, channels, TW)
    swap = [(0, 1), (1, 0)]
    pairs_a = [p for i in range(0, rows - 1, 2) for p in ((i, i + 1), (i + 1, i))]
    pairs_b = [p for i in range(1, rows - 1, 2) for p in ((i, i + 1), (i + 1, i))]
    side = lax.ppermute(own, "tx", swap)
    rim_a = lax.ppermute(rim_a, "ty", pairs_a)
    rim_b = lax.ppermute(rim_b, "ty", pairs_b)
    side_a = lax.ppermute(rim_a, "tx", swap)
    side_b = lax.ppermute(rim_b, "tx", swap)
    return encoder(place, field, rim_a, rim_b, own, side, side_a, side_b, weights, channels, hid)


def solution(mesh):
    split = ("group", "ty", "tx")
    in_specs = (
        P(split, None, None),
        P(split, None, None),
        P(split, None, None),
        P(split, None, None),
        P(split, None),
        P(),
        P(),
        P(),
        P(),
        P(),
    )
    out_specs = P(None, ("group", "ty"), "tx")
    return jax.shard_map(shards, mesh=mesh, in_specs=in_specs, out_specs=out_specs, check_vma=False)
```

```python
import functools

import jax
import jax.numpy as jnp
from jax import lax
from jax.experimental import pallas as pl
from jax.experimental.pallas import tpu as pltpu
from jax.sharding import PartitionSpec as P

TH = 192
TW = 256
CBLK = 384
LANES = 128
HALO = 2
EDGE_TILES = 2
LANE_BASE = 8
ROW_STEPS = 3
CHUNK = 8
LOADS = 2
GROUP = 2
OUT_ROWS = 48
LAG = 2
PACK_PARTS = 8
INFO_ROWS = 16
CELL_BASE = 32
MIB = 1024 * 1024
PACK_VMEM = 56 * MIB
COMPOSITE_VMEM = 26 * MIB
ENCODER_VMEM = 50 * MIB

F32 = jnp.float32
BF16 = jnp.bfloat16


def lane_index(shape):
    return lax.broadcasted_iota(jnp.int32, shape, len(shape) - 1)


def silu(value):
    half = 0.5 * value
    return half + half * jnp.tanh(half)


def pack_kernel(
    channels, block_ref, count_ref, sweeps_ref, cell_ref, templ_ref, out_ref, packets, padded, sems
):
    peers, capacity = block_ref.shape
    held = capacity * channels
    part = peers // PACK_PARTS

    def send_tile(d, carry):
        for q in range(capacity):
            pltpu.make_async_copy(
                sweeps_ref.at[block_ref[d, q]],
                packets.at[d, pl.ds(q * channels, channels), :],
                sems.at[d // part],
            ).start()
        return carry

    lax.fori_loop(0, peers, send_tile, 0)
    padded[...] = jnp.zeros(padded.shape, F32)
    padded[0, :, 0:capacity] = cell_ref[0].astype(F32)
    padded[1, :, 0:capacity] = templ_ref[0].astype(F32)
    lane = lane_index((1, LANES))
    which = lax.broadcasted_iota(jnp.int32, (INFO_ROWS, LANES), 0)
    for d in range(peers):
        live = lane < count_ref[0, d]
        cell = jnp.where(live, padded[0, d : d + 1, :], float(CBLK))
        high = jnp.floor(cell * (1.0 / CELL_BASE))
        low = cell - high * CELL_BASE
        template = padded[1, d : d + 1, :]
        rows = jnp.where(which == 0, high, jnp.where(which == 1, low, template))
        packets[d, held : held + INFO_ROWS, :] = rows.astype(BF16)
    leaving = []
    for k in range(PACK_PARTS):
        mine = pl.ds(k * part, part)
        arrived = packets.at[mine, pl.ds(0, held), :]
        pltpu.make_async_copy(arrived, arrived, sems.at[k]).wait()
        leaving.append(
            pltpu.make_async_copy(packets.at[mine], out_ref.at[mine], sems.at[PACK_PARTS + k])
        )
        leaving[-1].start()
    for copy in leaving:
        copy.wait()


def composite_kernel(
    capacity, channels, col_ref, recv_ref, table_ref, weight_ref,
    comp_ref, edge_ref, rim_a, rim_b, acc, den, strip, recv, table, raw, numbers, slots, sems,
):
    step = pl.program_id(0)
    peers = recv_ref.shape[0]
    part = peers // LOADS
    col = col_ref[0]
    odd = col_ref[3]

    @pl.when(step == 0)
    def add_up():
        held = capacity * channels
        listing = pltpu.make_async_copy(
            recv_ref.at[:, pl.ds(held, INFO_ROWS), :], raw, sems.at[LOADS]
        )
        listing.start()
        copies = [
            pltpu.make_async_copy(
                recv_ref.at[pl.ds(k * part, part), pl.ds(0, held), :],
                recv.at[pl.ds(k * part, part)],
                sems.at[k],
            )
            for k in range(LOADS)
        ]
        tables = pltpu.make_async_copy(table_ref, table, sems.at[LOADS + 2])
        tables.start()
        for copy in copies:
            copy.start()
        listing.wait()
        for source in range(peers):
            rows = raw[source].astype(F32)
            numbers[source : source + 1, :] = (
                rows[0:1] * CELL_BASE + rows[1:2]
            ).astype(jnp.int32)
            numbers[peers + source : peers + source + 1, :] = rows[2:3].astype(jnp.int32)
        moved = pltpu.make_async_copy(numbers, slots, sems.at[LOADS + 1])
        moved.start()

        def clear_block(i, carry):
            acc[i] = jnp.zeros(acc.shape[1:], F32)
            return carry

        lax.fori_loop(0, CBLK, clear_block, 0, unroll=8)
        den[...] = jnp.zeros(den.shape, F32)
        strip[...] = jnp.zeros(strip.shape, BF16)

        moved.wait()
        tables.wait()

        def add_slots(source, carry):
            terms = []
            for q in range(capacity):
                block = recv[source, q * channels : (q + 1) * channels, :]
                template = slots[peers + source, q]
                terms.append(jnp.dot(block, table[template], preferred_element_type=F32))
            for q in range(capacity):
                cell = slots[source, q]
                acc[cell] += terms[q]
                template = slots[peers + source, q]
                den[pl.ds(cell, 1), :] += weight_ref[pl.ds(template, 1), :]
            return carry

        for k in range(LOADS):
            copies[k].wait()
            lax.fori_loop(k * part, (k + 1) * part, add_slots, 0, unroll=8)
        den[...] = 1.0 / (1.0 + den[...])

    rows = TH // ROW_STEPS
    lane = lane_index((channels, LANES))
    near = jnp.where(col == 0, LANES - 1, 0)
    far = jnp.where(col == 0, LANES - 2, 1)

    def some_rows(i, carry):
        base = step * rows + i * CHUNK
        picked = [jnp.zeros((channels, LANES), BF16), jnp.zeros((channels, LANES), BF16)]
        for u in range(CHUNK):
            r = base + u
            out = pl.multiple_of((i * CHUNK + u) * channels, 16)
            parts = []
            for m in range(2):
                value = (acc[2 * r + m] * den[pl.ds(2 * r + m, 1), :]).astype(BF16)
                comp_ref[pl.ds(out, channels), m * LANES : (m + 1) * LANES] = value
                parts.append(value)
            side = jnp.where(col == 0, parts[1], parts[0])
            at = (r + LANE_BASE) % LANES
            for p, start in enumerate((near, far)):
                moved = pltpu.roll(side, (at - start + LANES) % LANES, 1)
                picked[p] = jnp.where(lane == at, moved, picked[p])
        tile = (base + LANE_BASE) // LANES
        first = (base + LANE_BASE) % LANES
        inside = (lane >= first) & (lane < first + CHUNK)
        for p in range(2):
            strip[p, tile] = jnp.where(inside, picked[p], strip[p, tile])
        return carry

    lax.fori_loop(0, rows // CHUNK, some_rows, 0, unroll=4)

    rim = HALO * channels
    top = step == 0
    bottom = step == ROW_STEPS - 1

    @pl.when((top & (odd == 1)) | (bottom & (odd == 0)))
    def rim_to_a():
        begin = pl.multiple_of(jnp.where(top, 0, rows * channels - rim), 16)
        rim_a[...] = comp_ref[pl.ds(begin, rim), :].reshape(HALO, channels, TW)

    @pl.when((top & (odd == 0)) | (bottom & (odd == 1)))
    def rim_to_b():
        begin = pl.multiple_of(jnp.where(top, 0, rows * channels - rim), 16)
        rim_b[...] = comp_ref[pl.ds(begin, rim), :].reshape(HALO, channels, TW)

    @pl.when(bottom)
    def finish():
        edge_ref[...] = strip[...]


def shifted(value, left, right):
    lane = lane_index((value.shape[0], LANES))
    first, last = value[:, :LANES], value[:, LANES:]
    first_left, last_left = pltpu.roll(first, 1, 1), pltpu.roll(last, 1, 1)
    first_right, last_right = pltpu.roll(first, LANES - 1, 1), pltpu.roll(last, LANES - 1, 1)
    before = (
        jnp.where(lane == 0, left, first_left),
        jnp.where(lane == 0, first_left, last_left),
    )
    after = (
        jnp.where(lane == LANES - 1, last_right, first_right),
        jnp.where(lane == LANES - 1, right, last_right),
    )
    return before, after


def encoder_kernel(
    channels, hid, place_ref, comp_ref, rim_a_ref, rim_b_ref, own_ref, side_ref, side_a_ref, side_b_ref,
    first_ref, second_ref, edge_first_ref, bias_first_ref, bias_second_ref,
    out_ref, field, hidden, edge_one, edge_two, biases, stage, sems,
):
    col = place_ref[0]
    at_top = place_ref[1]
    at_bottom = place_ref[2]
    odd = place_ref[3]
    target = jnp.where(col == 0, LANES - 1, 0)
    rows_hid = TH + 2
    span = EDGE_TILES * LANES
    step = pl.program_id(0)
    parts = TH // OUT_ROWS

    def halo_columns(strip, lane_at):
        moved = pltpu.roll(
            strip[lane_at // LANES], (target - lane_at % LANES + LANES) % LANES, 1
        )
        nothing = jnp.zeros_like(moved)
        return jnp.where(col == 0, nothing, moved), jnp.where(col == 0, moved, nothing)

    def put_row(ref, strip, row, value):
        left, right = halo_columns(strip, row + LANE_BASE - HALO)
        before, after = shifted(value, left, right)
        for half in range(2):
            place = slice(half * LANES, (half + 1) * LANES)
            ref[row, 0, :, place] = before[half]
            ref[row, 2, :, place] = after[half]

    def prepare(row):
        put_row(field, edge_one, row, field[row, 1])

    def first_group(first_row):
        window = field[pl.ds(first_row, GROUP + 2)].reshape((GROUP + 2) * 3 * channels, TW)
        full = jnp.dot(first_ref[...], window, preferred_element_type=F32)
        bias = jnp.concatenate([biases[0]] * 2, axis=1)
        for r in range(GROUP):
            value = silu(full[r * hid : (r + 1) * hid] + bias).astype(BF16)
            hidden[first_row + r, 1] = value
            put_row(hidden, edge_two, first_row + r, value)

    def second_group(g, first_row):
        window = hidden[pl.ds(first_row, GROUP + 2)].reshape((GROUP + 2) * 3 * hid, TW)
        full = jnp.dot(second_ref[...], window, preferred_element_type=F32)
        bias = jnp.concatenate([biases[1]] * GROUP, axis=0)
        for half in range(2):
            value = full[:, half * LANES : (half + 1) * LANES] + bias
            for r in range(GROUP):
                stage[half, g * GROUP + r] = value[r * hid : (r + 1) * hid]

    def rows_copy(k):
        return pltpu.make_async_copy(
            comp_ref.at[pl.ds(k * OUT_ROWS, OUT_ROWS)],
            field.at[pl.ds(HALO + k * OUT_ROWS, OUT_ROWS), 1],
            sems.at[k],
        )

    @pl.when(step == 0)
    def start():
        row_a = jnp.where(odd == 1, 0, TH + HALO)
        row_b = jnp.where(odd == 1, TH + HALO, 0)
        rims = [
            pltpu.make_async_copy(
                ref, field.at[pl.ds(row, HALO), 1], sems.at[parts + k]
            )
            for k, (ref, row) in enumerate(((rim_a_ref, row_a), (rim_b_ref, row_b)))
        ]
        for rim in rims:
            rim.start()
        for k in range(parts):
            rows_copy(k).start()
        for rim in rims:
            rim.wait()

        across = lax.broadcasted_iota(jnp.int32, (hid, hid), 0)
        for k, ref in enumerate((bias_first_ref, bias_second_ref)):
            square = jnp.where(across == lane_index((hid, hid)), ref[...], 0.0)
            biases[k] = jnp.broadcast_to(jnp.sum(square, axis=1, keepdims=True), (hid, LANES))

        wide = lane_index((channels, span))

        def strip_of(ref, p):
            return jnp.concatenate([ref[p, 0], ref[p, 1]], axis=1).astype(F32)

        def put(strip, lane_at, tile, start):
            moved = pltpu.roll(tile, (lane_at % LANES - start + LANES) % LANES, 1)
            return jnp.where(wide == lane_at, jnp.concatenate([moved, moved], axis=1), strip)

        own = strip_of(own_ref, 0)
        sides = [strip_of(side_ref, p) for p in range(2)]
        starts = [jnp.where(col == 0, 0, LANES - 1), jnp.where(col == 0, 1, LANES - 2)]
        for above, at_row, lane_at in (
            (1, 0, LANE_BASE - HALO),
            (0, TH + HALO, TH + LANE_BASE),
        ):
            for k in range(HALO):
                tiles = jnp.where(
                    odd == above, side_a_ref[k].astype(F32), side_b_ref[k].astype(F32)
                )
                tile = jnp.where(col == 0, tiles[:, :LANES], tiles[:, LANES:])
                sides = [put(sides[p], lane_at + k, tile, starts[p]) for p in range(2)]
                tiles = field[at_row + k, 1].astype(F32)
                tile = jnp.where(col == 0, tiles[:, LANES:], tiles[:, :LANES])
                own = put(own, lane_at + k, tile, target)

        stack = jnp.concatenate([sides[0], sides[1], own], axis=0).astype(BF16)
        result = jnp.dot(edge_first_ref[...], stack, preferred_element_type=F32)
        total = result[0:hid]
        for a in range(1, 3):
            total = total + pltpu.roll(result[hid * a : hid * (a + 1)], span - a, 1)
        beyond = silu(total + jnp.concatenate([biases[0]] * EDGE_TILES, axis=1))
        lane_hid = lane_index((hid, span))
        first_lane = LANE_BASE - HALO
        drop = ((lane_hid == first_lane) & (at_top == 1)) | (
            (lane_hid == first_lane + rows_hid - 1) & (at_bottom == 1)
        )
        beyond = jnp.where(drop, 0.0, beyond).astype(BF16)
        for tile in range(EDGE_TILES):
            edge_one[tile] = sides[0][:, tile * LANES : (tile + 1) * LANES].astype(BF16)
            edge_two[tile] = beyond[:, tile * LANES : (tile + 1) * LANES]

        rows_copy(0).wait()
        for row in range(2 * HALO):
            prepare(row)
        first_group(0)

        @pl.when(at_top == 1)
        def clear_top():
            hidden[0] = jnp.zeros(hidden.shape[1:], BF16)

    @pl.when(step < parts - 1)
    def arrive():
        rows_copy(step + 1).wait()

    @pl.when((step >= LAG) & (step < parts))
    def steady():
        second_row = jnp.maximum((step - LAG) * OUT_ROWS, 0)
        first_row = jnp.maximum((step - 1) * OUT_ROWS, 0) + GROUP
        for g in range(OUT_ROWS // GROUP):
            second_group(g, second_row + g * GROUP)
        for g in range(OUT_ROWS // GROUP):
            first_group(first_row + g * GROUP)
        for r in range(OUT_ROWS):
            prepare(step * OUT_ROWS + 2 * GROUP + r)
        for half in range(2):
            out_ref[:, :, half * LANES : (half + 1) * LANES] = jnp.swapaxes(stage[half], 0, 1).astype(
                BF16
            )


    @pl.when(step >= parts)
    def last_ones():
        for g in range(OUT_ROWS // GROUP):
            second_group(g, (step - LAG) * OUT_ROWS + g * GROUP)
        for half in range(2):
            out_ref[:, :, half * LANES : (half + 1) * LANES] = jnp.swapaxes(
                stage[half], 0, 1
            ).astype(BF16)

    @pl.when(((step >= 1) & (step < LAG)) | (step == parts))
    def first_ones():
        for g in range(OUT_ROWS // GROUP):
            first_group((step - 1) * OUT_ROWS + GROUP + g * GROUP)

    @pl.when(step < LAG)
    def shift_ones():
        for r in range(OUT_ROWS):
            prepare(step * OUT_ROWS + 2 * GROUP + r)

    @pl.when((step == parts) & (at_bottom == 1))
    def clear_bottom():
        hidden[rows_hid - 1] = jnp.zeros(hidden.shape[1:], BF16)


def banded(kernel, count):
    hid, channels = kernel.shape[1:]
    taps = jnp.transpose(kernel.reshape(3, 3, hid, channels), (2, 0, 1, 3))
    taps = taps.reshape(hid, 9 * channels)
    span = 3 * channels
    rows = [jnp.pad(taps, ((0, 0), (r * span, (count - 1 - r) * span))) for r in range(count)]
    return jnp.concatenate(rows, axis=0)


def whole_in_vmem():
    return pl.BlockSpec(memory_space=pltpu.VMEM)


def pack(route_block, route_count, sweeps, route_cell, route_templ):
    peers, capacity = route_block.shape
    channels = sweeps.shape[1]
    rows = capacity * channels + INFO_ROWS
    return pl.pallas_call(
        functools.partial(pack_kernel, channels),
        grid_spec=pltpu.PrefetchScalarGridSpec(
            num_scalar_prefetch=2,
            grid=(1,),
            in_specs=[pl.BlockSpec(memory_space=pl.ANY), whole_in_vmem(), whole_in_vmem()],
            out_specs=pl.BlockSpec(memory_space=pl.ANY),
            scratch_shapes=[
                pltpu.VMEM((peers, rows, LANES), BF16),
                pltpu.VMEM((2, peers, LANES), F32),
                pltpu.SemaphoreType.DMA((2 * PACK_PARTS,)),
            ],
        ),
        out_shape=jax.ShapeDtypeStruct((peers, rows, LANES), BF16),
        compiler_params=pltpu.CompilerParams(
            dimension_semantics=("arbitrary",), vmem_limit_bytes=PACK_VMEM
        ),
        name="pack",
    )(route_block, route_count, sweeps, route_cell, route_templ)


def composite(received, col, table, row_weight, capacity, channels):
    peers = received.shape[0]
    rows = TH // ROW_STEPS * channels
    return pl.pallas_call(
        functools.partial(composite_kernel, capacity, channels),
        grid_spec=pltpu.PrefetchScalarGridSpec(
            num_scalar_prefetch=1,
            grid=(ROW_STEPS,),
            in_specs=[
                pl.BlockSpec(memory_space=pl.ANY),
                pl.BlockSpec(memory_space=pltpu.HBM),
                whole_in_vmem(),
            ],
            out_specs=[pl.BlockSpec((rows, TW), lambda i, *_: (i, 0))] + [whole_in_vmem()] * 3,
            scratch_shapes=[
                pltpu.VMEM((CBLK + 1, channels, LANES), F32),
                pltpu.VMEM((CBLK + 8, LANES), F32),
                pltpu.VMEM((2, EDGE_TILES, channels, LANES), BF16),
                pltpu.VMEM((peers, capacity * channels, LANES), BF16),
                pltpu.VMEM(table.shape, BF16),
                pltpu.VMEM((peers, INFO_ROWS, LANES), BF16),
                pltpu.VMEM((2 * peers, LANES), jnp.int32),
                pltpu.SMEM((2 * peers, LANES), jnp.int32),
                pltpu.SemaphoreType.DMA((LOADS + 3,)),
            ],
        ),
        out_shape=[
            jax.ShapeDtypeStruct((TH * channels, TW), BF16),
            jax.ShapeDtypeStruct((2, EDGE_TILES, channels, LANES), BF16),
            jax.ShapeDtypeStruct((HALO, channels, TW), BF16),
            jax.ShapeDtypeStruct((HALO, channels, TW), BF16),
        ],
        compiler_params=pltpu.CompilerParams(
            dimension_semantics=("arbitrary",), vmem_limit_bytes=COMPOSITE_VMEM
        ),
        name="composite",
    )(col, received, table, row_weight)


def encoder(place, field, rim_a, rim_b, own, side, side_a, side_b, weights, channels, hid):
    parts = TH // OUT_ROWS
    steps = parts + LAG
    return pl.pallas_call(
        functools.partial(encoder_kernel, channels, hid),
        grid_spec=pltpu.PrefetchScalarGridSpec(
            num_scalar_prefetch=1,
            grid=(steps,),
            in_specs=[pl.BlockSpec(memory_space=pl.ANY)] * 3 + [whole_in_vmem()] * 9,
            out_specs=pl.BlockSpec(
                (hid, OUT_ROWS, TW), lambda i, *_: (0, jnp.maximum(i - LAG, 0), 0)
            ),
            scratch_shapes=[
                pltpu.VMEM((TH + 2 * HALO, 3, channels, TW), BF16),
                pltpu.VMEM((TH + 2, 3, hid, TW), BF16),
                pltpu.VMEM((EDGE_TILES, channels, LANES), BF16),
                pltpu.VMEM((EDGE_TILES, hid, LANES), BF16),
                pltpu.VMEM((2, hid, LANES), F32),
                pltpu.VMEM((2, OUT_ROWS, hid, LANES), F32),
                pltpu.SemaphoreType.DMA((parts + 2,)),
            ],
        ),
        out_shape=jax.ShapeDtypeStruct((hid, TH, TW), BF16),
        compiler_params=pltpu.CompilerParams(
            dimension_semantics=("arbitrary",), vmem_limit_bytes=ENCODER_VMEM
        ),
        name="encoder",
    )(place, field, rim_a, rim_b, own, side, side_a, side_b, *weights)


def layer_weights(conv_first, bias_first, conv_second, bias_second, col):
    hid = conv_first.shape[1]
    taps = conv_first.reshape(3, 3, hid, -1)
    inner = jnp.where(col == 0, taps[:, 2], taps[:, 0])
    outer = jnp.where(col == 0, taps[:, 0], taps[:, 2])
    edge_first = jnp.concatenate([taps[:, 1], inner, outer], axis=2).reshape(3 * hid, -1)
    return (
        banded(conv_first, GROUP),
        banded(conv_second, GROUP),
        edge_first,
        bias_first.reshape(1, hid),
        bias_second.reshape(1, hid),
    )


def shards(
    sweeps, route_block, route_cell, route_templ, route_count, footprint,
    conv_first, bias_first, conv_second, bias_second,
):
    peers, capacity = route_block.shape[1:]
    channels = sweeps.shape[1]
    hid = conv_first.shape[1]
    rows = lax.axis_size("ty")
    col = lax.axis_index("tx")
    row = lax.axis_index("ty")
    tiles = ("ty", "tx")

    packets = pack(route_block[0], route_count, sweeps, route_cell, route_templ)
    received = lax.all_to_all(packets, tiles, split_axis=0, concat_axis=0, tiled=True)
    table = jnp.transpose(footprint, (0, 2, 1))
    row_weight = jnp.sum(footprint.astype(F32), axis=2)
    place = jnp.stack([col, row == 0, row == rows - 1, row % 2]).astype(jnp.int32)
    weights = layer_weights(conv_first, bias_first, conv_second, bias_second, col)
    received, table, row_weight, place, weights = lax.optimization_barrier(
        (received, table, row_weight, place, weights)
    )
    field, own, rim_a, rim_b = composite(received, place, table, row_weight, capacity, channels)

    field = field.reshape(TH, channels, TW)
    swap = [(0, 1), (1, 0)]
    pairs_a = [p for i in range(0, rows - 1, 2) for p in ((i, i + 1), (i + 1, i))]
    pairs_b = [p for i in range(1, rows - 1, 2) for p in ((i, i + 1), (i + 1, i))]
    side = lax.ppermute(own, "tx", swap)
    rim_a = lax.ppermute(rim_a, "ty", pairs_a)
    rim_b = lax.ppermute(rim_b, "ty", pairs_b)
    side_a = lax.ppermute(rim_a, "tx", swap)
    side_b = lax.ppermute(rim_b, "tx", swap)
    return encoder(place, field, rim_a, rim_b, own, side, side_a, side_b, weights, channels, hid)


def solution(mesh):
    split = ("group", "ty", "tx")
    in_specs = (
        P(split, None, None),
        P(split, None, None),
        P(split, None, None),
        P(split, None, None),
        P(split, None),
        P(),
        P(),
        P(),
        P(),
        P(),
    )
    out_specs = P(None, ("group", "ty"), "tx")
    return jax.shard_map(shards, mesh=mesh, in_specs=in_specs, out_specs=out_specs, check_vma=False)
```
